32 devices in a mesh: ctx: 8 (over y, x, core), dp: 4 (over z).
Axes of the slice: x: 2, y: 2, z: 4, core: 2. Of those that a mesh axis runs over, the one named last changes fastest.
Arguments:
- q_proj: bfloat16 [4, 1024, 2048], P('dp', 'ctx'), may hold values from -6 to 6
- k_proj: bfloat16 [4, 1024, 2048], P('dp', 'ctx'), may hold values from -6 to 6
- v_proj: bfloat16 [4, 1024, 2048], P('dp', 'ctx'), may hold values from -6 to 6
- out_grad: bfloat16 [4, 1024, 2048], P('dp', 'ctx'), may hold values from -6 to 6
- contig_starts: int32 [4, 1024], P('dp', 'ctx'), may hold values 0 or 1
- filters: bfloat16 [128, 128], replicated, may hold values from -0.5 to 0.5
Outputs:
- mixed_out: bfloat16 [4, 1024, 2048], P('dp', 'ctx')
- grad_q: bfloat16 [4, 1024, 2048], P('dp', 'ctx')
- grad_k: bfloat16 [4, 1024, 2048], P('dp', 'ctx')
- grad_v: bfloat16 [4, 1024, 2048], P('dp', 'ctx')
- filter_grad: float32 [128, 128], replicated
The draws below stay inside these ranges and needn't reach their ends.
Inputs may be any that keep to these rules, and one draw needn't show every extreme that they name: `contig_starts`: a contig runs from a 1 to the token before the next 1 or to the end of its pack.
All inputs are finite; a program needn't handle non-finite values. No bound on the sum of `contig_starts` on one device may be relied on, other than what follows from the above.
Results may differ from the reference program's by a relative error of at most 0.0053.
Values may be sent and summed in bfloat16 or wider, within the bound.
No kernel may reach another device: no remote copies, remote signals or barrier semaphores. Data moves between devices by JAX's collectives and lax.ppermute only.
A program may use at most 64 MiB of HBM per device.

```python
import math
import jax
import jax.numpy as jnp
from jax import lax

D = 2048
FILT = 128
GSIZE = 16
GROUPS = 128
R_DEV = 128
TOKENS = 1024
BATCH = 4


def touch_ends(result, stream_key, least, largest):
    dims = result.shape
    place = [jax.random.randint(jax.random.fold_in(stream_key, axis), (), 0, dims[axis]) for axis in range(len(dims))]
    result = result.at[tuple(place)].set(least)
    longest = dims.index(max(dims))
    place[longest] = (place[longest] + 1) % dims[longest]
    return result.at[tuple(place)].set(largest)


def block_scale(rng, extent, shards, low, high):
    loudness = 1.0
    for position, blocks in shards:
        heights = jax.random.uniform(jax.random.fold_in(jax.random.fold_in(rng, 6), position), (blocks,), jnp.float32, low / len(shards), high / len(shards))
        loudness = loudness * jnp.repeat(jnp.exp(heights), extent[position] // blocks).reshape((-1,) + (1,) * (len(extent) - 1 - position))
    return loudness


def gaussian(stream_key, extent, deviation, bound, split=(), held_as=jnp.bfloat16):
    level = block_scale(stream_key, extent, split, -0.22, 0.18) if split else 1.0
    values = jax.random.normal(stream_key, extent, jnp.float32) * deviation * level
    return jnp.minimum(jnp.maximum(values, -bound), bound).astype(held_as)


def setup_inputs(seed: int = 0) -> dict:
    seeds = jax.random.split(jax.random.key(seed), 7)
    q_proj = gaussian(seeds[0], (BATCH, TOKENS, D), 1.0, 6.0, ((0, 4), (1, 8)))
    k_proj = gaussian(seeds[1], (BATCH, TOKENS, D), 1.0, 6.0, ((0, 4), (1, 8)))
    v_proj = gaussian(seeds[2], (BATCH, TOKENS, D), 1.0, 6.0, ((0, 4), (1, 8)))
    out_grad = gaussian(seeds[3], (BATCH, TOKENS, D), 1.0, 6.0, ((0, 4), (1, 8)))
    contig_starts = touch_ends((jax.random.randint(seeds[4], (BATCH, TOKENS), 0, R_DEV) < 1).astype(jnp.int32), jax.random.fold_in(seeds[4], 1), 0, 1)
    filters = gaussian(seeds[5], (GROUPS, FILT), FILT ** -0.5, 0.5)
    return dict(q_proj=q_proj, k_proj=k_proj, v_proj=v_proj, out_grad=out_grad, contig_starts=contig_starts, filters=filters)


HIGH = lax.Precision.HIGHEST

def skew_rows(row_table):
    count = row_table.shape[0]
    tiled = jnp.tile(row_table, (1, FILT))[:, :FILT * (2 * FILT - 1)]
    return tiled.reshape(count, FILT, 2 * FILT - 1)

def diagonal_sums(products):
    lead = products.shape[:-2]
    flat = products.reshape(lead + (FILT * (2 * FILT - 1),))
    flat = jnp.concatenate([flat, jnp.zeros(lead + (FILT,), flat.dtype)], axis=-1)
    return lax.optimization_barrier(jnp.sum(flat.reshape(lead + (FILT, 2 * FILT))[..., :FILT], axis=-2))

def windows(extended):
    nblocks = extended.shape[0] // FILT - 1
    blocks = extended.reshape((nblocks + 1, FILT) + extended.shape[1:])
    return jnp.concatenate([blocks[:-1], blocks[1:, :FILT - 1]], axis=1)

def intersection_add(pieces):
    nblocks = pieces.shape[0]
    first = pieces[:, :FILT]
    second = jnp.concatenate([pieces[:, FILT:], jnp.zeros_like(pieces[:, :1])], axis=1)
    zero_block = jnp.zeros_like(first[:1])
    total = jnp.concatenate([first, zero_block], 0) + jnp.concatenate([zero_block, second], 0)
    return total.reshape(((nblocks + 1) * FILT,) + pieces.shape[2:])

def one_pack(items, base_table):
    q_row, k_row, v_row, dy_row, starts_row = items
    prod_kv = (k_row.astype(jnp.float32) * v_row.astype(jnp.float32)).astype(jnp.bfloat16)
    cotangent = (dy_row.astype(jnp.float32) * q_row.astype(jnp.float32)).astype(jnp.bfloat16)
    segment_ids = jnp.cumsum(starts_row).astype(jnp.int32)
    kv_ext = jnp.concatenate([jnp.zeros((FILT - 1, D), jnp.bfloat16), prod_kv, jnp.zeros((1, D), jnp.bfloat16)], 0)
    seg_ext = jnp.concatenate([jnp.full((FILT - 1,), -1, jnp.int32), segment_ids, jnp.full((1,), -1, jnp.int32)], 0)
    kv_win = windows(kv_ext)
    seg_win = windows(seg_ext)
    seg_own = segment_ids.reshape(-1, FILT)
    cot_blocks = cotangent.reshape(-1, FILT, D)
    span = 2 * FILT - 1

    def per_block(block_items):
        kv_w, seg_w, seg_o, cot_b = block_items
        linked = (seg_w[None, :] == seg_o[:, None]).astype(jnp.float32)
        table = base_table * linked[None]
        kv_wide = kv_w.astype(jnp.float32).reshape(span, GROUPS, GSIZE)
        conv = jnp.einsum('gts,sgc->tgc', table, kv_wide, precision=HIGH).reshape(FILT, D)
        cot_wide = cot_b.astype(jnp.float32).reshape(FILT, GROUPS, GSIZE)
        back = jnp.einsum('gts,tgc->sgc', table, cot_wide, precision=HIGH).reshape(span, D)
        products = jnp.einsum('tgc,sgc->gts', cot_wide, kv_wide, precision=HIGH) * linked[None]
        return (conv, back, diagonal_sums(products))
    conv, back, diag = lax.map(per_block, (kv_win, seg_win, seg_own, cot_blocks))
    conv = conv.reshape(TOKENS, D)
    grad_kv = intersection_add(back)[FILT - 1:FILT - 1 + TOKENS]
    mixed = (q_row.astype(jnp.float32) * conv).astype(jnp.bfloat16)
    grad_q = (dy_row.astype(jnp.float32) * conv).astype(jnp.bfloat16)
    grad_k = (grad_kv * v_row.astype(jnp.float32)).astype(jnp.bfloat16)
    grad_v = (grad_kv * k_row.astype(jnp.float32)).astype(jnp.bfloat16)
    return (mixed, grad_q, grad_k, grad_v, lax.optimization_barrier(jnp.sum(diag, axis=0)))

def reference(q_proj, k_proj, v_proj, out_grad, contig_starts, filters):
    taps = filters.astype(jnp.float32)
    base_table = skew_rows(jnp.concatenate([taps[:, ::-1], jnp.zeros_like(taps)], axis=1))
    mixed, grad_q, grad_k, grad_v, diag = lax.map(lambda items: one_pack(items, base_table), (q_proj, k_proj, v_proj, out_grad, contig_starts))
    scale = 1.0 / math.sqrt(BATCH * TOKENS * GSIZE)
    filter_grad = lax.optimization_barrier(jnp.sum(diag, axis=0))[:, ::-1] * scale
    return (mixed, grad_q, grad_k, grad_v, filter_grad)
```

```python
import functools
import math

import jax
import jax.numpy as jnp
from jax import lax
from jax.experimental import pallas as pl
from jax.experimental.pallas import tpu as pltpu
from jax.sharding import PartitionSpec as P

GSIZE = 16
LANES = 128
BLOCK = 512


def product(a, b):
    return (a.astype(jnp.float32) * b.astype(jnp.float32)).astype(jnp.bfloat16)


def contig_masks(starts_ref):
    rows = starts_ref.shape[1]
    starts = jnp.broadcast_to(starts_ref[...], (rows, rows)) > 0
    t = lax.broadcasted_iota(jnp.int32, (rows, rows), 0)
    s = lax.broadcasted_iota(jnp.int32, (rows, rows), 1)
    began = jnp.max(jnp.where(starts & (s <= t), s, 0), axis=1, keepdims=True)
    own = (s <= t) & (s >= began)
    first = jnp.min(jnp.where(starts, s, rows), axis=1, keepdims=True)
    previous = (s > t) & (t < first)
    last = jnp.max(jnp.where(starts, s, 0), axis=1, keepdims=True)
    following = (s < t) & (t >= last)
    as_f32 = lambda mask: jnp.where(mask, 1.0, 0.0).astype(jnp.float32)
    return as_f32(own), as_f32(previous), as_f32(following)


def reversed_taps(rows_of_taps):
    taps = rows_of_taps.shape[1]
    i = lax.broadcasted_iota(jnp.int32, (taps, taps), 0)
    j = lax.broadcasted_iota(jnp.int32, (taps, taps), 1)
    flip = jnp.where((i + j == 0) | (i + j == taps), 1.0, 0.0).astype(jnp.float32)
    return jnp.dot(
        rows_of_taps.astype(jnp.float32), flip,
        preferred_element_type=jnp.float32, precision=lax.Precision.HIGHEST,
    )


def lane_groups():
    return lax.broadcasted_iota(jnp.int32, (1, LANES), 1) // GSIZE


def filter_kernel(q_ref, k_ref, v_ref, dy_ref, kv_prev_ref, starts_ref, out_ref, own_ref, prev_ref, sums_ref):
    rows = q_ref.shape[0]
    per_tile = LANES // GSIZE

    @pl.when(pl.program_id(0) == 0)
    def _():
        own, previous, _ = contig_masks(starts_ref)
        own_ref[...] = own
        prev_ref[...] = previous

    group = lane_groups()

    def tile(index, carry):
        lanes = pl.ds(pl.multiple_of(index * LANES, LANES), LANES)
        cot = product(dy_ref[:, lanes], q_ref[:, lanes])
        kv = jnp.concatenate([product(k_ref[:, lanes], v_ref[:, lanes]), kv_prev_ref[:, lanes]], axis=0)
        for g in range(per_tile):
            picked = jnp.where(group == g, cot, jnp.zeros_like(cot))
            pairs = lax.dot_general(
                picked, kv, (((1,), (1,)), ((), ())), preferred_element_type=jnp.float32
            )
            linked = pairs[:, :rows] * own_ref[...] + pairs[:, rows:] * prev_ref[...]
            total = linked[:8]
            for i in range(1, rows // 8):
                total = total + pltpu.roll(linked[8 * i : 8 * i + 8], rows - 8 * i, 1)
            at = pl.multiple_of((index * per_tile + g) * 8, 8)
            sums_ref[pl.ds(at, 8), :] = total
        return carry

    lax.fori_loop(0, q_ref.shape[1] // LANES, tile, 0)
    groups = out_ref.shape[0]
    diagonal = sums_ref[pl.ds(0, groups, stride=8), :]
    for r in range(1, 8):
        diagonal = diagonal + pltpu.roll(sums_ref[pl.ds(r, groups, stride=8), :], rows - r, 1)
    out_ref[...] = reversed_taps(diagonal)


def conv_kernel(
    q_ref, k_ref, v_ref, dy_ref, kv_prev_ref, cot_next_ref, starts_ref, taps_ref,
    mixed_ref, grad_q_ref, grad_k_ref, grad_v_ref,
    fwd_mask_ref, back_mask_ref, taps_scr, flipped_scr,
):
    rows = q_ref.shape[0]
    per_tile = LANES // GSIZE

    @pl.when(pl.program_id(0) == 0)
    def _():
        own, previous, following = contig_masks(starts_ref)
        fwd_mask_ref[:, :rows] = own.astype(jnp.bfloat16)
        fwd_mask_ref[:, rows:] = previous.astype(jnp.bfloat16)
        back_mask_ref[:, :rows] = own.T.astype(jnp.bfloat16)
        back_mask_ref[:, rows:] = following.astype(jnp.bfloat16)

    taps_scr[...] = taps_ref[...].astype(jnp.float32)
    flipped_scr[...] = reversed_taps(taps_ref[...])
    group = lane_groups()

    def circulant(row):
        wide = pltpu.roll(jnp.broadcast_to(row, (rows, rows)), 0, 1, stride=1, stride_axis=0)
        return wide.astype(jnp.bfloat16)

    def tile(index, carry):
        lanes = pl.ds(pl.multiple_of(index * LANES, LANES), LANES)
        q, k, v, dy = (ref[:, lanes] for ref in (q_ref, k_ref, v_ref, dy_ref))
        kv = jnp.concatenate([product(k, v), kv_prev_ref[:, lanes]], axis=0)
        cot = jnp.concatenate([product(dy, q), cot_next_ref[:, lanes]], axis=0)
        at = pl.ds(pl.multiple_of(index * per_tile, per_tile), per_tile)
        taps = taps_scr[at, :]
        flipped = flipped_scr[at, :]
        conv = jnp.zeros((rows, LANES), jnp.float32)
        grad_kv = jnp.zeros((rows, LANES), jnp.float32)
        for g in range(per_tile):
            c = circulant(flipped[g : g + 1])
            table = jnp.concatenate([c, c], axis=1) * fwd_mask_ref[...]
            conv = jnp.where(group == g, jnp.dot(table, kv, preferred_element_type=jnp.float32), conv)
            c = circulant(taps[g : g + 1])
            table = jnp.concatenate([c, c], axis=1) * back_mask_ref[...]
            grad_kv = jnp.where(group == g, jnp.dot(table, cot, preferred_element_type=jnp.float32), grad_kv)
        mixed_ref[:, lanes] = (q.astype(jnp.float32) * conv).astype(jnp.bfloat16)
        grad_q_ref[:, lanes] = (dy.astype(jnp.float32) * conv).astype(jnp.bfloat16)
        grad_k_ref[:, lanes] = (grad_kv * v.astype(jnp.float32)).astype(jnp.bfloat16)
        grad_v_ref[:, lanes] = (grad_kv * k.astype(jnp.float32)).astype(jnp.bfloat16)
        return carry

    lax.fori_loop(0, q_ref.shape[1] // LANES, tile, 0)


def filter_share(q, k, v, dy, kv_prev, starts, groups):
    rows, width = q.shape
    block = math.gcd(width, BLOCK)
    wide = pl.BlockSpec((rows, block), lambda i: (0, i))
    return pl.pallas_call(
        filter_kernel,
        grid=(width // block,),
        out_shape=jax.ShapeDtypeStruct((groups, rows), jnp.float32),
        in_specs=[wide] * 5 + [pl.BlockSpec((1, rows), lambda i: (0, 0))],
        out_specs=pl.BlockSpec((block // GSIZE, rows), lambda i: (i, 0)),
        scratch_shapes=[
            pltpu.VMEM((rows, rows), jnp.float32),
            pltpu.VMEM((rows, rows), jnp.float32),
            pltpu.VMEM((block // GSIZE * 8, rows), jnp.float32),
        ],
        cost_estimate=pl.CostEstimate(
            flops=2 * rows * 2 * rows * width, bytes_accessed=10 * rows * width, transcendentals=0
        ),
        compiler_params=pltpu.CompilerParams(vmem_limit_bytes=24 << 20),
        name="filter_share",
    )(q, k, v, dy, kv_prev, starts)


def convolutions(q, k, v, dy, kv_prev, cot_next, starts, filters):
    rows, width = q.shape
    block = math.gcd(width, BLOCK)
    wide = pl.BlockSpec((rows, block), lambda i: (0, i))
    few = pl.BlockSpec((block // GSIZE, rows), lambda i: (i, 0))
    return pl.pallas_call(
        conv_kernel,
        grid=(width // block,),
        out_shape=[jax.ShapeDtypeStruct((rows, width), jnp.bfloat16)] * 4,
        in_specs=[wide] * 6 + [pl.BlockSpec((1, rows), lambda i: (0, 0)), few],
        out_specs=[wide] * 4,
        scratch_shapes=[
            pltpu.VMEM((rows, 2 * rows), jnp.bfloat16),
            pltpu.VMEM((rows, 2 * rows), jnp.bfloat16),
            pltpu.VMEM((block // GSIZE, rows), jnp.float32),
            pltpu.VMEM((block // GSIZE, rows), jnp.float32),
        ],
        cost_estimate=pl.CostEstimate(
            flops=4 * rows * 2 * rows * width, bytes_accessed=20 * rows * width, transcendentals=0
        ),
        compiler_params=pltpu.CompilerParams(vmem_limit_bytes=24 << 20),
        name="convolutions",
    )(q, k, v, dy, kv_prev, cot_next, starts, filters)


def passed_along(block, axis, distance):
    devices = range(lax.axis_size(axis))
    route = [(i - distance, i) for i in devices if i - distance in devices]
    return lax.ppermute(block, axis, route)


def summed_everywhere(share):
    axes = ("dp", "ctx")
    count = lax.axis_size("dp") * lax.axis_size("ctx")
    if share.shape[0] % count:
        return lax.psum(share, axes)
    part = share.shape[0] // count
    pieces = lax.all_to_all(share.reshape(count, part, -1), axes, 0, 0, tiled=True)
    mine = jnp.sum(pieces, axis=0)
    spread = jnp.broadcast_to(mine[None], pieces.shape)
    return lax.all_to_all(spread, axes, 0, 0, tiled=True).reshape(share.shape)


def per_device(q_proj, k_proj, v_proj, out_grad, contig_starts, filters):
    q, k, v, dy = q_proj[0], k_proj[0], v_proj[0], out_grad[0]
    rows = q.shape[0]
    groups, taps = filters.shape
    assert rows == taps == LANES
    token = lax.broadcasted_iota(jnp.int32, (rows,), 0)
    last = jnp.max(jnp.where(contig_starts[0] > 0, token, 0))
    first = jnp.min(jnp.where(contig_starts[0] > 0, token, rows))
    kv_out = jnp.where((token >= last)[:, None], product(k, v), 0)
    cot_out = jnp.where((token < first)[:, None], product(dy, q), 0)
    kv_prev = passed_along(kv_out, "ctx", 1)
    cot_next = passed_along(cot_out, "ctx", -1)
    share = filter_share(q, k, v, dy, kv_prev, contig_starts, groups)
    scale = 1.0 / math.sqrt(rows * lax.axis_size("ctx") * lax.axis_size("dp") * GSIZE)
    filter_grad = summed_everywhere(share) * scale
    outs = convolutions(q, k, v, dy, kv_prev, cot_next, contig_starts, filters)
    return tuple(out[None] for out in outs) + (filter_grad,)


def solution(mesh):
    wide = P("dp", "ctx", None)
    return jax.shard_map(
        per_device,
        mesh=mesh,
        in_specs=(wide,) * 4 + (P("dp", "ctx"), P()),
        out_specs=(wide,) * 4 + (P(),),
        check_vma=False,
    )
```

```python
import functools
import math

import jax
import jax.numpy as jnp
from jax import lax
from jax.experimental import pallas as pl
from jax.experimental.pallas import tpu as pltpu
from jax.sharding import PartitionSpec as P

GSIZE = 16
LANES = 128
BLOCK = 512


def product(a, b):
    return (a.astype(jnp.float32) * b.astype(jnp.float32)).astype(jnp.bfloat16)


def contig_masks(starts_ref):
    rows = starts_ref.shape[1]
    starts = jnp.broadcast_to(starts_ref[...], (rows, rows)) > 0
    t = lax.broadcasted_iota(jnp.int32, (rows, rows), 0)
    s = lax.broadcasted_iota(jnp.int32, (rows, rows), 1)
    began = jnp.max(jnp.where(starts & (s <= t), s, 0), axis=1, keepdims=True)
    own = (s <= t) & (s >= began)
    first = jnp.min(jnp.where(starts, s, rows), axis=1, keepdims=True)
    previous = (s > t) & (t < first)
    last = jnp.max(jnp.where(starts, s, 0), axis=1, keepdims=True)
    following = (s < t) & (t >= last)
    as_f32 = lambda mask: jnp.where(mask, 1.0, 0.0).astype(jnp.float32)
    return as_f32(own), as_f32(previous), as_f32(following)


def reversed_taps(rows_of_taps):
    taps = rows_of_taps.shape[1]
    i = lax.broadcasted_iota(jnp.int32, (taps, taps), 0)
    j = lax.broadcasted_iota(jnp.int32, (taps, taps), 1)
    flip = jnp.where((i + j == 0) | (i + j == taps), 1.0, 0.0).astype(jnp.float32)
    return jnp.dot(
        rows_of_taps.astype(jnp.float32), flip,
        preferred_element_type=jnp.float32, precision=lax.Precision.HIGHEST,
    )


def lane_groups():
    return lax.broadcasted_iota(jnp.int32, (1, LANES), 1) // GSIZE


def send_kernel(a_ref, b_ref, starts_ref, out_ref, *, tail):
    rows = a_ref.shape[0]
    starts = starts_ref[...] > 0
    lane = lax.broadcasted_iota(jnp.int32, starts.shape, 1)
    token = lax.broadcasted_iota(jnp.int32, (rows, 1), 0)
    if tail:
        keep = token >= jnp.max(jnp.where(starts, lane, 0), axis=1, keepdims=True)
    else:
        keep = token < jnp.min(jnp.where(starts, lane, rows), axis=1, keepdims=True)
    out = a_ref[...].astype(jnp.float32) * b_ref[...].astype(jnp.float32)
    out_ref[...] = jnp.where(keep, out, 0.0).astype(jnp.bfloat16)


def filter_kernel(
    q_ref, k_ref, v_ref, dy_ref, kv_prev_ref, starts_ref, out_ref, own_ref, prev_ref, sums_ref, *, scale
):
    rows = q_ref.shape[0]
    per_tile = LANES // GSIZE

    @pl.when(pl.program_id(0) == 0)
    def _():
        own, previous, _ = contig_masks(starts_ref)
        own_ref[...] = own
        prev_ref[...] = previous

    group = lane_groups()

    def tile(index, carry):
        lanes = pl.ds(pl.multiple_of(index * LANES, LANES), LANES)
        cot = product(dy_ref[:, lanes], q_ref[:, lanes])
        kv = jnp.concatenate([product(k_ref[:, lanes], v_ref[:, lanes]), kv_prev_ref[:, lanes]], axis=0)
        picked = jnp.concatenate(
            [jnp.where(group == g, cot, jnp.zeros_like(cot)) for g in range(per_tile)], axis=0
        )
        pairs = lax.dot_general(
            picked, kv, (((1,), (1,)), ((), ())), preferred_element_type=jnp.float32
        )
        for g in range(per_tile):
            total = None
            for i in range(rows // 8):
                at = g * rows + 8 * i
                piece = (
                    pairs[at : at + 8, :rows] * own_ref[8 * i : 8 * i + 8, :]
                    + pairs[at : at + 8, rows:] * prev_ref[8 * i : 8 * i + 8, :]
                )
                total = piece if i == 0 else total + pltpu.roll(piece, rows - 8 * i, 1)
            at = pl.multiple_of((index * per_tile + g) * 8, 8)
            sums_ref[pl.ds(at, 8), :] = total
        return carry

    lax.fori_loop(0, q_ref.shape[1] // LANES, tile, 0)
    groups = out_ref.shape[0]
    diagonal = sums_ref[pl.ds(0, groups, stride=8), :]
    for r in range(1, 8):
        diagonal = diagonal + pltpu.roll(sums_ref[pl.ds(r, groups, stride=8), :], rows - r, 1)
    out_ref[...] = reversed_taps(diagonal) * scale


def conv_kernel(a_ref, b_ref, other_ref, c_ref, d_ref, starts_ref, taps_ref, out_c_ref, out_d_ref, mask_ref, taps_scr, *, backward):
    rows = a_ref.shape[0]
    per_tile = LANES // GSIZE

    @pl.when(pl.program_id(0) == 0)
    def _():
        own, previous, following = contig_masks(starts_ref)
        mask_ref[:, :rows] = (own.T if backward else own).astype(jnp.bfloat16)
        mask_ref[:, rows:] = (following if backward else previous).astype(jnp.bfloat16)

    taps_scr[...] = taps_ref[...].astype(jnp.float32) if backward else reversed_taps(taps_ref[...])
    group = lane_groups()

    def table(row):
        wide = pltpu.roll(jnp.broadcast_to(row, (rows, rows)), 0, 1, stride=1, stride_axis=0)
        wide = wide.astype(jnp.bfloat16)
        return jnp.concatenate([wide, wide], axis=1) * mask_ref[...]

    def tile(index, carry):
        lanes = pl.ds(pl.multiple_of(index * LANES, LANES), LANES)
        x = jnp.concatenate([product(a_ref[:, lanes], b_ref[:, lanes]), other_ref[:, lanes]], axis=0)
        taps = taps_scr[pl.ds(pl.multiple_of(index * per_tile, per_tile), per_tile), :]
        tables = jnp.concatenate([table(taps[g : g + 1]) for g in range(per_tile)], axis=0)
        every = jnp.dot(tables, x, preferred_element_type=jnp.float32)
        y = every[:rows]
        for g in range(1, per_tile):
            y = jnp.where(group == g, every[g * rows : (g + 1) * rows], y)
        out_c_ref[:, lanes] = (c_ref[:, lanes].astype(jnp.float32) * y).astype(jnp.bfloat16)
        out_d_ref[:, lanes] = (d_ref[:, lanes].astype(jnp.float32) * y).astype(jnp.bfloat16)
        return carry

    lax.fori_loop(0, a_ref.shape[1] // LANES, tile, 0)


def masked_product(a, b, starts, tail):
    rows, width = a.shape
    block = math.gcd(width, BLOCK)
    wide = pl.BlockSpec((rows, block), lambda i: (0, i))
    return pl.pallas_call(
        functools.partial(send_kernel, tail=tail),
        grid=(width // block,),
        out_shape=jax.ShapeDtypeStruct((rows, width), jnp.bfloat16),
        in_specs=[wide] * 2 + [pl.BlockSpec((1, rows), lambda i: (0, 0))],
        out_specs=wide,
        cost_estimate=pl.CostEstimate(flops=2 * rows * width, bytes_accessed=6 * rows * width, transcendentals=0),
        name="sent_kv" if tail else "sent_cot",
    )(a, b, starts)


def filter_share(q, k, v, dy, kv_prev, starts, groups, scale):
    rows, width = q.shape
    block = math.gcd(width, BLOCK)
    wide = pl.BlockSpec((rows, block), lambda i: (0, i))
    return pl.pallas_call(
        functools.partial(filter_kernel, scale=scale),
        grid=(width // block,),
        out_shape=jax.ShapeDtypeStruct((groups, rows), jnp.float32),
        in_specs=[wide] * 5 + [pl.BlockSpec((1, rows), lambda i: (0, 0))],
        out_specs=pl.BlockSpec((block // GSIZE, rows), lambda i: (i, 0)),
        scratch_shapes=[
            pltpu.VMEM((rows, rows), jnp.float32),
            pltpu.VMEM((rows, rows), jnp.float32),
            pltpu.VMEM((block // GSIZE * 8, rows), jnp.float32),
        ],
        cost_estimate=pl.CostEstimate(
            flops=2 * rows * 2 * rows * width, bytes_accessed=10 * rows * width, transcendentals=0
        ),
        compiler_params=pltpu.CompilerParams(vmem_limit_bytes=24 << 20),
        name="filter_share",
    )(q, k, v, dy, kv_prev, starts)


def convolution(a, b, other, c, d, starts, filters, backward):
    rows, width = a.shape
    block = math.gcd(width, BLOCK)
    wide = pl.BlockSpec((rows, block), lambda i: (0, i))
    few = pl.BlockSpec((block // GSIZE, rows), lambda i: (i, 0))
    return pl.pallas_call(
        functools.partial(conv_kernel, backward=backward),
        grid=(width // block,),
        out_shape=[jax.ShapeDtypeStruct((rows, width), jnp.bfloat16)] * 2,
        in_specs=[wide] * 5 + [pl.BlockSpec((1, rows), lambda i: (0, 0)), few],
        out_specs=[wide] * 2,
        scratch_shapes=[
            pltpu.VMEM((rows, 2 * rows), jnp.bfloat16),
            pltpu.VMEM((block // GSIZE, rows), jnp.float32),
        ],
        cost_estimate=pl.CostEstimate(
            flops=2 * rows * 2 * rows * width, bytes_accessed=14 * rows * width, transcendentals=0
        ),
        compiler_params=pltpu.CompilerParams(vmem_limit_bytes=24 << 20),
        name="backward" if backward else "forward",
    )(a, b, other, c, d, starts, filters)


def passed_along(block, axis, distance):
    devices = range(lax.axis_size(axis))
    route = [(i - distance, i) for i in devices if i - distance in devices]
    return lax.ppermute(block, axis, route)


def summed_everywhere(share):
    axes = ("dp", "ctx")
    count = lax.axis_size("dp") * lax.axis_size("ctx")
    if share.shape[0] % count:
        return lax.psum(share, axes)
    part = share.shape[0] // count
    pieces = lax.all_to_all(share.reshape(count, part, -1), axes, 0, 0, tiled=True)
    mine = jnp.sum(pieces, axis=0)
    spread = jnp.broadcast_to(mine[None], pieces.shape)
    return lax.all_to_all(spread, axes, 0, 0, tiled=True).reshape(share.shape)


def per_device(q_proj, k_proj, v_proj, out_grad, contig_starts, filters):
    q, k, v, dy = q_proj[0], k_proj[0], v_proj[0], out_grad[0]
    rows = q.shape[0]
    groups, taps = filters.shape
    assert rows == taps == LANES
    scale = 1.0 / math.sqrt(rows * lax.axis_size("ctx") * lax.axis_size("dp") * GSIZE)
    kv_prev = passed_along(masked_product(k, v, contig_starts, True), "ctx", 1)
    cot_next = passed_along(masked_product(dy, q, contig_starts, False), "ctx", -1)
    share = filter_share(q, k, v, dy, kv_prev, contig_starts, groups, scale)
    filter_grad = summed_everywhere(share)
    mixed, grad_q = convolution(k, v, kv_prev, q, dy, contig_starts, filters, False)
    grad_k, grad_v = convolution(dy, q, cot_next, v, k, contig_starts, filters, True)
    return (mixed[None], grad_q[None], grad_k[None], grad_v[None], filter_grad)


def solution(mesh):
    wide = P("dp", "ctx", None)
    return jax.shard_map(
        per_device,
        mesh=mesh,
        in_specs=(wide,) * 4 + (P("dp", "ctx"), P()),
        out_specs=(wide,) * 4 + (P(),),
        check_vma=False,
    )
```

```python
import functools
import math

import jax
import jax.numpy as jnp
from jax import lax
from jax.experimental import pallas as pl
from jax.experimental.pallas import tpu as pltpu
from jax.sharding import PartitionSpec as P

GSIZE = 16
LANES = 128


def product(a, b):
    return (a.astype(jnp.float32) * b.astype(jnp.float32)).astype(jnp.bfloat16)


def contig_masks(starts_ref):
    rows = starts_ref.shape[1]
    starts = jnp.broadcast_to(starts_ref[...], (rows, rows)) > 0
    t = lax.broadcasted_iota(jnp.int32, (rows, rows), 0)
    s = lax.broadcasted_iota(jnp.int32, (rows, rows), 1)
    began = jnp.max(jnp.where(starts & (s <= t), s, 0), axis=1, keepdims=True)
    own = (s <= t) & (s >= began)
    first = jnp.min(jnp.where(starts, s, rows), axis=1, keepdims=True)
    previous = (s > t) & (t < first)
    last = jnp.max(jnp.where(starts, s, 0), axis=1, keepdims=True)
    following = (s < t) & (t >= last)
    as_f32 = lambda mask: jnp.where(mask, 1.0, 0.0).astype(jnp.float32)
    return as_f32(own), as_f32(previous), as_f32(following)


def reversed_taps(rows_of_taps):
    taps = rows_of_taps.shape[1]
    i = lax.broadcasted_iota(jnp.int32, (taps, taps), 0)
    j = lax.broadcasted_iota(jnp.int32, (taps, taps), 1)
    flip = jnp.where((i + j == 0) | (i + j == taps), 1.0, 0.0).astype(jnp.float32)
    return jnp.dot(
        rows_of_taps.astype(jnp.float32), flip,
        preferred_element_type=jnp.float32, precision=lax.Precision.HIGHEST,
    )


def lane_groups():
    return lax.broadcasted_iota(jnp.int32, (1, LANES), 1) // GSIZE


def send_kernel(a_ref, b_ref, starts_ref, out_ref, *, tail):
    rows = a_ref.shape[0]
    starts = starts_ref[...] > 0
    lane = lax.broadcasted_iota(jnp.int32, starts.shape, 1)
    token = lax.broadcasted_iota(jnp.int32, (rows, 1), 0)
    if tail:
        keep = token >= jnp.max(jnp.where(starts, lane, 0), axis=1, keepdims=True)
    else:
        keep = token < jnp.min(jnp.where(starts, lane, rows), axis=1, keepdims=True)
    out = a_ref[...].astype(jnp.float32) * b_ref[...].astype(jnp.float32)
    out_ref[...] = jnp.where(keep, out, 0.0).astype(jnp.bfloat16)


def filter_kernel(
    q_ref, k_ref, v_ref, dy_ref, kv_prev_ref, starts_ref, out_ref, own_ref, prev_ref, sums_ref, *, scale
):
    rows = q_ref.shape[0]
    per_tile = LANES // GSIZE

    own_ref[...], prev_ref[...], _ = contig_masks(starts_ref)

    group = lane_groups()

    def tile(index, carry):
        lanes = pl.ds(pl.multiple_of(index * LANES, LANES), LANES)
        cot = product(dy_ref[:, lanes], q_ref[:, lanes])
        kv = jnp.concatenate([product(k_ref[:, lanes], v_ref[:, lanes]), kv_prev_ref[:, lanes]], axis=0)
        picked = jnp.concatenate(
            [jnp.where(group == g, cot, jnp.zeros_like(cot)) for g in range(per_tile)], axis=0
        )
        pairs = lax.dot_general(
            picked, kv, (((1,), (1,)), ((), ())), preferred_element_type=jnp.float32
        )
        for g in range(per_tile):
            total = None
            for i in range(rows // 8):
                at = g * rows + 8 * i
                piece = (
                    pairs[at : at + 8, :rows] * own_ref[8 * i : 8 * i + 8, :]
                    + pairs[at : at + 8, rows:] * prev_ref[8 * i : 8 * i + 8, :]
                )
                total = piece if i == 0 else total + pltpu.roll(piece, rows - 8 * i, 1)
            at = pl.multiple_of((index * per_tile + g) * 8, 8)
            sums_ref[pl.ds(at, 8), :] = total
        return carry

    lax.fori_loop(0, q_ref.shape[1] // LANES, tile, 0)
    groups = out_ref.shape[0]
    diagonal = sums_ref[pl.ds(0, groups, stride=8), :]
    for r in range(1, 8):
        diagonal = diagonal + pltpu.roll(sums_ref[pl.ds(r, groups, stride=8), :], rows - r, 1)
    out_ref[...] = reversed_taps(diagonal) * scale


def conv_kernel(a_ref, b_ref, other_ref, c_ref, d_ref, starts_ref, taps_ref, out_c_ref, out_d_ref, mask_ref, taps_scr, *, backward):
    rows = a_ref.shape[0]
    per_tile = LANES // GSIZE

    own, previous, following = contig_masks(starts_ref)
    mask_ref[:, :rows] = (own.T if backward else own).astype(jnp.bfloat16)
    mask_ref[:, rows:] = (following if backward else previous).astype(jnp.bfloat16)
    taps_scr[...] = taps_ref[...].astype(jnp.float32) if backward else reversed_taps(taps_ref[...])
    group = lane_groups()

    def table(row):
        wide = pltpu.roll(jnp.broadcast_to(row, (rows, rows)), 0, 1, stride=1, stride_axis=0)
        wide = wide.astype(jnp.bfloat16)
        return jnp.concatenate([wide, wide], axis=1) * mask_ref[...]

    def tile(index, carry):
        lanes = pl.ds(pl.multiple_of(index * LANES, LANES), LANES)
        x = jnp.concatenate([product(a_ref[:, lanes], b_ref[:, lanes]), other_ref[:, lanes]], axis=0)
        taps = taps_scr[pl.ds(pl.multiple_of(index * per_tile, per_tile), per_tile), :]
        tables = jnp.concatenate([table(taps[g : g + 1]) for g in range(per_tile)], axis=0)
        every = jnp.dot(tables, x, preferred_element_type=jnp.float32)
        y = every[:rows]
        for g in range(1, per_tile):
            y = jnp.where(group == g, every[g * rows : (g + 1) * rows], y)
        out_c_ref[:, lanes] = (c_ref[:, lanes].astype(jnp.float32) * y).astype(jnp.bfloat16)
        out_d_ref[:, lanes] = (d_ref[:, lanes].astype(jnp.float32) * y).astype(jnp.bfloat16)
        return carry

    lax.fori_loop(0, a_ref.shape[1] // LANES, tile, 0)


VMEM = pl.BlockSpec(memory_space=pltpu.VMEM)


def local_call(kernel, name, out_shape, scratch_shapes, flops, operands):
    outs = out_shape if isinstance(out_shape, list) else [out_shape]
    moved = sum(math.prod(x.shape) * x.dtype.itemsize for x in [*operands, *outs])
    return pl.pallas_call(
        kernel,
        out_shape=out_shape,
        in_specs=[VMEM] * len(operands),
        out_specs=[VMEM] * len(outs) if isinstance(out_shape, list) else VMEM,
        scratch_shapes=scratch_shapes,
        cost_estimate=pl.CostEstimate(flops=flops, bytes_accessed=moved, transcendentals=0),
        compiler_params=pltpu.CompilerParams(vmem_limit_bytes=24 << 20),
        name=name,
    )(*operands)


def masked_product(a, b, starts, tail):
    return local_call(
        functools.partial(send_kernel, tail=tail),
        "sent_kv" if tail else "sent_cot",
        jax.ShapeDtypeStruct(a.shape, jnp.bfloat16), [], 2 * a.size, (a, b, starts),
    )


def filter_share(q, k, v, dy, kv_prev, starts, groups, scale):
    rows, width = q.shape
    table = pltpu.VMEM((rows, rows), jnp.float32)
    return local_call(
        functools.partial(filter_kernel, scale=scale),
        "filter_share",
        jax.ShapeDtypeStruct((groups, rows), jnp.float32),
        [table, table, pltpu.VMEM((groups * 8, rows), jnp.float32)],
        32 * rows * rows * width,
        (q, k, v, dy, kv_prev, starts),
    )


def convolution(a, b, other, c, d, starts, filters, backward):
    rows, width = a.shape
    return local_call(
        functools.partial(conv_kernel, backward=backward),
        "backward" if backward else "forward",
        [jax.ShapeDtypeStruct((rows, width), jnp.bfloat16)] * 2,
        [pltpu.VMEM((rows, 2 * rows), jnp.bfloat16), pltpu.VMEM(filters.shape, jnp.float32)],
        32 * rows * rows * width,
        (a, b, other, c, d, starts, filters),
    )


def passed_along(block, axis, distance):
    devices = range(lax.axis_size(axis))
    route = [(i - distance, i) for i in devices if i - distance in devices]
    return lax.ppermute(block, axis, route)


def summed_everywhere(share):
    groups, taps = share.shape
    ctx, dp = lax.axis_size("ctx"), lax.axis_size("dp")
    part = -(-groups // ctx)
    padded = jnp.pad(share, ((0, part * ctx - groups), (0, 0))).reshape(ctx, part, taps)
    mine = jnp.sum(lax.all_to_all(padded, "ctx", 0, 0, tiled=True), axis=0)
    spread = jnp.broadcast_to(mine[None], (dp, part, taps))
    mine = jnp.sum(lax.all_to_all(spread, "dp", 0, 0, tiled=True), axis=0)
    spread = jnp.broadcast_to(mine[None], (ctx, part, taps))
    every = lax.all_to_all(spread, "ctx", 0, 0, tiled=True)
    return every.reshape(ctx * part, taps)[:groups]


def per_device(q_proj, k_proj, v_proj, out_grad, contig_starts, filters):
    q, k, v, dy = q_proj[0], k_proj[0], v_proj[0], out_grad[0]
    rows = q.shape[0]
    groups, taps = filters.shape
    assert rows == taps == LANES
    scale = 1.0 / math.sqrt(rows * lax.axis_size("ctx") * lax.axis_size("dp") * GSIZE)
    kv_prev = passed_along(masked_product(k, v, contig_starts, True), "ctx", 1)
    cot_next = passed_along(masked_product(dy, q, contig_starts, False), "ctx", -1)
    share = filter_share(q, k, v, dy, kv_prev, contig_starts, groups, scale)
    filter_grad = summed_everywhere(share)
    mixed, grad_q = convolution(k, v, kv_prev, q, dy, contig_starts, filters, False)
    grad_k, grad_v = convolution(dy, q, cot_next, v, k, contig_starts, filters, True)
    return (mixed[None], grad_q[None], grad_k[None], grad_v[None], filter_grad)


def solution(mesh):
    wide = P("dp", "ctx", None)
    return jax.shard_map(
        per_device,
        mesh=mesh,
        in_specs=(wide,) * 4 + (P("dp", "ctx"), P()),
        out_specs=(wide,) * 4 + (P(),),
        check_vma=False,
    )
```

```python
import functools
import math

import jax
import jax.numpy as jnp
from jax import lax
from jax.experimental import pallas as pl
from jax.experimental.pallas import tpu as pltpu
from jax.sharding import PartitionSpec as P

GSIZE = 16
LANES = 128


def product(a, b):
    return (a.astype(jnp.float32) * b.astype(jnp.float32)).astype(jnp.bfloat16)


def contig_masks(starts_ref):
    rows = starts_ref.shape[1]
    starts = jnp.broadcast_to(starts_ref[...], (rows, rows)) > 0
    t = lax.broadcasted_iota(jnp.int32, (rows, rows), 0)
    s = lax.broadcasted_iota(jnp.int32, (rows, rows), 1)
    began = jnp.max(jnp.where(starts & (s <= t), s, 0), axis=1, keepdims=True)
    own = (s <= t) & (s >= began)
    first = jnp.min(jnp.where(starts, s, rows), axis=1, keepdims=True)
    previous = (s > t) & (t < first)
    last = jnp.max(jnp.where(starts, s, 0), axis=1, keepdims=True)
    following = (s < t) & (t >= last)
    as_f32 = lambda mask: jnp.where(mask, 1.0, 0.0).astype(jnp.float32)
    return as_f32(own), as_f32(previous), as_f32(following)


def reversed_taps(rows_of_taps):
    taps = rows_of_taps.shape[1]
    i = lax.broadcasted_iota(jnp.int32, (taps, taps), 0)
    j = lax.broadcasted_iota(jnp.int32, (taps, taps), 1)
    flip = jnp.where((i + j == 0) | (i + j == taps), 1.0, 0.0).astype(jnp.float32)
    return jnp.dot(
        rows_of_taps.astype(jnp.float32), flip,
        preferred_element_type=jnp.float32, precision=lax.Precision.HIGHEST,
    )


def lane_groups():
    return lax.broadcasted_iota(jnp.int32, (1, LANES), 1) // GSIZE


def each_tile(tile, width):
    count = width // LANES
    step = math.gcd(count, 4)

    def body(i, carry):
        for j in range(step):
            tile(i * step + j)
        return carry

    lax.fori_loop(0, count // step, body, 0)


def kept_rows(starts_ref, rows, tail):
    starts = starts_ref[...] > 0
    lane = lax.broadcasted_iota(jnp.int32, starts.shape, 1)
    token = lax.broadcasted_iota(jnp.int32, (rows, 1), 0)
    if tail:
        return token >= jnp.max(jnp.where(starts, lane, 0), axis=1, keepdims=True)
    return token < jnp.min(jnp.where(starts, lane, rows), axis=1, keepdims=True)


def sent_product(a, b, keep):
    out = a.astype(jnp.float32) * b.astype(jnp.float32)
    return jnp.where(keep, out, 0.0).astype(jnp.bfloat16)


def sent_cot_kernel(a_ref, b_ref, starts_ref, out_ref):
    out_ref[...] = sent_product(a_ref[...], b_ref[...], kept_rows(starts_ref, a_ref.shape[0], False))


def sent_kv_kernel(a_hbm, b_hbm, starts_hbm, out_ref, a_ref, b_ref, starts_ref, sems):
    rows = a_ref.shape[0]
    half = rows // 2
    copies = [pltpu.make_async_copy(starts_hbm, starts_ref, sems.at[0])]
    for h in range(2):
        part = pl.ds(h * half, half)
        copies.append(pltpu.make_async_copy(a_hbm.at[part], a_ref.at[part], sems.at[2 * h + 1]))
        copies.append(pltpu.make_async_copy(b_hbm.at[part], b_ref.at[part], sems.at[2 * h + 2]))
    for copy in copies:
        copy.start()
    copies[0].wait()
    keep = kept_rows(starts_ref, rows, True)
    for h in range(2):
        copies[2 * h + 1].wait()
        copies[2 * h + 2].wait()
        at = slice(h * half, (h + 1) * half)
        out_ref[at, :] = sent_product(a_ref[at, :], b_ref[at, :], keep[at])


def filter_kernel(
    q_ref, k_ref, v_ref, dy_ref, kv_prev_ref, starts_ref, out_ref, own_ref, prev_ref, sums_ref, *, scale
):
    rows = q_ref.shape[0]
    per_tile = LANES // GSIZE

    own_ref[...], prev_ref[...], _ = contig_masks(starts_ref)

    group = lane_groups()

    def tile(index):
        lanes = pl.ds(pl.multiple_of(index * LANES, LANES), LANES)
        cot = product(dy_ref[:, lanes], q_ref[:, lanes])
        kv = jnp.concatenate([product(k_ref[:, lanes], v_ref[:, lanes]), kv_prev_ref[:, lanes]], axis=0)
        for g in range(per_tile):
            picked = jnp.where(group == g, cot, jnp.zeros_like(cot))
            pairs = lax.dot_general(
                picked, kv, (((1,), (1,)), ((), ())), preferred_element_type=jnp.float32
            )
            linked = pairs[:, :rows] * own_ref[...] + pairs[:, rows:] * prev_ref[...]
            total = linked[:8]
            for i in range(1, rows // 8):
                total = total + pltpu.roll(linked[8 * i : 8 * i + 8], rows - 8 * i, 1)
            at = pl.multiple_of((index * per_tile + g) * 8, 8)
            sums_ref[pl.ds(at, 8), :] = total

    each_tile(tile, q_ref.shape[1])
    groups = out_ref.shape[0]
    diagonal = sums_ref[pl.ds(0, groups, stride=8), :]
    for r in range(1, 8):
        diagonal = diagonal + pltpu.roll(sums_ref[pl.ds(r, groups, stride=8), :], rows - r, 1)
    out_ref[...] = reversed_taps(diagonal) * scale


def conv_kernel(a_ref, b_ref, other_ref, c_ref, d_ref, starts_ref, taps_ref, out_c_ref, out_d_ref, mask_ref, taps_scr, *, backward):
    rows = a_ref.shape[0]
    per_tile = LANES // GSIZE

    own, previous, following = contig_masks(starts_ref)
    mask_ref[:, :rows] = (own.T if backward else own).astype(jnp.bfloat16)
    mask_ref[:, rows:] = (following if backward else previous).astype(jnp.bfloat16)
    taps_scr[...] = taps_ref[...].astype(jnp.float32) if backward else reversed_taps(taps_ref[...])
    group = lane_groups()

    def table(row):
        wide = pltpu.roll(jnp.broadcast_to(row, (rows, rows)), 0, 1, stride=1, stride_axis=0)
        wide = wide.astype(jnp.bfloat16)
        return jnp.concatenate([wide, wide], axis=1) * mask_ref[...]

    def tile(index):
        lanes = pl.ds(pl.multiple_of(index * LANES, LANES), LANES)
        x = jnp.concatenate([product(a_ref[:, lanes], b_ref[:, lanes]), other_ref[:, lanes]], axis=0)
        taps = taps_scr[pl.ds(pl.multiple_of(index * per_tile, per_tile), per_tile), :]
        y = jnp.zeros((rows, LANES), jnp.float32)
        for g in range(per_tile):
            y = jnp.where(group == g, jnp.dot(table(taps[g : g + 1]), x, preferred_element_type=jnp.float32), y)
        out_c_ref[:, lanes] = (c_ref[:, lanes].astype(jnp.float32) * y).astype(jnp.bfloat16)
        out_d_ref[:, lanes] = (d_ref[:, lanes].astype(jnp.float32) * y).astype(jnp.bfloat16)

    each_tile(tile, a_ref.shape[1])


VMEM = pl.BlockSpec(memory_space=pltpu.VMEM)


def local_call(kernel, name, out_shape, scratch_shapes, flops, operands, placed=VMEM):
    outs = out_shape if isinstance(out_shape, list) else [out_shape]
    moved = sum(math.prod(x.shape) * x.dtype.itemsize for x in [*operands, *outs])
    return pl.pallas_call(
        kernel,
        out_shape=out_shape,
        in_specs=[placed] * len(operands),
        out_specs=[VMEM] * len(outs) if isinstance(out_shape, list) else VMEM,
        scratch_shapes=scratch_shapes,
        cost_estimate=pl.CostEstimate(flops=flops, bytes_accessed=moved, transcendentals=0),
        compiler_params=pltpu.CompilerParams(vmem_limit_bytes=24 << 20),
        name=name,
    )(*operands)


def sent_kv(k, v, starts):
    whole = pltpu.VMEM(k.shape, k.dtype)
    return local_call(
        sent_kv_kernel, "sent_kv", jax.ShapeDtypeStruct(k.shape, jnp.bfloat16),
        [whole, whole, pltpu.VMEM(starts.shape, starts.dtype), pltpu.SemaphoreType.DMA((5,))],
        2 * k.size, (k, v, starts), pl.BlockSpec(memory_space=pltpu.HBM),
    )


def sent_cot(dy, q, starts):
    return local_call(
        sent_cot_kernel, "sent_cot", jax.ShapeDtypeStruct(q.shape, jnp.bfloat16),
        [], 2 * q.size, (dy, q, starts),
    )


def filter_share(q, k, v, dy, kv_prev, starts, groups, scale):
    rows, width = q.shape
    table = pltpu.VMEM((rows, rows), jnp.float32)
    return local_call(
        functools.partial(filter_kernel, scale=scale),
        "filter_share",
        jax.ShapeDtypeStruct((groups, rows), jnp.float32),
        [table, table, pltpu.VMEM((groups * 8, rows), jnp.float32)],
        32 * rows * rows * width,
        (q, k, v, dy, kv_prev, starts),
    )


def convolution(a, b, other, c, d, starts, filters, backward):
    rows, width = a.shape
    return local_call(
        functools.partial(conv_kernel, backward=backward),
        "backward" if backward else "forward",
        [jax.ShapeDtypeStruct((rows, width), jnp.bfloat16)] * 2,
        [pltpu.VMEM((rows, 2 * rows), jnp.bfloat16), pltpu.VMEM(filters.shape, jnp.float32)],
        32 * rows * rows * width,
        (a, b, other, c, d, starts, filters),
    )


def passed_along(block, axis, distance):
    devices = range(lax.axis_size(axis))
    route = [(i - distance, i) for i in devices if i - distance in devices]
    return lax.ppermute(block, axis, route)


def factors(size):
    found, p = [], 2
    while size > 1:
        while size % p == 0:
            found.append(p)
            size //= p
        p += 1
    return found


def summed_along(total, axis):
    size = lax.axis_size(axis)
    stride = 1
    for p in factors(size):
        turned = lambda i, k: i + ((i // stride + k) % p - i // stride % p) * stride
        got = [
            lax.ppermute(total, axis, [(turned(i, k), i) for i in range(size)]) for k in range(1, p)
        ]
        if p == 2:
            total = total + got[0]
        else:
            digit = lax.axis_index(axis) // stride % p
            total = jnp.sum(jnp.roll(jnp.stack([total, *got]), digit, axis=0), axis=0)
        stride *= p
    return total


def per_device(q_proj, k_proj, v_proj, out_grad, contig_starts, filters):
    q, k, v, dy = q_proj[0], k_proj[0], v_proj[0], out_grad[0]
    rows = q.shape[0]
    groups, taps = filters.shape
    assert rows == taps == LANES
    scale = 1.0 / math.sqrt(rows * lax.axis_size("ctx") * lax.axis_size("dp") * GSIZE)
    kv_prev = passed_along(sent_kv(k, v, contig_starts), "ctx", 1)
    cot_next = passed_along(sent_cot(dy, q, contig_starts), "ctx", -1)
    share = filter_share(q, k, v, dy, kv_prev, contig_starts, groups, scale)
    filter_grad = summed_along(summed_along(share, "ctx"), "dp")
    mixed, grad_q = convolution(k, v, kv_prev, q, dy, contig_starts, filters, False)
    grad_k, grad_v = convolution(dy, q, cot_next, v, k, contig_starts, filters, True)
    return (mixed[None], grad_q[None], grad_k[None], grad_v[None], filter_grad)


def solution(mesh):
    wide = P("dp", "ctx", None)
    return jax.shard_map(
        per_device,
        mesh=mesh,
        in_specs=(wide,) * 4 + (P("dp", "ctx"), P()),
        out_specs=(wide,) * 4 + (P(),),
        check_vma=False,
    )
```

```python
import functools
import math

import jax
import jax.numpy as jnp
from jax import lax
from jax.experimental import pallas as pl
from jax.experimental.pallas import tpu as pltpu
from jax.sharding import PartitionSpec as P

GSIZE = 16
LANES = 128


def product(a, b):
    return (a.astype(jnp.float32) * b.astype(jnp.float32)).astype(jnp.bfloat16)


def contig_masks(starts_ref):
    rows = starts_ref.shape[1]
    starts = jnp.broadcast_to(starts_ref[...], (rows, rows)) > 0
    t = lax.broadcasted_iota(jnp.int32, (rows, rows), 0)
    s = lax.broadcasted_iota(jnp.int32, (rows, rows), 1)
    began = jnp.max(jnp.where(starts & (s <= t), s, 0), axis=1, keepdims=True)
    own = (s <= t) & (s >= began)
    first = jnp.min(jnp.where(starts, s, rows), axis=1, keepdims=True)
    previous = (s > t) & (t < first)
    last = jnp.max(jnp.where(starts, s, 0), axis=1, keepdims=True)
    following = (s < t) & (t >= last)
    as_f32 = lambda mask: jnp.where(mask, 1.0, 0.0).astype(jnp.float32)
    return as_f32(own), as_f32(previous), as_f32(following)


def reversed_taps(rows_of_taps):
    taps = rows_of_taps.shape[1]
    i = lax.broadcasted_iota(jnp.int32, (taps, taps), 0)
    j = lax.broadcasted_iota(jnp.int32, (taps, taps), 1)
    flip = jnp.where((i + j == 0) | (i + j == taps), 1.0, 0.0).astype(jnp.float32)
    return jnp.dot(
        rows_of_taps.astype(jnp.float32), flip,
        preferred_element_type=jnp.float32, precision=lax.Precision.HIGHEST,
    )


def lane_groups():
    return lax.broadcasted_iota(jnp.int32, (1, LANES), 1) // GSIZE


def each_tile(tile, width):
    count = width // LANES
    step = math.gcd(count, 4)

    def body(i, carry):
        for j in range(step):
            tile(i * step + j)
        return carry

    lax.fori_loop(0, count // step, body, 0)


def kept_rows(starts_ref, rows, tail):
    starts = starts_ref[...] > 0
    lane = lax.broadcasted_iota(jnp.int32, starts.shape, 1)
    token = lax.broadcasted_iota(jnp.int32, (rows, 1), 0)
    if tail:
        return token >= jnp.max(jnp.where(starts, lane, 0), axis=1, keepdims=True)
    return token < jnp.min(jnp.where(starts, lane, rows), axis=1, keepdims=True)


def sent_product(a, b, keep):
    out = a.astype(jnp.float32) * b.astype(jnp.float32)
    return jnp.where(keep, out, 0.0).astype(jnp.bfloat16)


def sent_kv_kernel(a_hbm, b_hbm, starts_hbm, out_ref, a_ref, b_ref, starts_ref, sems):
    rows = a_ref.shape[0]
    half = rows // 2
    copies = [pltpu.make_async_copy(starts_hbm, starts_ref, sems.at[0])]
    for h in range(2):
        part = pl.ds(h * half, half)
        copies.append(pltpu.make_async_copy(a_hbm.at[part], a_ref.at[part], sems.at[2 * h + 1]))
        copies.append(pltpu.make_async_copy(b_hbm.at[part], b_ref.at[part], sems.at[2 * h + 2]))
    for copy in copies:
        copy.start()
    copies[0].wait()
    keep = kept_rows(starts_ref, rows, True)
    for h in range(2):
        copies[2 * h + 1].wait()
        copies[2 * h + 2].wait()
        at = slice(h * half, (h + 1) * half)
        out_ref[at, :] = sent_product(a_ref[at, :], b_ref[at, :], keep[at])


def filter_kernel(
    q_ref, k_ref, v_ref, dy_ref, kv_prev_ref, starts_ref, out_ref, own_ref, prev_ref, sums_ref, *, scale
):
    rows = q_ref.shape[0]
    per_tile = LANES // GSIZE

    own_ref[...], prev_ref[...], _ = contig_masks(starts_ref)

    group = lane_groups()

    def tile(index):
        lanes = pl.ds(pl.multiple_of(index * LANES, LANES), LANES)
        cot = product(dy_ref[:, lanes], q_ref[:, lanes])
        kv = jnp.concatenate([product(k_ref[:, lanes], v_ref[:, lanes]), kv_prev_ref[:, lanes]], axis=0)
        for g in range(per_tile):
            picked = jnp.where(group == g, cot, jnp.zeros_like(cot))
            pairs = lax.dot_general(
                picked, kv, (((1,), (1,)), ((), ())), preferred_element_type=jnp.float32
            )
            linked = pairs[:, :rows] * own_ref[...] + pairs[:, rows:] * prev_ref[...]
            total = linked[:8]
            for i in range(1, rows // 8):
                total = total + pltpu.roll(linked[8 * i : 8 * i + 8], rows - 8 * i, 1)
            at = pl.multiple_of((index * per_tile + g) * 8, 8)
            sums_ref[pl.ds(at, 8), :] = total

    each_tile(tile, q_ref.shape[1])
    groups = out_ref.shape[0]
    diagonal = sums_ref[pl.ds(0, groups, stride=8), :]
    for r in range(1, 8):
        diagonal = diagonal + pltpu.roll(sums_ref[pl.ds(r, groups, stride=8), :], rows - r, 1)
    out_ref[...] = reversed_taps(diagonal) * scale


def tables_kernel(q_ref, dy_ref, starts_ref, taps_ref, sent_cot_ref, fwd_ref, back_ref, fwd_mask_ref, back_mask_ref):
    rows = q_ref.shape[0]
    groups = taps_ref.shape[0]
    own, previous, following = contig_masks(starts_ref)
    fwd_mask_ref[:, :rows] = own.astype(jnp.bfloat16)
    fwd_mask_ref[:, rows:] = previous.astype(jnp.bfloat16)
    back_mask_ref[:, :rows] = own.T.astype(jnp.bfloat16)
    back_mask_ref[:, rows:] = following.astype(jnp.bfloat16)
    sent_cot_ref[...] = sent_product(dy_ref[...], q_ref[...], kept_rows(starts_ref, rows, False))

    def circulant(row):
        wide = pltpu.roll(jnp.broadcast_to(row, (rows, rows)), 0, 1, stride=1, stride_axis=0)
        return wide.astype(jnp.bfloat16)

    def some(i, carry):
        at = pl.multiple_of(i * 16, 16)
        taps = taps_ref[pl.ds(at, 16), :].astype(jnp.float32)
        flipped = reversed_taps(taps)
        for g in range(16):
            wide = circulant(flipped[g : g + 1])
            fwd_ref[at + g, :, :rows] = wide * fwd_mask_ref[:, :rows]
            fwd_ref[at + g, :, rows:] = wide * fwd_mask_ref[:, rows:]
            wide = circulant(taps[g : g + 1])
            back_ref[at + g, :, :rows] = wide * back_mask_ref[:, :rows]
            back_ref[at + g, :, rows:] = wide * back_mask_ref[:, rows:]
        return carry

    lax.fori_loop(0, groups // 16, some, 0)


def conv_kernel(a_ref, b_ref, other_ref, c_ref, d_ref, tables_ref, out_c_ref, out_d_ref):
    rows = a_ref.shape[0]
    per_tile = LANES // GSIZE
    group = lane_groups()

    def tile(index):
        lanes = pl.ds(pl.multiple_of(index * LANES, LANES), LANES)
        x = jnp.concatenate([product(a_ref[:, lanes], b_ref[:, lanes]), other_ref[:, lanes]], axis=0)
        y = jnp.zeros((rows, LANES), jnp.float32)
        for g in range(per_tile):
            table = tables_ref[index * per_tile + g]
            y = jnp.where(group == g, jnp.dot(table, x, preferred_element_type=jnp.float32), y)
        out_c_ref[:, lanes] = (c_ref[:, lanes].astype(jnp.float32) * y).astype(jnp.bfloat16)
        out_d_ref[:, lanes] = (d_ref[:, lanes].astype(jnp.float32) * y).astype(jnp.bfloat16)

    each_tile(tile, a_ref.shape[1])


VMEM = pl.BlockSpec(memory_space=pltpu.VMEM)


def local_call(kernel, name, out_shape, scratch_shapes, flops, operands, placed=VMEM, limit=24):
    outs = out_shape if isinstance(out_shape, list) else [out_shape]
    moved = sum(math.prod(x.shape) * x.dtype.itemsize for x in [*operands, *outs])
    return pl.pallas_call(
        kernel,
        out_shape=out_shape,
        in_specs=[placed] * len(operands),
        out_specs=[VMEM] * len(outs) if isinstance(out_shape, list) else VMEM,
        scratch_shapes=scratch_shapes,
        cost_estimate=pl.CostEstimate(flops=flops, bytes_accessed=moved, transcendentals=0),
        compiler_params=pltpu.CompilerParams(vmem_limit_bytes=limit << 20),
        name=name,
    )(*operands)


def sent_kv(k, v, starts):
    whole = pltpu.VMEM(k.shape, k.dtype)
    return local_call(
        sent_kv_kernel, "sent_kv", jax.ShapeDtypeStruct(k.shape, jnp.bfloat16),
        [whole, whole, pltpu.VMEM(starts.shape, starts.dtype), pltpu.SemaphoreType.DMA((5,))],
        2 * k.size, (k, v, starts), pl.BlockSpec(memory_space=pltpu.HBM), 60,
    )


def tables_and_cot(q, dy, starts, filters):
    rows, width = q.shape
    groups = filters.shape[0]
    tables = jax.ShapeDtypeStruct((groups, rows, 2 * rows), jnp.bfloat16)
    mask = pltpu.VMEM((rows, 2 * rows), jnp.bfloat16)
    return local_call(
        tables_kernel, "tables", [jax.ShapeDtypeStruct((rows, width), jnp.bfloat16), tables, tables],
        [mask, mask], 64 * rows * rows * width, (q, dy, starts, filters),
    )


def filter_share(q, k, v, dy, kv_prev, starts, groups, scale):
    rows, width = q.shape
    table = pltpu.VMEM((rows, rows), jnp.float32)
    return local_call(
        functools.partial(filter_kernel, scale=scale), "filter_share",
        jax.ShapeDtypeStruct((groups, rows), jnp.float32),
        [table, table, pltpu.VMEM((groups * 8, rows), jnp.float32)],
        32 * rows * rows * width, (q, k, v, dy, kv_prev, starts),
    )


def convolution(a, b, other, c, d, tables, name):
    rows, width = a.shape
    out = jax.ShapeDtypeStruct((rows, width), jnp.bfloat16)
    return local_call(
        conv_kernel, name, [out, out], [], 32 * rows * rows * width, (a, b, other, c, d, tables)
    )


def passed_along(block, axis, distance):
    devices = range(lax.axis_size(axis))
    route = [(i - distance, i) for i in devices if i - distance in devices]
    return lax.ppermute(block, axis, route)


def factors(size):
    found, p = [], 2
    while size > 1:
        while size % p == 0:
            found.append(p)
            size //= p
        p += 1
    return found


def summed_everywhere(total, beside):
    done = 0
    for axis in ("ctx", "dp"):
        size = lax.axis_size(axis)
        stride = 1
        for p in factors(size):
            if done in beside:
                total, _ = lax.optimization_barrier((total, beside[done]))
            turned = lambda i, k: i + ((i // stride + k) % p - i // stride % p) * stride
            got = [
                lax.ppermute(total, axis, [(turned(i, k), i) for i in range(size)]) for k in range(1, p)
            ]
            if p == 2:
                total = total + got[0]
            else:
                digit = lax.axis_index(axis) // stride % p
                total = jnp.sum(jnp.roll(jnp.stack([total, *got]), digit, axis=0), axis=0)
            stride *= p
            done += 1
    return total


def per_device(q_proj, k_proj, v_proj, out_grad, contig_starts, filters):
    q, k, v, dy = q_proj[0], k_proj[0], v_proj[0], out_grad[0]
    rows = q.shape[0]
    groups, taps = filters.shape
    assert rows == taps == LANES
    scale = 1.0 / math.sqrt(rows * lax.axis_size("ctx") * lax.axis_size("dp") * GSIZE)
    kv_prev = passed_along(sent_kv(k, v, contig_starts), "ctx", 1)
    cot_out, fwd_tables, back_tables = tables_and_cot(q, dy, contig_starts, filters)
    cot_next = passed_along(cot_out, "ctx", -1)
    share = filter_share(q, k, v, dy, kv_prev, contig_starts, groups, scale)
    mixed, grad_q = convolution(k, v, kv_prev, q, dy, fwd_tables, "forward")
    grad_k, grad_v = convolution(dy, q, cot_next, v, k, back_tables, "backward")
    beside = {2: (mixed, grad_q), 4: (grad_k, grad_v)}
    filter_grad = summed_everywhere(share, beside)
    return (mixed[None], grad_q[None], grad_k[None], grad_v[None], filter_grad)


def solution(mesh):
    wide = P("dp", "ctx", None)
    return jax.shard_map(
        per_device,
        mesh=mesh,
        in_specs=(wide,) * 4 + (P("dp", "ctx"), P()),
        out_specs=(wide,) * 4 + (P(),),
        check_vma=False,
    )
```

```python
import functools
import math

import jax
import jax.numpy as jnp
from jax import lax
from jax.experimental import pallas as pl
from jax.experimental.pallas import tpu as pltpu
from jax.sharding import PartitionSpec as P

GSIZE = 16
LANES = 128
STEP = 4


def product(a, b):
    return (a.astype(jnp.float32) * b.astype(jnp.float32)).astype(jnp.bfloat16)


def contig_masks(starts_ref):
    rows = starts_ref.shape[1]
    starts = jnp.broadcast_to(starts_ref[...], (rows, rows)) > 0
    t = lax.broadcasted_iota(jnp.int32, (rows, rows), 0)
    s = lax.broadcasted_iota(jnp.int32, (rows, rows), 1)
    began = jnp.max(jnp.where(starts & (s <= t), s, 0), axis=1, keepdims=True)
    own = (s <= t) & (s >= began)
    first = jnp.min(jnp.where(starts, s, rows), axis=1, keepdims=True)
    previous = (s > t) & (t < first)
    last = jnp.max(jnp.where(starts, s, 0), axis=1, keepdims=True)
    following = (s < t) & (t >= last)
    as_f32 = lambda mask: jnp.where(mask, 1.0, 0.0).astype(jnp.float32)
    return as_f32(own), as_f32(previous), as_f32(following)


def reversed_taps(rows_of_taps):
    taps = rows_of_taps.shape[1]
    i = lax.broadcasted_iota(jnp.int32, (taps, taps), 0)
    j = lax.broadcasted_iota(jnp.int32, (taps, taps), 1)
    flip = jnp.where((i + j == 0) | (i + j == taps), 1.0, 0.0).astype(jnp.float32)
    return jnp.dot(
        rows_of_taps.astype(jnp.float32), flip,
        preferred_element_type=jnp.float32, precision=lax.Precision.HIGHEST,
    )


def lane_groups():
    return lax.broadcasted_iota(jnp.int32, (1, LANES), 1) // GSIZE


def half_index(partner):
    core = lax.axis_index("ctx") % 2
    return 1 - core if partner else core


def each_tile(tile, width):
    count = width // LANES
    step = math.gcd(count, STEP)

    def body(i, carry):
        for j in range(step):
            tile(i * step + j)
        return carry

    lax.fori_loop(0, count // step, body, 0)


def filter_kernel(
    q_ref, k_ref, v_ref, dy_ref, kv_prev_ref, starts_ref, out_ref, own_ref, prev_ref, sums_ref, *, scale, partner
):
    rows = q_ref.shape[0]
    per_tile = LANES // GSIZE

    own_ref[...], prev_ref[...], _ = contig_masks(starts_ref)

    group = lane_groups()
    width = q_ref.shape[1] // 2
    base = half_index(partner) * width

    def tile(index):
        here = pl.ds(pl.multiple_of(index * LANES, LANES), LANES)
        lanes = pl.ds(pl.multiple_of(base + index * LANES, LANES), LANES)
        cot = product(dy_ref[:, lanes], q_ref[:, lanes])
        kv = jnp.concatenate([product(k_ref[:, lanes], v_ref[:, lanes]), kv_prev_ref[:, here]], axis=0)
        for g in range(per_tile):
            picked = jnp.where(group == g, cot, jnp.zeros_like(cot))
            pairs = lax.dot_general(
                picked, kv, (((1,), (1,)), ((), ())), preferred_element_type=jnp.float32
            )
            linked = pairs[:, :rows] * own_ref[...] + pairs[:, rows:] * prev_ref[...]
            total = linked[:8]
            for i in range(1, rows // 8):
                total = total + pltpu.roll(linked[8 * i : 8 * i + 8], rows - 8 * i, 1)
            at = pl.multiple_of((index * per_tile + g) * 8, 8)
            sums_ref[pl.ds(at, 8), :] = total

    each_tile(tile, width)
    groups = out_ref.shape[0]
    diagonal = sums_ref[pl.ds(0, groups, stride=8), :]
    for r in range(1, 8):
        diagonal = diagonal + pltpu.roll(sums_ref[pl.ds(r, groups, stride=8), :], rows - r, 1)
    out_ref[...] = reversed_taps(diagonal) * scale


def conv_kernel(
    a_ref, b_ref, other_ref, c_ref, d_ref, starts_ref, taps_ref, c_in_hbm, d_in_hbm, out_c_hbm, out_d_hbm,
    mask_ref, taps_scr, out_c_ref, out_d_ref, sems, *, backward, partner,
):
    del c_in_hbm, d_in_hbm
    rows = a_ref.shape[0]
    per_tile = LANES // GSIZE
    width = a_ref.shape[1] // 2
    half = half_index(partner)
    base = half * width
    own, previous, following = contig_masks(starts_ref)
    mask_ref[:, :rows] = (own.T if backward else own).astype(jnp.bfloat16)
    mask_ref[:, rows:] = (following if backward else previous).astype(jnp.bfloat16)
    groups = width // GSIZE
    taps = taps_ref[pl.ds(pl.multiple_of(half * groups, groups), groups), :]
    taps_scr[...] = taps.astype(jnp.float32) if backward else reversed_taps(taps)
    group = lane_groups()

    def table(row):
        wide = pltpu.roll(jnp.broadcast_to(row, (rows, rows)), 0, 1, stride=1, stride_axis=0)
        wide = wide.astype(jnp.bfloat16)
        return jnp.concatenate([wide, wide], axis=1) * mask_ref[...]

    def tile(index):
        here = pl.ds(pl.multiple_of(index * LANES, LANES), LANES)
        lanes = pl.ds(pl.multiple_of(base + index * LANES, LANES), LANES)
        other = other_ref[:, here if other_ref.shape[1] == width else lanes]
        x = jnp.concatenate([product(a_ref[:, lanes], b_ref[:, lanes]), other], axis=0)
        taps = taps_scr[pl.ds(pl.multiple_of(index * per_tile, per_tile), per_tile), :]
        y = jnp.zeros((rows, LANES), jnp.float32)
        for g in range(per_tile):
            y = jnp.where(group == g, jnp.dot(table(taps[g : g + 1]), x, preferred_element_type=jnp.float32), y)
        out_c_ref[:, here] = (c_ref[:, lanes].astype(jnp.float32) * y).astype(jnp.bfloat16)
        out_d_ref[:, here] = (d_ref[:, lanes].astype(jnp.float32) * y).astype(jnp.bfloat16)

    step = math.gcd(width // LANES, STEP) * LANES

    def stored(i):
        here = pl.ds(pl.multiple_of(i * step, step), step)
        there = pl.ds(pl.multiple_of(base + i * step, step), step)
        return [
            pltpu.make_async_copy(out_c_ref.at[:, here], out_c_hbm.at[:, there], sems.at[0, i]),
            pltpu.make_async_copy(out_d_ref.at[:, here], out_d_hbm.at[:, there], sems.at[1, i]),
        ]

    def body(i, carry):
        for j in range(step // LANES):
            tile(i * (step // LANES) + j)
        for copy in stored(i):
            copy.start()
        return carry

    lax.fori_loop(0, width // step, body, 0)
    for i in range(width // step):
        for copy in stored(i):
            copy.wait()


VMEM = pl.BlockSpec(memory_space=pltpu.VMEM)


def local_call(kernel, name, out_shape, scratch_shapes, flops, operands, in_specs=None, out_specs=VMEM, aliases={}):
    outs = out_shape if isinstance(out_shape, list) else [out_shape]
    moved = sum(math.prod(x.shape) * x.dtype.itemsize for x in [*operands, *outs])
    return pl.pallas_call(
        kernel,
        out_shape=out_shape,
        in_specs=in_specs or [VMEM] * len(operands),
        out_specs=out_specs,
        scratch_shapes=scratch_shapes,
        input_output_aliases=aliases,
        cost_estimate=pl.CostEstimate(flops=flops, bytes_accessed=moved, transcendentals=0),
        compiler_params=pltpu.CompilerParams(vmem_limit_bytes=24 << 20),
        name=name,
    )(*operands)


def filter_share(q, k, v, dy, kv_prev, starts, groups, scale, partner):
    rows, width = q.shape
    table = pltpu.VMEM((rows, rows), jnp.float32)
    return local_call(
        functools.partial(filter_kernel, scale=scale, partner=partner),
        "filter_partner" if partner else "filter_own",
        jax.ShapeDtypeStruct((groups // 2, rows), jnp.float32),
        [table, table, pltpu.VMEM((groups * 4, rows), jnp.float32)],
        16 * rows * rows * width, (q, k, v, dy, kv_prev, starts),
    )


def convolution(a, b, other, c, d, starts, filters, outs, backward, partner):
    rows, width = a.shape
    steps = width // 2 // LANES // math.gcd(width // 2 // LANES, STEP)
    out = jax.ShapeDtypeStruct((rows, width), jnp.bfloat16)
    half = pltpu.VMEM((rows, width // 2), jnp.bfloat16)
    anywhere = pl.BlockSpec(memory_space=pl.ANY)
    kernel = functools.partial(conv_kernel, backward=backward, partner=partner)
    operands = (a, b, other, c, d, starts, filters)
    if outs is None:
        body = kernel
        kernel = lambda *refs: body(*refs[:7], None, None, *refs[7:])
    return local_call(
        kernel,
        ("backward" if backward else "forward") + ("_partner" if partner else "_own"),
        [out, out],
        [
            pltpu.VMEM((rows, 2 * rows), jnp.bfloat16), pltpu.VMEM((filters.shape[0] // 2, rows), jnp.float32),
            half, half, pltpu.SemaphoreType.DMA((2, steps)),
        ],
        16 * rows * rows * width,
        operands + tuple(outs or ()),
        [VMEM] * 7 + [anywhere] * (2 if outs else 0),
        [anywhere] * 2,
        {7: 0, 8: 1} if outs else {},
    )


def passed_along(block, axis, distance):
    devices = range(lax.axis_size(axis))
    route = [(i - distance, i) for i in devices if i - distance in devices]
    return lax.ppermute(block, axis, route)


def factors(size):
    found, p = [], 2
    while size > 1:
        while size % p == 0:
            found.append(p)
            size //= p
        p += 1
    return found


def other_core(block):
    size = lax.axis_size("ctx")
    return lax.ppermute(block, "ctx", [(i, i ^ 1) for i in range(size)])


def rounds_over_chips():
    return [
        (axis, first * math.prod(factors(lax.axis_size(axis) // first)[:n]), p)
        for axis, first in (("ctx", 2), ("dp", 1))
        for n, p in enumerate(factors(lax.axis_size(axis) // first))
    ]


def summed_over(total, axis, stride, p):
    size = lax.axis_size(axis)
    turned = lambda i, k: i + ((i // stride + k) % p - i // stride % p) * stride
    got = [lax.ppermute(total, axis, [(turned(i, k), i) for i in range(size)]) for k in range(1, p)]
    if p == 2:
        return total + got[0]
    digit = lax.axis_index(axis) // stride % p
    return jnp.sum(jnp.roll(jnp.stack([total, *got]), digit, axis=0), axis=0)


def after(value, *others):
    return lax.optimization_barrier((value, *others))[0]


def per_device(q_proj, k_proj, v_proj, out_grad, contig_starts, filters):
    q, k, v, dy = q_proj[0], k_proj[0], v_proj[0], out_grad[0]
    rows = q.shape[0]
    groups, taps = filters.shape
    assert rows == taps == LANES and lax.axis_size("ctx") % 2 == 0
    scale = 1.0 / math.sqrt(rows * lax.axis_size("ctx") * lax.axis_size("dp") * GSIZE)
    starts = contig_starts[0] > 0
    token = jnp.arange(rows)
    tail = ~jnp.any(starts[None, :] & (token[None, :] > token[:, None]), axis=1)
    head = ~jnp.any(starts[None, :] & (token[None, :] <= token[:, None]), axis=1)
    core = lax.axis_index("ctx") % 2
    width = q.shape[1] // 2

    def sent(a, b, keep, half):
        part = lambda x: lax.dynamic_slice_in_dim(x, half * width, width, 1)
        return jnp.where(keep[:, None], product(part(a), part(b)), 0)

    kv_out = sent(k, v, tail, core)
    kv_theirs = passed_along(kv_out, "ctx", 1)
    kv_mine = passed_along(sent(after(k, kv_out), v, tail, 1 - core), "ctx", 1)
    theirs = filter_share(q, k, v, dy, kv_theirs, contig_starts, groups, scale, True)
    mine = filter_share(q, k, v, dy, after(kv_mine, theirs), contig_starts, groups, scale, False)
    mine = mine + other_core(theirs)

    def forward(other, outs, partner):
        return convolution(k, v, other, q, dy, contig_starts, filters, outs, False, partner)

    def backward(other, outs, partner):
        return convolution(dy, q, other, v, k, contig_starts, filters, outs, True, partner)

    cot_out = [sent(dy, q, head, core), sent(dy, q, head, 1 - core)]
    rounds = rounds_over_chips()
    for n, place in enumerate(rounds):
        if n == 0:
            cot_theirs = passed_along(after(cot_out[0], mine), "ctx", -1)
            half_forward = forward(kv_theirs, None, True)
        if n == 1:
            mine = after(mine, *half_forward)
            cot_mine = passed_along(after(cot_out[1], mine), "ctx", -1)
            mixed, grad_q = forward(kv_mine, half_forward, False)
        if n == 2:
            mine = after(mine, mixed, grad_q, cot_theirs)
            half_backward = backward(cot_theirs, None, True)
        if n == 3:
            mine = after(mine, *half_backward, cot_mine)
            grad_k, grad_v = backward(cot_mine, half_backward, False)
        mine = summed_over(mine, *place)
    mine = after(mine, grad_k, grad_v)
    halves = [mine, other_core(mine)]
    filter_grad = jnp.where(core == 0, jnp.concatenate(halves), jnp.concatenate(halves[::-1]))
    return (mixed[None], grad_q[None], grad_k[None], grad_v[None], filter_grad)


def solution(mesh):
    wide = P("dp", "ctx", None)
    return jax.shard_map(
        per_device,
        mesh=mesh,
        in_specs=(wide,) * 4 + (P("dp", "ctx"), P()),
        out_specs=(wide,) * 4 + (P(),),
        check_vma=False,
    )
```

```python
import functools
import math

import jax
import jax.numpy as jnp
from jax import lax
from jax.experimental import pallas as pl
from jax.experimental.pallas import tpu as pltpu
from jax.sharding import PartitionSpec as P

GSIZE = 16
LANES = 128
STEP = 4


def product(a, b):
    return (a.astype(jnp.float32) * b.astype(jnp.float32)).astype(jnp.bfloat16)


def contig_masks(starts_ref):
    rows = starts_ref.shape[1]
    starts = jnp.broadcast_to(starts_ref[...], (rows, rows)) > 0
    t = lax.broadcasted_iota(jnp.int32, (rows, rows), 0)
    s = lax.broadcasted_iota(jnp.int32, (rows, rows), 1)
    began = jnp.max(jnp.where(starts & (s <= t), s, 0), axis=1, keepdims=True)
    own = (s <= t) & (s >= began)
    first = jnp.min(jnp.where(starts, s, rows), axis=1, keepdims=True)
    previous = (s > t) & (t < first)
    last = jnp.max(jnp.where(starts, s, 0), axis=1, keepdims=True)
    following = (s < t) & (t >= last)
    as_f32 = lambda mask: jnp.where(mask, 1.0, 0.0).astype(jnp.float32)
    return as_f32(own), as_f32(previous), as_f32(following)


def reversed_taps(rows_of_taps):
    taps = rows_of_taps.shape[1]
    i = lax.broadcasted_iota(jnp.int32, (taps, taps), 0)
    j = lax.broadcasted_iota(jnp.int32, (taps, taps), 1)
    flip = jnp.where((i + j == 0) | (i + j == taps), 1.0, 0.0).astype(jnp.float32)
    return jnp.dot(
        rows_of_taps.astype(jnp.float32), flip,
        preferred_element_type=jnp.float32, precision=lax.Precision.HIGHEST,
    )


def lane_groups():
    return lax.broadcasted_iota(jnp.int32, (1, LANES), 1) // GSIZE


def each_tile(tile, width):
    count = width // LANES
    step = math.gcd(count, STEP)

    def body(i, carry):
        for j in range(step):
            tile(i * step + j)
        return carry

    lax.fori_loop(0, count // step, body, 0)


def filter_kernel(
    q_ref, k_ref, v_ref, dy_ref, other_ref, starts_ref, out_ref, own_ref, other_mask_ref, sums_ref, *, scale, partner
):
    rows = q_ref.shape[0]
    per_tile = LANES // GSIZE
    width = q_ref.shape[1] // 2
    core = lax.axis_index("ctx") % 2
    half = 1 - core if partner else core
    low = half == 0
    base = half * width
    own, previous, following = contig_masks(starts_ref)
    own_ref[...] = jnp.where(low, own, own.T)
    other_mask_ref[...] = jnp.where(low, previous, following)
    group = lane_groups()

    def tile(index):
        here = pl.ds(pl.multiple_of(index * LANES, LANES), LANES)
        lanes = pl.ds(pl.multiple_of(base + index * LANES, LANES), LANES)
        cot = product(dy_ref[:, lanes], q_ref[:, lanes])
        kv = product(k_ref[:, lanes], v_ref[:, lanes])
        left = jnp.where(low, cot, kv)
        right = jnp.concatenate(
            [jnp.where(low, kv, cot), other_ref[:, here if other_ref.shape[1] == width else lanes]], axis=0
        )
        for g in range(per_tile):
            picked = jnp.where(group == g, left, jnp.zeros_like(left))
            pairs = lax.dot_general(
                picked, right, (((1,), (1,)), ((), ())), preferred_element_type=jnp.float32
            )
            linked = pairs[:, :rows] * own_ref[...] + pairs[:, rows:] * other_mask_ref[...]
            total = linked[:8]
            for i in range(1, rows // 8):
                total = total + pltpu.roll(linked[8 * i : 8 * i + 8], rows - 8 * i, 1)
            at = pl.multiple_of((index * per_tile + g) * 8, 8)
            sums_ref[pl.ds(at, 8), :] = total

    each_tile(tile, width)
    groups = out_ref.shape[0]
    diagonal = sums_ref[pl.ds(0, groups, stride=8), :]
    for r in range(1, 8):
        diagonal = diagonal + pltpu.roll(sums_ref[pl.ds(r, groups, stride=8), :], rows - r, 1)
    out_ref[...] = jnp.where(low, reversed_taps(diagonal), diagonal) * scale


def conv_kernel(
    a_ref, b_ref, pair_ref, far_ref, c_ref, d_ref, starts_ref, taps_ref, c_in_hbm, d_in_hbm, out_c_hbm, out_d_hbm,
    mask_ref, taps_scr, out_c_ref, out_d_ref, sems, *, backward, half,
):
    del c_in_hbm, d_in_hbm
    rows = a_ref.shape[0]
    per_tile = LANES // GSIZE
    width = a_ref.shape[1] // 2
    base = half * width
    even = lax.axis_index("ctx") % 2 == 0
    own, previous, following = contig_masks(starts_ref)
    mask_ref[:, :rows] = (own.T if backward else own).astype(jnp.bfloat16)
    mask_ref[:, rows:] = (following if backward else previous).astype(jnp.bfloat16)
    groups = width // GSIZE
    taps = taps_ref[half * groups : (half + 1) * groups, :]
    taps_scr[...] = taps.astype(jnp.float32) if backward else reversed_taps(taps)
    group = lane_groups()

    def table(row):
        wide = pltpu.roll(jnp.broadcast_to(row, (rows, rows)), 0, 1, stride=1, stride_axis=0)
        wide = wide.astype(jnp.bfloat16)
        return jnp.concatenate([wide, wide], axis=1) * mask_ref[...]

    def tile(index):
        here = pl.ds(pl.multiple_of(index * LANES, LANES), LANES)
        lanes = pl.ds(pl.multiple_of(base + index * LANES, LANES), LANES)
        from_pair = even if backward else jnp.logical_not(even)
        other = jnp.where(from_pair, pair_ref[:, lanes], far_ref[:, here])
        x = jnp.concatenate([product(a_ref[:, lanes], b_ref[:, lanes]), other], axis=0)
        taps = taps_scr[pl.ds(pl.multiple_of(index * per_tile, per_tile), per_tile), :]
        y = jnp.zeros((rows, LANES), jnp.float32)
        for g in range(per_tile):
            y = jnp.where(group == g, jnp.dot(table(taps[g : g + 1]), x, preferred_element_type=jnp.float32), y)
        out_c_ref[:, here] = (c_ref[:, lanes].astype(jnp.float32) * y).astype(jnp.bfloat16)
        out_d_ref[:, here] = (d_ref[:, lanes].astype(jnp.float32) * y).astype(jnp.bfloat16)

    step = math.gcd(width // LANES, STEP) * LANES

    def stored(i):
        here = pl.ds(pl.multiple_of(i * step, step), step)
        there = pl.ds(pl.multiple_of(base + i * step, step), step)
        return [
            pltpu.make_async_copy(out_c_ref.at[:, here], out_c_hbm.at[:, there], sems.at[0, i]),
            pltpu.make_async_copy(out_d_ref.at[:, here], out_d_hbm.at[:, there], sems.at[1, i]),
        ]

    def body(i, carry):
        for j in range(step // LANES):
            tile(i * (step // LANES) + j)
        for copy in stored(i):
            copy.start()
        return carry

    lax.fori_loop(0, width // step, body, 0)
    for i in range(width // step):
        for copy in stored(i):
            copy.wait()


VMEM = pl.BlockSpec(memory_space=pltpu.VMEM)


def local_call(kernel, name, out_shape, scratch_shapes, flops, operands, in_specs=None, out_specs=VMEM, aliases={}, moved=None):
    outs = out_shape if isinstance(out_shape, list) else [out_shape]
    if moved is None:
        moved = sum(math.prod(x.shape) * x.dtype.itemsize for x in [*operands, *outs])
    return pl.pallas_call(
        kernel,
        out_shape=out_shape,
        in_specs=in_specs or [VMEM] * len(operands),
        out_specs=out_specs,
        scratch_shapes=scratch_shapes,
        input_output_aliases=aliases,
        cost_estimate=pl.CostEstimate(flops=flops, bytes_accessed=moved, transcendentals=0),
        compiler_params=pltpu.CompilerParams(vmem_limit_bytes=24 << 20),
        name=name,
    )(*operands)


def filter_share(q, k, v, dy, other, starts, groups, scale, partner):
    rows, width = q.shape
    table = pltpu.VMEM((rows, rows), jnp.float32)
    return local_call(
        functools.partial(filter_kernel, scale=scale, partner=partner),
        "filter_partner" if partner else "filter_own",
        jax.ShapeDtypeStruct((groups // 2, rows), jnp.float32),
        [table, table, pltpu.VMEM((groups * 4, rows), jnp.float32)],
        0, (q, k, v, dy, other, starts), moved=0,
    )


def convolution(a, b, pair, far, c, d, starts, filters, outs, backward, half):
    rows, width = a.shape
    steps = width // 2 // LANES // math.gcd(width // 2 // LANES, STEP)
    out = jax.ShapeDtypeStruct((rows, width), jnp.bfloat16)
    part = pltpu.VMEM((rows, width // 2), jnp.bfloat16)
    anywhere = pl.BlockSpec(memory_space=pl.ANY)
    body = functools.partial(conv_kernel, backward=backward, half=half)
    operands = (a, b, pair, far, c, d, starts, filters)
    n = len(operands)
    return local_call(
        body if outs else lambda *refs: body(*refs[:n], None, None, *refs[n:]),
        ("backward" if backward else "forward") + ("_high" if half else "_low"),
        [out, out],
        [
            pltpu.VMEM((rows, 2 * rows), jnp.bfloat16), pltpu.VMEM((filters.shape[0] // 2, rows), jnp.float32),
            part, part, pltpu.SemaphoreType.DMA((2, steps)),
        ],
        16 * rows * rows * width,
        operands + tuple(outs or ()),
        [VMEM] * n + [anywhere] * (2 if outs else 0),
        [anywhere] * 2,
        {n: 0, n + 1: 1} if outs else {},
    )


def other_core(block):
    return lax.ppermute(block, "ctx", [(i, i ^ 1) for i in range(lax.axis_size("ctx"))])


def next_chip(block):
    size = lax.axis_size("ctx")
    pairs = [(i, i + 1) for i in range(1, size - 1, 2)]
    return lax.ppermute(block, "ctx", pairs + [(j, i) for i, j in pairs])


def factors(size):
    found, p = [], 2
    while size > 1:
        while size % p == 0:
            found.append(p)
            size //= p
        p += 1
    return found


def rounds_over_chips():
    return [
        (axis, first * math.prod(factors(lax.axis_size(axis) // first)[:n]), p)
        for axis, first in (("ctx", 2), ("dp", 1))
        for n, p in enumerate(factors(lax.axis_size(axis) // first))
    ]


def summed_over(total, axis, stride, p):
    size = lax.axis_size(axis)
    turned = lambda i, k: i + ((i // stride + k) % p - i // stride % p) * stride
    got = [lax.ppermute(total, axis, [(turned(i, k), i) for i in range(size)]) for k in range(1, p)]
    if p == 2:
        return total + got[0]
    digit = lax.axis_index(axis) // stride % p
    return jnp.sum(jnp.roll(jnp.stack([total, *got]), digit, axis=0), axis=0)


def after(value, *others):
    return lax.optimization_barrier((value, *others))[0]


def per_device(q_proj, k_proj, v_proj, out_grad, contig_starts, filters):
    q, k, v, dy = q_proj[0], k_proj[0], v_proj[0], out_grad[0]
    rows = q.shape[0]
    groups, taps = filters.shape
    assert rows == taps == LANES and lax.axis_size("ctx") % 2 == 0
    scale = 1.0 / math.sqrt(rows * lax.axis_size("ctx") * lax.axis_size("dp") * GSIZE)
    flags = lax.optimization_barrier(jnp.minimum(contig_starts, 1))
    starts = flags[0] > 0
    token = jnp.arange(rows)
    tail = ~jnp.any(starts[None, :] & (token[None, :] > token[:, None]), axis=1)
    head = ~jnp.any(starts[None, :] & (token[None, :] <= token[:, None]), axis=1)
    even = lax.axis_index("ctx") % 2 == 0
    width = q.shape[1] // 2
    low, high, every = slice(0, width), slice(width, None), slice(None)

    def sent(from_even, kv_part, cot_part, earlier=()):
        to_next = even if from_even else ~even
        q_, k_, v_, dy_ = lax.optimization_barrier((q, k, v, dy, *earlier))[:4]
        kv = product(k_[:, kv_part], v_[:, kv_part])
        cot = product(dy_[:, cot_part], q_[:, cot_part])
        keep = jnp.where(to_next, tail, head)
        return jnp.where(keep[:, None], jnp.where(to_next, kv, cot), 0)

    far_out = sent(False, low, high)
    far_first = next_chip(far_out)
    pair_out = sent(True, every, every, (far_out,))
    pair = other_core(pair_out)
    theirs = filter_share(q, k, v, dy, pair, flags, groups, scale, True)
    mine = filter_share(q, k, v, dy, after(far_first, theirs), flags, groups, scale, False)
    mine = mine + other_core(theirs)

    def forward(far, outs, half):
        return convolution(k, v, pair, far, q, dy, flags, filters, outs, False, half)

    def backward(far, outs, half):
        return convolution(dy, q, pair, far, v, k, flags, filters, outs, True, half)

    far_out = sent(False, high, low, (pair_out,))
    for n, place in enumerate(rounds_over_chips()):
        if n == 0:
            far_second = next_chip(after(far_out, mine))
            half_forward = forward(far_first, None, 0)
        if n == 1:
            mine = after(mine, *half_forward)
            half_backward = backward(far_first, None, 1)
        if n == 2:
            mine = after(mine, *half_backward, far_second)
            mixed, grad_q = forward(far_second, half_forward, 1)
        if n == 3:
            mine = after(mine, mixed, grad_q)
            grad_k, grad_v = backward(far_second, half_backward, 0)
        mine = summed_over(mine, *place)
    mine = after(mine, grad_k, grad_v)
    halves = [mine, other_core(mine)]
    filter_grad = jnp.where(even, jnp.concatenate(halves), jnp.concatenate(halves[::-1]))
    return (mixed[None], grad_q[None], grad_k[None], grad_v[None], filter_grad)


def solution(mesh):
    wide = P("dp", "ctx", None)
    return jax.shard_map(
        per_device,
        mesh=mesh,
        in_specs=(wide,) * 4 + (P("dp", "ctx"), P()),
        out_specs=(wide,) * 4 + (P(),),
        check_vma=False,
    )
```

```python
import functools
import math

import jax
import jax.numpy as jnp
from jax import lax
from jax.experimental import pallas as pl
from jax.experimental.pallas import tpu as pltpu
from jax.sharding import PartitionSpec as P

GSIZE = 16
LANES = 128
STEP = 4


def product(a, b):
    return (a.astype(jnp.float32) * b.astype(jnp.float32)).astype(jnp.bfloat16)


def contig_masks(starts_ref):
    rows = starts_ref.shape[1]
    starts = jnp.broadcast_to(starts_ref[...], (rows, rows)) > 0
    t = lax.broadcasted_iota(jnp.int32, (rows, rows), 0)
    s = lax.broadcasted_iota(jnp.int32, (rows, rows), 1)
    began = jnp.max(jnp.where(starts & (s <= t), s, 0), axis=1, keepdims=True)
    own = (s <= t) & (s >= began)
    first = jnp.min(jnp.where(starts, s, rows), axis=1, keepdims=True)
    previous = (s > t) & (t < first)
    last = jnp.max(jnp.where(starts, s, 0), axis=1, keepdims=True)
    following = (s < t) & (t >= last)
    as_f32 = lambda mask: jnp.where(mask, 1.0, 0.0).astype(jnp.float32)
    return as_f32(own), as_f32(previous), as_f32(following)


def reversed_taps(rows_of_taps):
    taps = rows_of_taps.shape[1]
    i = lax.broadcasted_iota(jnp.int32, (taps, taps), 0)
    j = lax.broadcasted_iota(jnp.int32, (taps, taps), 1)
    flip = jnp.where((i + j == 0) | (i + j == taps), 1.0, 0.0).astype(jnp.float32)
    return jnp.dot(
        rows_of_taps.astype(jnp.float32), flip,
        preferred_element_type=jnp.float32, precision=lax.Precision.HIGHEST,
    )


def lane_groups():
    return lax.broadcasted_iota(jnp.int32, (1, LANES), 1) // GSIZE


def each_tile(tile, width):
    count = width // LANES
    step = math.gcd(count, STEP)

    def body(i, carry):
        for j in range(step):
            tile(i * step + j)
        return carry

    lax.fori_loop(0, count // step, body, 0)


def filter_kernel(
    q_ref, k_ref, v_ref, dy_ref, other_ref, starts_ref, out_ref, own_ref, other_mask_ref, sums_ref, *, scale, partner
):
    rows = q_ref.shape[0]
    per_tile = LANES // GSIZE
    width = q_ref.shape[1] // 2
    core = lax.axis_index("ctx") % 2
    half = 1 - core if partner else core
    low = half == 0
    base = half * width
    own, previous, following = contig_masks(starts_ref)
    own_ref[...] = jnp.where(low, own, own.T)
    other_mask_ref[...] = jnp.where(low, previous, following)
    group = lane_groups()

    def tile(index):
        here = pl.ds(pl.multiple_of(index * LANES, LANES), LANES)
        lanes = pl.ds(pl.multiple_of(base + index * LANES, LANES), LANES)
        cot = product(dy_ref[:, lanes], q_ref[:, lanes])
        kv = product(k_ref[:, lanes], v_ref[:, lanes])
        left = jnp.where(low, cot, kv)
        right = jnp.concatenate(
            [jnp.where(low, kv, cot), other_ref[:, here]], axis=0
        )
        for g in range(per_tile):
            picked = jnp.where(group == g, left, jnp.zeros_like(left))
            pairs = lax.dot_general(
                picked, right, (((1,), (1,)), ((), ())), preferred_element_type=jnp.float32
            )
            linked = pairs[:, :rows] * own_ref[...] + pairs[:, rows:] * other_mask_ref[...]
            total = linked[:8]
            for i in range(1, rows // 8):
                total = total + pltpu.roll(linked[8 * i : 8 * i + 8], rows - 8 * i, 1)
            at = pl.multiple_of((index * per_tile + g) * 8, 8)
            sums_ref[pl.ds(at, 8), :] = total

    each_tile(tile, width)
    groups = out_ref.shape[0]
    diagonal = sums_ref[pl.ds(0, groups, stride=8), :]
    for r in range(1, 8):
        diagonal = diagonal + pltpu.roll(sums_ref[pl.ds(r, groups, stride=8), :], rows - r, 1)
    out_ref[...] = jnp.where(low, reversed_taps(diagonal), diagonal) * scale


def conv_kernel(
    a_ref, b_ref, pair_ref, far_ref, c_ref, d_ref, starts_ref, taps_ref, c_in_hbm, d_in_hbm, out_c_hbm, out_d_hbm,
    mask_ref, taps_scr, out_c_ref, out_d_ref, sems, *, backward, half,
):
    del c_in_hbm, d_in_hbm
    rows = a_ref.shape[0]
    per_tile = LANES // GSIZE
    width = a_ref.shape[1] // 2
    base = half * width
    even = lax.axis_index("ctx") % 2 == 0
    own, previous, following = contig_masks(starts_ref)
    mask_ref[:, :rows] = (own.T if backward else own).astype(jnp.bfloat16)
    mask_ref[:, rows:] = (following if backward else previous).astype(jnp.bfloat16)
    groups = width // GSIZE
    taps = taps_ref[half * groups : (half + 1) * groups, :]
    taps_scr[...] = taps.astype(jnp.float32) if backward else reversed_taps(taps)
    group = lane_groups()

    def table(row):
        wide = pltpu.roll(jnp.broadcast_to(row, (rows, rows)), 0, 1, stride=1, stride_axis=0)
        wide = wide.astype(jnp.bfloat16)
        return jnp.concatenate([wide, wide], axis=1) * mask_ref[...]

    def tile(index):
        here = pl.ds(pl.multiple_of(index * LANES, LANES), LANES)
        lanes = pl.ds(pl.multiple_of(base + index * LANES, LANES), LANES)
        from_pair = even if backward else jnp.logical_not(even)
        other = jnp.where(from_pair, pair_ref[:, here], far_ref[:, here])
        x = jnp.concatenate([product(a_ref[:, lanes], b_ref[:, lanes]), other], axis=0)
        taps = taps_scr[pl.ds(pl.multiple_of(index * per_tile, per_tile), per_tile), :]
        y = jnp.zeros((rows, LANES), jnp.float32)
        for g in range(per_tile):
            y = jnp.where(group == g, jnp.dot(table(taps[g : g + 1]), x, preferred_element_type=jnp.float32), y)
        out_c_ref[:, here] = (c_ref[:, lanes].astype(jnp.float32) * y).astype(jnp.bfloat16)
        out_d_ref[:, here] = (d_ref[:, lanes].astype(jnp.float32) * y).astype(jnp.bfloat16)

    step = math.gcd(width // LANES, STEP) * LANES

    def stored(i):
        here = pl.ds(pl.multiple_of(i * step, step), step)
        there = pl.ds(pl.multiple_of(base + i * step, step), step)
        return [
            pltpu.make_async_copy(out_c_ref.at[:, here], out_c_hbm.at[:, there], sems.at[0, i]),
            pltpu.make_async_copy(out_d_ref.at[:, here], out_d_hbm.at[:, there], sems.at[1, i]),
        ]

    def body(i, carry):
        for j in range(step // LANES):
            tile(i * (step // LANES) + j)
        for copy in stored(i):
            copy.start()
        return carry

    lax.fori_loop(0, width // step, body, 0)
    for i in range(width // step):
        for copy in stored(i):
            copy.wait()


VMEM = pl.BlockSpec(memory_space=pltpu.VMEM)


def local_call(kernel, name, out_shape, scratch_shapes, flops, operands, in_specs=None, out_specs=VMEM, aliases={}, moved=None):
    outs = out_shape if isinstance(out_shape, list) else [out_shape]
    if moved is None:
        moved = sum(math.prod(x.shape) * x.dtype.itemsize for x in [*operands, *outs])
    return pl.pallas_call(
        kernel,
        out_shape=out_shape,
        in_specs=in_specs or [VMEM] * len(operands),
        out_specs=out_specs,
        scratch_shapes=scratch_shapes,
        input_output_aliases=aliases,
        cost_estimate=pl.CostEstimate(flops=flops, bytes_accessed=moved, transcendentals=0),
        compiler_params=pltpu.CompilerParams(vmem_limit_bytes=24 << 20),
        name=name,
    )(*operands)


def filter_share(q, k, v, dy, other, starts, groups, scale, partner):
    rows, width = q.shape
    table = pltpu.VMEM((rows, rows), jnp.float32)
    return local_call(
        functools.partial(filter_kernel, scale=scale, partner=partner),
        "filter_partner" if partner else "filter_own",
        jax.ShapeDtypeStruct((groups // 2, rows), jnp.float32),
        [table, table, pltpu.VMEM((groups * 4, rows), jnp.float32)],
        1000, (q, k, v, dy, other, starts), moved=1000,
    )


def convolution(a, b, pair, far, c, d, starts, filters, outs, backward, half):
    rows, width = a.shape
    steps = width // 2 // LANES // math.gcd(width // 2 // LANES, STEP)
    out = jax.ShapeDtypeStruct((rows, width), jnp.bfloat16)
    part = pltpu.VMEM((rows, width // 2), jnp.bfloat16)
    anywhere = pl.BlockSpec(memory_space=pl.ANY)
    body = functools.partial(conv_kernel, backward=backward, half=half)
    operands = (a, b, pair, far, c, d, starts, filters)
    n = len(operands)
    return local_call(
        body if outs else lambda *refs: body(*refs[:n], None, None, *refs[n:]),
        ("backward" if backward else "forward") + ("_high" if half else "_low"),
        [out, out],
        [
            pltpu.VMEM((rows, 2 * rows), jnp.bfloat16), pltpu.VMEM((filters.shape[0] // 2, rows), jnp.float32),
            part, part, pltpu.SemaphoreType.DMA((2, steps)),
        ],
        16 * rows * rows * width,
        operands + tuple(outs or ()),
        [VMEM] * n + [anywhere] * (2 if outs else 0),
        [anywhere] * 2,
        {n: 0, n + 1: 1} if outs else {},
    )


def other_core(block):
    return lax.ppermute(block, "ctx", [(i, i ^ 1) for i in range(lax.axis_size("ctx"))])


def next_chip(block):
    size = lax.axis_size("ctx")
    pairs = [(i, i + 1) for i in range(1, size - 1, 2)]
    return lax.ppermute(block, "ctx", pairs + [(j, i) for i, j in pairs])


def factors(size):
    found, p = [], 2
    while size > 1:
        while size % p == 0:
            found.append(p)
            size //= p
        p += 1
    return found


def rounds_over_chips():
    return [
        (axis, first * math.prod(factors(lax.axis_size(axis) // first)[:n]), p)
        for axis, first in (("dp", 1), ("ctx", 2))
        for n, p in enumerate(factors(lax.axis_size(axis) // first))
    ]


def summed_over(total, axis, stride, p):
    size = lax.axis_size(axis)
    turned = lambda i, k: i + ((i // stride + k) % p - i // stride % p) * stride
    got = [lax.ppermute(total, axis, [(turned(i, k), i) for i in range(size)]) for k in range(1, p)]
    if p == 2:
        return total + got[0]
    digit = lax.axis_index(axis) // stride % p
    return jnp.sum(jnp.roll(jnp.stack([total, *got]), digit, axis=0), axis=0)


def after(value, *others):
    return lax.optimization_barrier((value, *others))[0]


def per_device(q_proj, k_proj, v_proj, out_grad, contig_starts, filters):
    q, k, v, dy = q_proj[0], k_proj[0], v_proj[0], out_grad[0]
    rows = q.shape[0]
    groups, taps = filters.shape
    assert rows == taps == LANES and lax.axis_size("ctx") % 2 == 0
    scale = 1.0 / math.sqrt(rows * lax.axis_size("ctx") * lax.axis_size("dp") * GSIZE)
    flags = lax.optimization_barrier(jnp.minimum(contig_starts, 1))
    starts = flags[0] > 0
    token = jnp.arange(rows)
    tail = ~jnp.any(starts[None, :] & (token[None, :] > token[:, None]), axis=1)
    head = ~jnp.any(starts[None, :] & (token[None, :] <= token[:, None]), axis=1)
    even = lax.axis_index("ctx") % 2 == 0
    width = q.shape[1] // 2
    low, high, every = slice(0, width), slice(width, None), slice(None)

    def sent(from_even, kv_part, cot_part, *earlier):
        to_next = even if from_even else ~even
        q_, k_, v_, dy_ = lax.optimization_barrier((q, k, v, dy, *earlier))[:4]
        kv = product(k_[:, kv_part], v_[:, kv_part])
        cot = product(dy_[:, cot_part], q_[:, cot_part])
        keep = jnp.where(to_next, tail, head)
        return jnp.where(keep[:, None], jnp.where(to_next, kv, cot), 0)

    far_out = sent(False, low, high)
    far = next_chip(far_out)
    pair_out = sent(True, low, high)
    pair = other_core(pair_out)
    theirs = filter_share(q, k, v, dy, pair, flags, groups, scale, True)
    mine = filter_share(q, k, v, dy, after(far, theirs), flags, groups, scale, False)
    mine = mine + other_core(theirs)
    later_out = sent(False, high, low, pair_out, far_out), sent(True, high, low, pair_out, far_out)

    def forward(pair, far, outs, half):
        return convolution(k, v, pair, far, q, dy, flags, filters, outs, False, half)

    def backward(pair, far, outs, half):
        return convolution(dy, q, pair, far, v, k, flags, filters, outs, True, half)

    for n, place in enumerate(rounds_over_chips()):
        if n == 0:
            later_far = next_chip(after(later_out[0], mine))
            later_pair = other_core(after(later_out[1], mine))
            half_forward = forward(pair, far, None, 0)
        if n == 1:
            mine = after(mine, *half_forward)
            half_backward = backward(pair, far, None, 1)
        if n == 2:
            mine = after(mine, *half_backward, later_far, later_pair)
            mixed, grad_q = forward(later_pair, later_far, half_forward, 1)
        if n == 3:
            mine = after(mine, mixed, grad_q)
            grad_k, grad_v = backward(later_pair, later_far, half_backward, 0)
        mine = summed_over(mine, *place)
    mine = after(mine, grad_k, grad_v)
    halves = [mine, other_core(mine)]
    filter_grad = jnp.where(even, jnp.concatenate(halves), jnp.concatenate(halves[::-1]))
    return (mixed[None], grad_q[None], grad_k[None], grad_v[None], filter_grad)


def solution(mesh):
    wide = P("dp", "ctx", None)
    return jax.shard_map(
        per_device,
        mesh=mesh,
        in_specs=(wide,) * 4 + (P("dp", "ctx"), P()),
        out_specs=(wide,) * 4 + (P(),),
        check_vma=False,
    )
```

```python
import functools
import math

import jax
import jax.numpy as jnp
from jax import lax
from jax.experimental import pallas as pl
from jax.experimental.pallas import tpu as pltpu
from jax.sharding import PartitionSpec as P

GSIZE = 16
LANES = 128
STEP = 4


def product(a, b):
    return (a.astype(jnp.float32) * b.astype(jnp.float32)).astype(jnp.bfloat16)


def contig_masks(starts_ref):
    rows = starts_ref.shape[1]
    starts = jnp.broadcast_to(starts_ref[...], (rows, rows)) > 0
    t = lax.broadcasted_iota(jnp.int32, (rows, rows), 0)
    s = lax.broadcasted_iota(jnp.int32, (rows, rows), 1)
    began = jnp.max(jnp.where(starts & (s <= t), s, 0), axis=1, keepdims=True)
    own = (s <= t) & (s >= began)
    first = jnp.min(jnp.where(starts, s, rows), axis=1, keepdims=True)
    previous = (s > t) & (t < first)
    last = jnp.max(jnp.where(starts, s, 0), axis=1, keepdims=True)
    following = (s < t) & (t >= last)
    as_f32 = lambda mask: jnp.where(mask, 1.0, 0.0).astype(jnp.float32)
    return as_f32(own), as_f32(previous), as_f32(following)


def reversed_taps(rows_of_taps):
    taps = rows_of_taps.shape[1]
    i = lax.broadcasted_iota(jnp.int32, (taps, taps), 0)
    j = lax.broadcasted_iota(jnp.int32, (taps, taps), 1)
    flip = jnp.where((i + j == 0) | (i + j == taps), 1.0, 0.0).astype(jnp.float32)
    return jnp.dot(
        rows_of_taps.astype(jnp.float32), flip,
        preferred_element_type=jnp.float32, precision=lax.Precision.HIGHEST,
    )


def lane_groups():
    return lax.broadcasted_iota(jnp.int32, (1, LANES), 1) // GSIZE


def each_tile(tile, width):
    count = width // LANES
    step = math.gcd(count, STEP)

    def body(i, carry):
        for j in range(step):
            tile(i * step + j)
        return carry

    lax.fori_loop(0, count // step, body, 0)


def filter_kernel(
    q_ref, k_ref, v_ref, dy_ref, other_ref, starts_ref, out_ref, own_ref, other_mask_ref, sums_ref, *, scale, partner
):
    rows = q_ref.shape[0]
    per_tile = LANES // GSIZE
    width = q_ref.shape[1] // 2
    core = lax.axis_index("ctx") % 2
    half = 1 - core if partner else core
    low = half == 0
    base = half * width
    own, previous, following = contig_masks(starts_ref)
    own_ref[...] = jnp.where(low, own, own.T)
    other_mask_ref[...] = jnp.where(low, previous, following)
    group = lane_groups()

    def tile(index):
        here = pl.ds(pl.multiple_of(index * LANES, LANES), LANES)
        lanes = pl.ds(pl.multiple_of(base + index * LANES, LANES), LANES)
        cot = product(dy_ref[:, lanes], q_ref[:, lanes])
        kv = product(k_ref[:, lanes], v_ref[:, lanes])
        left = jnp.where(low, cot, kv)
        right = jnp.concatenate(
            [jnp.where(low, kv, cot), other_ref[:, here]], axis=0
        )
        for g in range(per_tile):
            picked = jnp.where(group == g, left, jnp.zeros_like(left))
            pairs = lax.dot_general(
                picked, right, (((1,), (1,)), ((), ())), preferred_element_type=jnp.float32
            )
            linked = pairs[:, :rows] * own_ref[...] + pairs[:, rows:] * other_mask_ref[...]
            total = linked[:8]
            for i in range(1, rows // 8):
                total = total + pltpu.roll(linked[8 * i : 8 * i + 8], rows - 8 * i, 1)
            at = pl.multiple_of((index * per_tile + g) * 8, 8)
            sums_ref[pl.ds(at, 8), :] = total

    each_tile(tile, width)
    groups = out_ref.shape[0]
    diagonal = sums_ref[pl.ds(0, groups, stride=8), :]
    for r in range(1, 8):
        diagonal = diagonal + pltpu.roll(sums_ref[pl.ds(r, groups, stride=8), :], rows - r, 1)
    out_ref[...] = jnp.where(low, reversed_taps(diagonal), diagonal) * scale


def conv_kernel(
    a_ref, b_ref, pair_ref, far_ref, c_ref, d_ref, starts_ref, taps_ref, c_in_hbm, d_in_hbm, out_c_hbm, out_d_hbm,
    mask_ref, taps_scr, out_c_ref, out_d_ref, sems, *, backward, half,
):
    del c_in_hbm, d_in_hbm
    rows = a_ref.shape[0]
    per_tile = LANES // GSIZE
    width = a_ref.shape[1] // 2
    base = half * width
    even = lax.axis_index("ctx") % 2 == 0
    own, previous, following = contig_masks(starts_ref)
    mask_ref[:, :rows] = (own.T if backward else own).astype(jnp.bfloat16)
    mask_ref[:, rows:] = (following if backward else previous).astype(jnp.bfloat16)
    groups = width // GSIZE
    taps = taps_ref[half * groups : (half + 1) * groups, :]
    taps_scr[...] = taps.astype(jnp.float32) if backward else reversed_taps(taps)
    group = lane_groups()

    def table(row):
        wide = pltpu.roll(jnp.broadcast_to(row, (rows, rows)), 0, 1, stride=1, stride_axis=0)
        wide = wide.astype(jnp.bfloat16)
        return jnp.concatenate([wide, wide], axis=1) * mask_ref[...]

    def tile(index):
        here = pl.ds(pl.multiple_of(index * LANES, LANES), LANES)
        lanes = pl.ds(pl.multiple_of(base + index * LANES, LANES), LANES)
        from_pair = even if backward else jnp.logical_not(even)
        other = jnp.where(from_pair, pair_ref[:, here], far_ref[:, here])
        x = jnp.concatenate([product(a_ref[:, lanes], b_ref[:, lanes]), other], axis=0)
        taps = taps_scr[pl.ds(pl.multiple_of(index * per_tile, per_tile), per_tile), :]
        y = jnp.zeros((rows, LANES), jnp.float32)
        for g in range(per_tile):
            y = jnp.where(group == g, jnp.dot(table(taps[g : g + 1]), x, preferred_element_type=jnp.float32), y)
        out_c_ref[:, here] = (c_ref[:, lanes].astype(jnp.float32) * y).astype(jnp.bfloat16)
        out_d_ref[:, here] = (d_ref[:, lanes].astype(jnp.float32) * y).astype(jnp.bfloat16)

    step = math.gcd(width // LANES, STEP) * LANES

    def stored(i):
        here = pl.ds(pl.multiple_of(i * step, step), step)
        there = pl.ds(pl.multiple_of(base + i * step, step), step)
        return [
            pltpu.make_async_copy(out_c_ref.at[:, here], out_c_hbm.at[:, there], sems.at[0, i]),
            pltpu.make_async_copy(out_d_ref.at[:, here], out_d_hbm.at[:, there], sems.at[1, i]),
        ]

    def body(i, carry):
        for j in range(step // LANES):
            tile(i * (step // LANES) + j)
        for copy in stored(i):
            copy.start()
        return carry

    lax.fori_loop(0, width // step, body, 0)
    for i in range(width // step):
        for copy in stored(i):
            copy.wait()


VMEM = pl.BlockSpec(memory_space=pltpu.VMEM)


def local_call(kernel, name, out_shape, scratch_shapes, flops, operands, in_specs=None, out_specs=VMEM, aliases={}, moved=None):
    outs = out_shape if isinstance(out_shape, list) else [out_shape]
    if moved is None:
        moved = sum(math.prod(x.shape) * x.dtype.itemsize for x in [*operands, *outs])
    return pl.pallas_call(
        kernel,
        out_shape=out_shape,
        in_specs=in_specs or [VMEM] * len(operands),
        out_specs=out_specs,
        scratch_shapes=scratch_shapes,
        input_output_aliases=aliases,
        cost_estimate=pl.CostEstimate(flops=flops, bytes_accessed=moved, transcendentals=0),
        compiler_params=pltpu.CompilerParams(vmem_limit_bytes=24 << 20),
        name=name,
    )(*operands)


def filter_share(q, k, v, dy, other, starts, groups, scale, partner):
    rows, width = q.shape
    table = pltpu.VMEM((rows, rows), jnp.float32)
    return local_call(
        functools.partial(filter_kernel, scale=scale, partner=partner),
        "filter_partner" if partner else "filter_own",
        jax.ShapeDtypeStruct((groups // 2, rows), jnp.float32),
        [table, table, pltpu.VMEM((groups * 4, rows), jnp.float32)],
        1000, (q, k, v, dy, other, starts), moved=1000,
    )


def convolution(a, b, pair, far, c, d, starts, filters, outs, backward, half):
    rows, width = a.shape
    steps = width // 2 // LANES // math.gcd(width // 2 // LANES, STEP)
    out = jax.ShapeDtypeStruct((rows, width), jnp.bfloat16)
    part = pltpu.VMEM((rows, width // 2), jnp.bfloat16)
    anywhere = pl.BlockSpec(memory_space=pl.ANY)
    body = functools.partial(conv_kernel, backward=backward, half=half)
    operands = (a, b, pair, far, c, d, starts, filters)
    n = len(operands)
    return local_call(
        body if outs else lambda *refs: body(*refs[:n], None, None, *refs[n:]),
        ("backward" if backward else "forward") + ("_high" if half else "_low"),
        [out, out],
        [
            pltpu.VMEM((rows, 2 * rows), jnp.bfloat16), pltpu.VMEM((filters.shape[0] // 2, rows), jnp.float32),
            part, part, pltpu.SemaphoreType.DMA((2, steps)),
        ],
        16 * rows * rows * width,
        operands + tuple(outs or ()),
        [VMEM] * n + [anywhere] * (2 if outs else 0),
        [anywhere] * 2,
        {n: 0, n + 1: 1} if outs else {},
    )


def other_core(block):
    return lax.ppermute(block, "ctx", [(i, i ^ 1) for i in range(lax.axis_size("ctx"))])


def next_chip(block):
    size = lax.axis_size("ctx")
    pairs = [(i, i + 1) for i in range(1, size - 1, 2)]
    return lax.ppermute(block, "ctx", pairs + [(j, i) for i, j in pairs])


def factors(size):
    found, p = [], 2
    while size > 1:
        while size % p == 0:
            found.append(p)
            size //= p
        p += 1
    return found


def rounds_over_chips():
    return [
        (axis, first * math.prod(factors(lax.axis_size(axis) // first)[:n]), p)
        for axis, first in (("dp", 1), ("ctx", 2))
        for n, p in enumerate(factors(lax.axis_size(axis) // first))
    ]


def summed_over(total, axis, stride, p):
    size = lax.axis_size(axis)
    turned = lambda i, k: i + ((i // stride + k) % p - i // stride % p) * stride
    got = [lax.ppermute(total, axis, [(turned(i, k), i) for i in range(size)]) for k in range(1, p)]
    if p == 2:
        return total + got[0]
    digit = lax.axis_index(axis) // stride % p
    return jnp.sum(jnp.roll(jnp.stack([total, *got]), digit, axis=0), axis=0)


def after(value, *others):
    return lax.optimization_barrier((value, *others))[0]


def per_device(q_proj, k_proj, v_proj, out_grad, contig_starts, filters):
    q, k, v, dy = q_proj[0], k_proj[0], v_proj[0], out_grad[0]
    rows = q.shape[0]
    groups, taps = filters.shape
    assert rows == taps == LANES and lax.axis_size("ctx") % 2 == 0
    scale = 1.0 / math.sqrt(rows * lax.axis_size("ctx") * lax.axis_size("dp") * GSIZE)
    flags = lax.optimization_barrier(jnp.minimum(contig_starts, 1))
    starts = flags[0] > 0
    token = jnp.arange(rows)
    tail = ~jnp.any(starts[None, :] & (token[None, :] > token[:, None]), axis=1)
    head = ~jnp.any(starts[None, :] & (token[None, :] <= token[:, None]), axis=1)
    even = lax.axis_index("ctx") % 2 == 0
    width = q.shape[1] // 2
    low, high, every = slice(0, width), slice(width, None), slice(None)

    def sent(from_even, kv_part, cot_part, *earlier):
        to_next = even if from_even else ~even
        q_, k_, v_, dy_ = lax.optimization_barrier((q, k, v, dy, *earlier))[:4]
        kv = product(k_[:, kv_part], v_[:, kv_part])
        cot = product(dy_[:, cot_part], q_[:, cot_part])
        keep = jnp.where(to_next, tail, head)
        return jnp.where(keep[:, None], jnp.where(to_next, kv, cot), 0)

    far_out = sent(False, low, high)
    far = next_chip(far_out)
    pair_out = sent(True, low, high)
    pair = other_core(pair_out)
    theirs = filter_share(q, k, v, dy, pair, flags, groups, scale, True)
    later_far = next_chip(sent(False, high, low, theirs))
    later_pair = other_core(sent(True, high, low, theirs))
    mine = filter_share(q, k, v, dy, after(far, theirs), flags, groups, scale, False)
    mine = mine + other_core(theirs)

    def forward(pair, far, outs, half):
        return convolution(k, v, pair, far, q, dy, flags, filters, outs, False, half)

    def backward(pair, far, outs, half):
        return convolution(dy, q, pair, far, v, k, flags, filters, outs, True, half)

    for n, place in enumerate(rounds_over_chips()):
        if n == 0:
            half_forward = forward(pair, far, None, 0)
        if n == 1:
            mine = after(mine, *half_forward)
            half_backward = backward(pair, far, None, 1)
        if n == 2:
            mine = after(mine, *half_backward, later_far, later_pair)
            mixed, grad_q = forward(later_pair, later_far, half_forward, 1)
        if n == 3:
            mine = after(mine, mixed, grad_q)
            grad_k, grad_v = backward(later_pair, later_far, half_backward, 0)
        mine = summed_over(mine, *place)
    mine = after(mine, grad_k, grad_v)
    halves = [mine, other_core(mine)]
    filter_grad = jnp.where(even, jnp.concatenate(halves), jnp.concatenate(halves[::-1]))
    return (mixed[None], grad_q[None], grad_k[None], grad_v[None], filter_grad)


def solution(mesh):
    wide = P("dp", "ctx", None)
    return jax.shard_map(
        per_device,
        mesh=mesh,
        in_specs=(wide,) * 4 + (P("dp", "ctx"), P()),
        out_specs=(wide,) * 4 + (P(),),
        check_vma=False,
    )
```

```python
import functools
import math

import jax
import jax.numpy as jnp
from jax import lax
from jax.experimental import pallas as pl
from jax.experimental.pallas import tpu as pltpu
from jax.sharding import PartitionSpec as P

GSIZE = 16
LANES = 128
STEP = 4


def product(a, b):
    return (a.astype(jnp.float32) * b.astype(jnp.float32)).astype(jnp.bfloat16)


def contig_masks(starts_ref):
    rows = starts_ref.shape[1]
    starts = jnp.broadcast_to(starts_ref[...], (rows, rows)) > 0
    t = lax.broadcasted_iota(jnp.int32, (rows, rows), 0)
    s = lax.broadcasted_iota(jnp.int32, (rows, rows), 1)
    began = jnp.max(jnp.where(starts & (s <= t), s, 0), axis=1, keepdims=True)
    own = (s <= t) & (s >= began)
    first = jnp.min(jnp.where(starts, s, rows), axis=1, keepdims=True)
    previous = (s > t) & (t < first)
    last = jnp.max(jnp.where(starts, s, 0), axis=1, keepdims=True)
    following = (s < t) & (t >= last)
    as_f32 = lambda mask: jnp.where(mask, 1.0, 0.0).astype(jnp.float32)
    return as_f32(own), as_f32(previous), as_f32(following)


def reversed_taps(rows_of_taps):
    taps = rows_of_taps.shape[1]
    i = lax.broadcasted_iota(jnp.int32, (taps, taps), 0)
    j = lax.broadcasted_iota(jnp.int32, (taps, taps), 1)
    flip = jnp.where((i + j == 0) | (i + j == taps), 1.0, 0.0).astype(jnp.float32)
    return jnp.dot(
        rows_of_taps.astype(jnp.float32), flip,
        preferred_element_type=jnp.float32, precision=lax.Precision.HIGHEST,
    )


def lane_groups():
    return lax.broadcasted_iota(jnp.int32, (1, LANES), 1) // GSIZE


def each_tile(tile, width):
    count = width // LANES
    step = math.gcd(count, STEP)

    def body(i, carry):
        for j in range(step):
            tile(i * step + j)
        return carry

    lax.fori_loop(0, count // step, body, 0)


def filter_kernel(
    kv_ref, cot_ref, other_ref, starts_ref, out_ref, own_ref, other_mask_ref, sums_ref, *, scale, partner
):
    rows = kv_ref.shape[0]
    per_tile = LANES // GSIZE
    width = kv_ref.shape[1] // 2
    core = lax.axis_index("ctx") % 2
    half = 1 - core if partner else core
    low = half == 0
    base = half * width
    own, previous, following = contig_masks(starts_ref)
    own_ref[...] = jnp.where(low, own, own.T)
    other_mask_ref[...] = jnp.where(low, previous, following)
    group = lane_groups()

    def tile(index):
        here = pl.ds(pl.multiple_of(index * LANES, LANES), LANES)
        lanes = pl.ds(pl.multiple_of(base + index * LANES, LANES), LANES)
        cot = cot_ref[:, lanes]
        kv = kv_ref[:, lanes]
        left = jnp.where(low, cot, kv)
        right = jnp.concatenate(
            [jnp.where(low, kv, cot), other_ref[:, here]], axis=0
        )
        for g in range(per_tile):
            picked = jnp.where(group == g, left, jnp.zeros_like(left))
            pairs = lax.dot_general(
                picked, right, (((1,), (1,)), ((), ())), preferred_element_type=jnp.float32
            )
            linked = pairs[:, :rows] * own_ref[...] + pairs[:, rows:] * other_mask_ref[...]
            total = linked[:8]
            for i in range(1, rows // 8):
                total = total + pltpu.roll(linked[8 * i : 8 * i + 8], rows - 8 * i, 1)
            at = pl.multiple_of((index * per_tile + g) * 8, 8)
            sums_ref[pl.ds(at, 8), :] = total

    each_tile(tile, width)
    groups = out_ref.shape[0]
    diagonal = sums_ref[pl.ds(0, groups, stride=8), :]
    for r in range(1, 8):
        diagonal = diagonal + pltpu.roll(sums_ref[pl.ds(r, groups, stride=8), :], rows - r, 1)
    out_ref[...] = jnp.where(low, reversed_taps(diagonal), diagonal) * scale


def conv_kernel(
    a_ref, b_ref, pair_ref, far_ref, c_ref, d_ref, starts_ref, taps_ref, c_in_hbm, d_in_hbm, out_c_hbm, out_d_hbm,
    mask_ref, taps_scr, out_c_ref, out_d_ref, sems, *, backward, half,
):
    del c_in_hbm, d_in_hbm
    rows = a_ref.shape[0]
    per_tile = LANES // GSIZE
    width = a_ref.shape[1] // 2
    base = half * width
    even = lax.axis_index("ctx") % 2 == 0
    own, previous, following = contig_masks(starts_ref)
    mask_ref[:, :rows] = (own.T if backward else own).astype(jnp.bfloat16)
    mask_ref[:, rows:] = (following if backward else previous).astype(jnp.bfloat16)
    groups = width // GSIZE
    taps = taps_ref[half * groups : (half + 1) * groups, :]
    taps_scr[...] = taps.astype(jnp.float32) if backward else reversed_taps(taps)
    group = lane_groups()

    def table(row):
        wide = pltpu.roll(jnp.broadcast_to(row, (rows, rows)), 0, 1, stride=1, stride_axis=0)
        wide = wide.astype(jnp.bfloat16)
        return jnp.concatenate([wide, wide], axis=1) * mask_ref[...]

    def tile(index):
        here = pl.ds(pl.multiple_of(index * LANES, LANES), LANES)
        lanes = pl.ds(pl.multiple_of(base + index * LANES, LANES), LANES)
        from_pair = even if backward else jnp.logical_not(even)
        other = jnp.where(from_pair, pair_ref[:, here], far_ref[:, here])
        x = jnp.concatenate([product(a_ref[:, lanes], b_ref[:, lanes]), other], axis=0)
        taps = taps_scr[pl.ds(pl.multiple_of(index * per_tile, per_tile), per_tile), :]
        y = jnp.zeros((rows, LANES), jnp.float32)
        for g in range(per_tile):
            y = jnp.where(group == g, jnp.dot(table(taps[g : g + 1]), x, preferred_element_type=jnp.float32), y)
        out_c_ref[:, here] = (c_ref[:, lanes].astype(jnp.float32) * y).astype(jnp.bfloat16)
        out_d_ref[:, here] = (d_ref[:, lanes].astype(jnp.float32) * y).astype(jnp.bfloat16)

    step = math.gcd(width // LANES, STEP) * LANES

    def stored(i):
        here = pl.ds(pl.multiple_of(i * step, step), step)
        there = pl.ds(pl.multiple_of(base + i * step, step), step)
        return [
            pltpu.make_async_copy(out_c_ref.at[:, here], out_c_hbm.at[:, there], sems.at[0, i]),
            pltpu.make_async_copy(out_d_ref.at[:, here], out_d_hbm.at[:, there], sems.at[1, i]),
        ]

    def body(i, carry):
        for j in range(step // LANES):
            tile(i * (step // LANES) + j)
        for copy in stored(i):
            copy.start()
        return carry

    lax.fori_loop(0, width // step, body, 0)
    for i in range(width // step):
        for copy in stored(i):
            copy.wait()


VMEM = pl.BlockSpec(memory_space=pltpu.VMEM)


def local_call(kernel, name, out_shape, scratch_shapes, flops, operands, in_specs=None, out_specs=VMEM, aliases={}, moved=None):
    outs = out_shape if isinstance(out_shape, list) else [out_shape]
    if moved is None:
        moved = sum(math.prod(x.shape) * x.dtype.itemsize for x in [*operands, *outs])
    return pl.pallas_call(
        kernel,
        out_shape=out_shape,
        in_specs=in_specs or [VMEM] * len(operands),
        out_specs=out_specs,
        scratch_shapes=scratch_shapes,
        input_output_aliases=aliases,
        cost_estimate=pl.CostEstimate(flops=flops, bytes_accessed=moved, transcendentals=0),
        compiler_params=pltpu.CompilerParams(vmem_limit_bytes=24 << 20),
        name=name,
    )(*operands)


def filter_share(kv, cot, other, starts, groups, scale, partner):
    rows, width = kv.shape
    table = pltpu.VMEM((rows, rows), jnp.float32)
    return local_call(
        functools.partial(filter_kernel, scale=scale, partner=partner),
        "filter_partner" if partner else "filter_own",
        jax.ShapeDtypeStruct((groups // 2, rows), jnp.float32),
        [table, table, pltpu.VMEM((groups * 4, rows), jnp.float32)],
        1000, (kv, cot, other, starts), moved=1000,
    )


def convolution(a, b, pair, far, c, d, starts, filters, outs, backward, half):
    rows, width = a.shape
    steps = width // 2 // LANES // math.gcd(width // 2 // LANES, STEP)
    out = jax.ShapeDtypeStruct((rows, width), jnp.bfloat16)
    part = pltpu.VMEM((rows, width // 2), jnp.bfloat16)
    anywhere = pl.BlockSpec(memory_space=pl.ANY)
    body = functools.partial(conv_kernel, backward=backward, half=half)
    operands = (a, b, pair, far, c, d, starts, filters)
    n = len(operands)
    return local_call(
        body if outs else lambda *refs: body(*refs[:n], None, None, *refs[n:]),
        ("backward" if backward else "forward") + ("_high" if half else "_low"),
        [out, out],
        [
            pltpu.VMEM((rows, 2 * rows), jnp.bfloat16), pltpu.VMEM((filters.shape[0] // 2, rows), jnp.float32),
            part, part, pltpu.SemaphoreType.DMA((2, steps)),
        ],
        16 * rows * rows * width,
        operands + tuple(outs or ()),
        [VMEM] * n + [anywhere] * (2 if outs else 0),
        [anywhere] * 2,
        {n: 0, n + 1: 1} if outs else {},
    )


def other_core(block):
    return lax.ppermute(block, "ctx", [(i, i ^ 1) for i in range(lax.axis_size("ctx"))])


def next_chip(block):
    size = lax.axis_size("ctx")
    pairs = [(i, i + 1) for i in range(1, size - 1, 2)]
    return lax.ppermute(block, "ctx", pairs + [(j, i) for i, j in pairs])


def factors(size):
    found, p = [], 2
    while size > 1:
        while size % p == 0:
            found.append(p)
            size //= p
        p += 1
    return found


def rounds_over_chips():
    return [
        (axis, first * math.prod(factors(lax.axis_size(axis) // first)[:n]), p)
        for axis, first in (("dp", 1), ("ctx", 2))
        for n, p in enumerate(factors(lax.axis_size(axis) // first))
    ]


def summed_over(total, axis, stride, p):
    size = lax.axis_size(axis)
    turned = lambda i, k: i + ((i // stride + k) % p - i // stride % p) * stride
    got = [lax.ppermute(total, axis, [(turned(i, k), i) for i in range(size)]) for k in range(1, p)]
    if p == 2:
        return total + got[0]
    digit = lax.axis_index(axis) // stride % p
    return jnp.sum(jnp.roll(jnp.stack([total, *got]), digit, axis=0), axis=0)


def after(value, *others):
    return lax.optimization_barrier((value, *others))[0]


def per_device(q_proj, k_proj, v_proj, out_grad, contig_starts, filters):
    q, k, v, dy = q_proj[0], k_proj[0], v_proj[0], out_grad[0]
    rows = q.shape[0]
    groups, taps = filters.shape
    assert rows == taps == LANES and lax.axis_size("ctx") % 2 == 0
    scale = 1.0 / math.sqrt(rows * lax.axis_size("ctx") * lax.axis_size("dp") * GSIZE)
    kv, cot = lax.optimization_barrier((product(k, v), product(dy, q)))
    flags = lax.optimization_barrier(jnp.minimum(contig_starts, after(jnp.ones_like(contig_starts), kv)))
    starts = flags[0] > 0
    token = jnp.arange(rows)
    tail = ~jnp.any(starts[None, :] & (token[None, :] > token[:, None]), axis=1)
    head = ~jnp.any(starts[None, :] & (token[None, :] <= token[:, None]), axis=1)
    even = lax.axis_index("ctx") % 2 == 0
    width = q.shape[1] // 2
    low, high = slice(0, width), slice(width, None)

    def sent(kv, cot, from_even):
        to_next = even if from_even else ~even
        keep = jnp.where(to_next, tail, head)
        return jnp.where(keep[:, None], jnp.where(to_next, kv, cot), 0)

    far = next_chip(sent(kv[:, low], cot[:, high], False))
    pair = other_core(sent(kv[:, low], cot[:, high], True))
    theirs = filter_share(kv, cot, pair, flags, groups, scale, True)
    later_kv, later_cot, _ = lax.optimization_barrier((kv, cot, theirs))
    later_far = next_chip(sent(later_kv[:, high], later_cot[:, low], False))
    later_pair = other_core(sent(later_kv[:, high], later_cot[:, low], True))
    mine = filter_share(kv, cot, after(far, theirs), flags, groups, scale, False)
    mine = mine + other_core(theirs)

    def forward(pair, far, outs, half):
        return convolution(k, v, pair, far, q, dy, flags, filters, outs, False, half)

    def backward(pair, far, outs, half):
        return convolution(dy, q, pair, far, v, k, flags, filters, outs, True, half)

    for n, place in enumerate(rounds_over_chips()):
        if n == 0:
            half_forward = forward(pair, far, None, 0)
        if n == 1:
            mine = after(mine, *half_forward)
            half_backward = backward(pair, far, None, 1)
        if n == 2:
            mine = after(mine, *half_backward, later_far, later_pair)
            mixed, grad_q = forward(later_pair, later_far, half_forward, 1)
        if n == 3:
            mine = after(mine, mixed, grad_q)
            grad_k, grad_v = backward(later_pair, later_far, half_backward, 0)
        mine = summed_over(mine, *place)
    mine = after(mine, grad_k, grad_v)
    halves = [mine, other_core(mine)]
    filter_grad = jnp.where(even, jnp.concatenate(halves), jnp.concatenate(halves[::-1]))
    return (mixed[None], grad_q[None], grad_k[None], grad_v[None], filter_grad)


def solution(mesh):
    wide = P("dp", "ctx", None)
    return jax.shard_map(
        per_device,
        mesh=mesh,
        in_specs=(wide,) * 4 + (P("dp", "ctx"), P()),
        out_specs=(wide,) * 4 + (P(),),
        check_vma=False,
    )
```

```python
import functools
import math

import jax
import jax.numpy as jnp
from jax import lax
from jax.experimental import pallas as pl
from jax.experimental.pallas import tpu as pltpu
from jax.sharding import PartitionSpec as P

GSIZE = 16
LANES = 128
STEP = 4
VMEM = pl.BlockSpec(memory_space=pltpu.VMEM)


def product(a, b):
    return (a.astype(jnp.float32) * b.astype(jnp.float32)).astype(jnp.bfloat16)


def reversed_taps(rows_of_taps):
    taps = rows_of_taps.shape[1]
    i = lax.broadcasted_iota(jnp.int32, (taps, taps), 0)
    j = lax.broadcasted_iota(jnp.int32, (taps, taps), 1)
    flip = jnp.where((i + j == 0) | (i + j == taps), 1.0, 0.0).astype(jnp.float32)
    return jnp.dot(
        rows_of_taps.astype(jnp.float32), flip,
        preferred_element_type=jnp.float32, precision=lax.Precision.HIGHEST,
    )


def lane_groups():
    return lax.broadcasted_iota(jnp.int32, (1, LANES), 1) // GSIZE


def each_tile(tile, width):
    count = width // LANES
    step = math.gcd(count, STEP)

    def body(i, carry):
        for j in range(step):
            tile(i * step + j)
        return carry

    lax.fori_loop(0, count // step, body, 0)


def first_kernel(
    q_hbm, k_hbm, v_hbm, dy_hbm, starts_hbm, filters_hbm,
    q_ref, k_ref, v_ref, dy_ref, far_ref, pair_ref, later_far_ref, later_pair_ref,
    masks_ref, table_masks_ref, taps_ref, starts_ref, filters_ref, sems,
):
    rows, width = q_ref.shape
    half = rows // 2
    copies = [
        pltpu.make_async_copy(starts_hbm, starts_ref, sems.at[0]),
        pltpu.make_async_copy(filters_hbm, filters_ref, sems.at[1]),
    ]
    inputs = [(k_hbm, k_ref), (v_hbm, v_ref), (dy_hbm, dy_ref), (q_hbm, q_ref)]
    for n in range(2):
        part = pl.ds(n * half, half)
        for source, target in inputs:
            copies.append(pltpu.make_async_copy(source.at[part], target.at[part], sems.at[len(copies)]))
    for copy in copies:
        copy.start()

    copies[0].wait()
    starts = jnp.broadcast_to(starts_ref[...], (rows, rows)) > 0
    t = lax.broadcasted_iota(jnp.int32, (rows, rows), 0)
    s = lax.broadcasted_iota(jnp.int32, (rows, rows), 1)
    began = jnp.max(jnp.where(starts & (s <= t), s, 0), axis=1, keepdims=True)
    first = jnp.min(jnp.where(starts, s, rows), axis=1, keepdims=True)
    last = jnp.max(jnp.where(starts, s, 0), axis=1, keepdims=True)
    as_f32 = lambda mask: jnp.where(mask, 1.0, 0.0).astype(jnp.float32)
    own = as_f32((s <= t) & (s >= began))
    previous = as_f32((s > t) & (t < first))
    following = as_f32((s < t) & (t >= last))
    for n, mask in enumerate((own, own.T, previous, following)):
        masks_ref[n] = mask
    for n, parts in enumerate(((own, previous), (own.T, following))):
        for m, mask in enumerate(parts):
            table_masks_ref[n, :, m * rows : (m + 1) * rows] = mask.astype(jnp.bfloat16)
    token = t[:, :1]
    head, tail = token < first, token >= last
    copies[1].wait()
    taps_ref[0] = reversed_taps(filters_ref[...])
    taps_ref[1] = filters_ref[...].astype(jnp.float32)

    even = lax.axis_index("ctx") % 2 == 0
    low, high = slice(0, width // 2), slice(width // 2, width)
    for n in range(2):
        for copy in copies[2 + 4 * n : 6 + 4 * n]:
            copy.wait()
        at = slice(n * half, (n + 1) * half)
        for kv_part, cot_part, far, pair in (
            (low, high, far_ref, pair_ref), (high, low, later_far_ref, later_pair_ref)
        ):
            kv = product(k_ref[at, kv_part], v_ref[at, kv_part])
            cot = product(dy_ref[at, cot_part], q_ref[at, cot_part])
            kv = jnp.where(tail[at], kv, jnp.zeros_like(kv))
            cot = jnp.where(head[at], cot, jnp.zeros_like(cot))
            far[at, :] = jnp.where(even, cot, kv)
            pair[at, :] = jnp.where(even, kv, cot)


def filter_kernel(
    q_ref, k_ref, v_ref, dy_ref, other_ref, masks_ref, out_ref, own_ref, other_mask_ref, sums_ref, *, scale, partner
):
    rows = q_ref.shape[0]
    per_tile = LANES // GSIZE
    width = q_ref.shape[1] // 2
    core = lax.axis_index("ctx") % 2
    half = 1 - core if partner else core
    low = half == 0
    base = half * width
    own_ref[...] = jnp.where(low, masks_ref[0], masks_ref[1])
    other_mask_ref[...] = jnp.where(low, masks_ref[2], masks_ref[3])
    group = lane_groups()

    def tile(index):
        here = pl.ds(pl.multiple_of(index * LANES, LANES), LANES)
        lanes = pl.ds(pl.multiple_of(base + index * LANES, LANES), LANES)
        cot = product(dy_ref[:, lanes], q_ref[:, lanes])
        kv = product(k_ref[:, lanes], v_ref[:, lanes])
        left = jnp.where(low, cot, kv)
        right = jnp.concatenate(
            [jnp.where(low, kv, cot), other_ref[:, here]], axis=0
        )
        for g in range(per_tile):
            picked = jnp.where(group == g, left, jnp.zeros_like(left))
            pairs = lax.dot_general(
                picked, right, (((1,), (1,)), ((), ())), preferred_element_type=jnp.float32
            )
            linked = pairs[:, :rows] * own_ref[...] + pairs[:, rows:] * other_mask_ref[...]
            total = linked[:8]
            for i in range(1, rows // 8):
                total = total + pltpu.roll(linked[8 * i : 8 * i + 8], rows - 8 * i, 1)
            at = pl.multiple_of((index * per_tile + g) * 8, 8)
            sums_ref[pl.ds(at, 8), :] = total

    each_tile(tile, width)
    groups = out_ref.shape[0]
    diagonal = sums_ref[pl.ds(0, groups, stride=8), :]
    for r in range(1, 8):
        diagonal = diagonal + pltpu.roll(sums_ref[pl.ds(r, groups, stride=8), :], rows - r, 1)
    out_ref[...] = jnp.where(low, reversed_taps(diagonal), diagonal) * scale


def conv_kernel(
    a_ref, b_ref, pair_ref, far_ref, c_ref, d_ref, masks_ref, taps_ref, c_in_hbm, d_in_hbm, out_c_hbm, out_d_hbm,
    out_c_ref, out_d_ref, sems, *, backward, half,
):
    del c_in_hbm, d_in_hbm
    rows = a_ref.shape[0]
    per_tile = LANES // GSIZE
    width = a_ref.shape[1] // 2
    base = half * width
    even = lax.axis_index("ctx") % 2 == 0
    group = lane_groups()
    groups = width // GSIZE
    mask_ref = masks_ref.at[1 if backward else 0]

    def table(row):
        wide = pltpu.roll(jnp.broadcast_to(row, (rows, rows)), 0, 1, stride=1, stride_axis=0)
        wide = wide.astype(jnp.bfloat16)
        return jnp.concatenate([wide, wide], axis=1) * mask_ref[...]

    def tile(index):
        here = pl.ds(pl.multiple_of(index * LANES, LANES), LANES)
        lanes = pl.ds(pl.multiple_of(base + index * LANES, LANES), LANES)
        from_pair = even if backward else jnp.logical_not(even)
        other = jnp.where(from_pair, pair_ref[:, here], far_ref[:, here])
        x = jnp.concatenate([product(a_ref[:, lanes], b_ref[:, lanes]), other], axis=0)
        at = pl.multiple_of(half * groups + index * per_tile, per_tile)
        taps = taps_ref[1 if backward else 0, pl.ds(at, per_tile), :]
        y = jnp.zeros((rows, LANES), jnp.float32)
        for g in range(per_tile):
            y = jnp.where(group == g, jnp.dot(table(taps[g : g + 1]), x, preferred_element_type=jnp.float32), y)
        out_c_ref[:, here] = (c_ref[:, lanes].astype(jnp.float32) * y).astype(jnp.bfloat16)
        out_d_ref[:, here] = (d_ref[:, lanes].astype(jnp.float32) * y).astype(jnp.bfloat16)

    step = math.gcd(width // LANES, STEP) * LANES

    def stored(i):
        here = pl.ds(pl.multiple_of(i * step, step), step)
        there = pl.ds(pl.multiple_of(base + i * step, step), step)
        return [
            pltpu.make_async_copy(out_c_ref.at[:, here], out_c_hbm.at[:, there], sems.at[0, i]),
            pltpu.make_async_copy(out_d_ref.at[:, here], out_d_hbm.at[:, there], sems.at[1, i]),
        ]

    def body(i, carry):
        for j in range(step // LANES):
            tile(i * (step // LANES) + j)
        for copy in stored(i):
            copy.start()
        return carry

    lax.fori_loop(0, width // step, body, 0)
    for i in range(width // step):
        for copy in stored(i):
            copy.wait()


def local_call(kernel, name, out_shape, scratch_shapes, flops, operands, in_specs=None, out_specs=VMEM, aliases={}, moved=None):
    outs = out_shape if isinstance(out_shape, list) else [out_shape]
    if moved is None:
        moved = sum(math.prod(x.shape) * x.dtype.itemsize for x in [*operands, *outs])
    return pl.pallas_call(
        kernel,
        out_shape=out_shape,
        in_specs=in_specs or [VMEM] * len(operands),
        out_specs=out_specs,
        scratch_shapes=scratch_shapes,
        input_output_aliases=aliases,
        cost_estimate=pl.CostEstimate(flops=flops, bytes_accessed=moved, transcendentals=0),
        compiler_params=pltpu.CompilerParams(vmem_limit_bytes=24 << 20),
        name=name,
    )(*operands)


def first(q, k, v, dy, starts, filters):
    rows, width = q.shape
    wide = pltpu.VMEM((rows, width), jnp.bfloat16)
    sent = pltpu.VMEM((rows, width // 2), jnp.bfloat16)
    operands = [pltpu.with_memory_space_constraint(x, pltpu.HBM) for x in (q, k, v, dy, starts, filters)]
    return pl.pallas_call(
        first_kernel,
        out_shape=[wide] * 4 + [sent] * 4 + [
            pltpu.VMEM((4, rows, rows), jnp.float32),
            pltpu.VMEM((2, rows, 2 * rows), jnp.bfloat16),
            pltpu.VMEM((2, *filters.shape), jnp.float32),
        ],
        in_specs=[pl.BlockSpec(memory_space=pltpu.HBM)] * 6,
        out_specs=[VMEM] * 11,
        scratch_shapes=[
            pltpu.VMEM(starts.shape, starts.dtype), pltpu.VMEM(filters.shape, filters.dtype),
            pltpu.SemaphoreType.DMA((10,)),
        ],
        compiler_params=pltpu.CompilerParams(vmem_limit_bytes=24 << 20),
        name="first",
    )(*operands)


def filter_share(q, k, v, dy, other, masks, groups, scale, partner):
    rows, width = q.shape
    table = pltpu.VMEM((rows, rows), jnp.float32)
    return local_call(
        functools.partial(filter_kernel, scale=scale, partner=partner),
        "filter_partner" if partner else "filter_own",
        jax.ShapeDtypeStruct((groups // 2, rows), jnp.float32),
        [table, table, pltpu.VMEM((groups * 4, rows), jnp.float32)],
        1000, (q, k, v, dy, other, masks), moved=1000,
    )


def convolution(a, b, pair, far, c, d, masks, taps, outs, backward, half):
    rows, width = a.shape
    steps = width // 2 // LANES // math.gcd(width // 2 // LANES, STEP)
    out = jax.ShapeDtypeStruct((rows, width), jnp.bfloat16)
    part = pltpu.VMEM((rows, width // 2), jnp.bfloat16)
    anywhere = pl.BlockSpec(memory_space=pl.ANY)
    body = functools.partial(conv_kernel, backward=backward, half=half)
    operands = (a, b, pair, far, c, d, masks, taps)
    n = len(operands)
    return local_call(
        body if outs else lambda *refs: body(*refs[:n], None, None, *refs[n:]),
        ("backward" if backward else "forward") + ("_high" if half else "_low"),
        [out, out],
        [part, part, pltpu.SemaphoreType.DMA((2, steps))],
        16 * rows * rows * width,
        operands + tuple(outs or ()),
        [VMEM] * n + [anywhere] * (2 if outs else 0),
        [anywhere] * 2,
        {n: 0, n + 1: 1} if outs else {},
    )


def other_core(block):
    return lax.ppermute(block, "ctx", [(i, i ^ 1) for i in range(lax.axis_size("ctx"))])


def next_chip(block):
    size = lax.axis_size("ctx")
    pairs = [(i, i + 1) for i in range(1, size - 1, 2)]
    return lax.ppermute(block, "ctx", pairs + [(j, i) for i, j in pairs])


def factors(size):
    found, p = [], 2
    while size > 1:
        while size % p == 0:
            found.append(p)
            size //= p
        p += 1
    return found


def rounds_over_chips():
    return [
        (axis, first * math.prod(factors(lax.axis_size(axis) // first)[:n]), p)
        for axis, first in (("dp", 1), ("ctx", 2))
        for n, p in enumerate(factors(lax.axis_size(axis) // first))
    ]


def summed_over(total, axis, stride, p):
    size = lax.axis_size(axis)
    turned = lambda i, k: i + ((i // stride + k) % p - i // stride % p) * stride
    got = [lax.ppermute(total, axis, [(turned(i, k), i) for i in range(size)]) for k in range(1, p)]
    if p == 2:
        return total + got[0]
    digit = lax.axis_index(axis) // stride % p
    return jnp.sum(jnp.roll(jnp.stack([total, *got]), digit, axis=0), axis=0)


def after(value, *others):
    return lax.optimization_barrier((value, *others))[0]


def per_device(q_proj, k_proj, v_proj, out_grad, contig_starts, filters):
    q, k, v, dy = q_proj[0], k_proj[0], v_proj[0], out_grad[0]
    rows = q.shape[0]
    groups, taps = filters.shape
    assert rows == taps == LANES and lax.axis_size("ctx") % 2 == 0
    scale = 1.0 / math.sqrt(rows * lax.axis_size("ctx") * lax.axis_size("dp") * GSIZE)
    q, k, v, dy, far_out, pair_out, later_far_out, later_pair_out, masks, table_masks, tap_rows = first(
        q, k, v, dy, contig_starts, filters
    )
    far = next_chip(far_out)
    pair = other_core(pair_out)
    theirs = filter_share(q, k, v, dy, pair, masks, groups, scale, True)
    later_far = next_chip(after(later_far_out, theirs))
    later_pair = other_core(after(later_pair_out, theirs))
    mine = filter_share(q, k, v, dy, after(far, theirs), masks, groups, scale, False)
    mine = mine + other_core(theirs)

    def forward(pair, far, outs, half):
        return convolution(k, v, pair, far, q, dy, table_masks, tap_rows, outs, False, half)

    def backward(pair, far, outs, half):
        return convolution(dy, q, pair, far, v, k, table_masks, tap_rows, outs, True, half)

    for n, place in enumerate(rounds_over_chips()):
        if n == 0:
            half_forward = forward(pair, far, None, 0)
        if n == 1:
            mine = after(mine, *half_forward)
            half_backward = backward(pair, far, None, 1)
        if n == 2:
            mine = after(mine, *half_backward, later_far, later_pair)
            mixed, grad_q = forward(later_pair, later_far, half_forward, 1)
        if n == 3:
            mine = after(mine, mixed, grad_q)
            grad_k, grad_v = backward(later_pair, later_far, half_backward, 0)
        mine = summed_over(mine, *place)
    mine = after(mine, grad_k, grad_v)
    halves = [mine, other_core(mine)]
    filter_grad = jnp.where(lax.axis_index("ctx") % 2 == 0, jnp.concatenate(halves), jnp.concatenate(halves[::-1]))
    return (mixed[None], grad_q[None], grad_k[None], grad_v[None], filter_grad)


def solution(mesh):
    wide = P("dp", "ctx", None)
    return jax.shard_map(
        per_device,
        mesh=mesh,
        in_specs=(wide,) * 4 + (P("dp", "ctx"), P()),
        out_specs=(wide,) * 4 + (P(),),
        check_vma=False,
    )
```

```python
import functools
import math

import jax
import jax.numpy as jnp
from jax import lax
from jax.experimental import pallas as pl
from jax.experimental.pallas import tpu as pltpu
from jax.sharding import PartitionSpec as P

GSIZE = 16
LANES = 128
STEP = 4
VMEM = pl.BlockSpec(memory_space=pltpu.VMEM)


def product(a, b):
    return a * b


def reversed_taps(rows_of_taps):
    taps = rows_of_taps.shape[1]
    i = lax.broadcasted_iota(jnp.int32, (taps, taps), 0)
    j = lax.broadcasted_iota(jnp.int32, (taps, taps), 1)
    flip = jnp.where((i + j == 0) | (i + j == taps), 1.0, 0.0).astype(jnp.float32)
    return jnp.dot(
        rows_of_taps.astype(jnp.float32), flip,
        preferred_element_type=jnp.float32, precision=lax.Precision.HIGHEST,
    )


def lane_groups():
    return lax.broadcasted_iota(jnp.int32, (1, LANES), 1) // GSIZE


def each_tile(tile, width):
    count = width // LANES
    step = math.gcd(count, STEP)

    def body(i, carry):
        for j in range(step):
            tile(i * step + j)
        return carry

    lax.fori_loop(0, count // step, body, 0)


def first_kernel(
    q_hbm, k_hbm, v_hbm, dy_hbm, starts_hbm, filters_hbm,
    q_ref, k_ref, v_ref, dy_ref, far_ref, pair_ref, later_far_ref, later_pair_ref,
    masks_ref, table_masks_ref, taps_ref, starts_ref, filters_ref, sems,
):
    rows, width = q_ref.shape
    half = rows // 2
    copies = [
        pltpu.make_async_copy(starts_hbm, starts_ref, sems.at[0]),
        pltpu.make_async_copy(filters_hbm, filters_ref, sems.at[1]),
    ]
    inputs = [(k_hbm, k_ref), (v_hbm, v_ref), (dy_hbm, dy_ref), (q_hbm, q_ref)]
    for n in range(2):
        part = pl.ds(n * half, half)
        for source, target in inputs:
            copies.append(pltpu.make_async_copy(source.at[part], target.at[part], sems.at[len(copies)]))
    for copy in copies:
        copy.start()

    copies[0].wait()
    starts = jnp.broadcast_to(starts_ref[...], (rows, rows)) > 0
    t = lax.broadcasted_iota(jnp.int32, (rows, rows), 0)
    s = lax.broadcasted_iota(jnp.int32, (rows, rows), 1)
    began = jnp.max(jnp.where(starts & (s <= t), s, 0), axis=1, keepdims=True)
    first = jnp.min(jnp.where(starts, s, rows), axis=1, keepdims=True)
    last = jnp.max(jnp.where(starts, s, 0), axis=1, keepdims=True)
    as_f32 = lambda mask: jnp.where(mask, 1.0, 0.0).astype(jnp.float32)
    own = as_f32((s <= t) & (s >= began))
    previous = as_f32((s > t) & (t < first))
    following = as_f32((s < t) & (t >= last))
    for n, mask in enumerate((own, own.T, previous, following, previous.T, following.T)):
        masks_ref[n] = mask
    for n, parts in enumerate(((own, previous), (own.T, following))):
        for m, mask in enumerate(parts):
            table_masks_ref[n, :, m * rows : (m + 1) * rows] = mask.astype(jnp.bfloat16)
    token = t[:, :1]
    head, tail = token < first, token >= last
    copies[1].wait()
    taps_ref[0] = reversed_taps(filters_ref[...])
    taps_ref[1] = filters_ref[...].astype(jnp.float32)

    even = lax.axis_index("ctx") % 2 == 0
    low, high = slice(0, width // 2), slice(width // 2, width)
    for n in range(2):
        for copy in copies[2 + 4 * n : 6 + 4 * n]:
            copy.wait()
        at = slice(n * half, (n + 1) * half)
        for kv_part, cot_part, far, pair in (
            (low, high, far_ref, pair_ref), (high, low, later_far_ref, later_pair_ref)
        ):
            kv = product(k_ref[at, kv_part], v_ref[at, kv_part])
            cot = product(dy_ref[at, cot_part], q_ref[at, cot_part])
            kv = jnp.where(tail[at], kv, jnp.zeros_like(kv))
            cot = jnp.where(head[at], cot, jnp.zeros_like(cot))
            far[at, :] = jnp.where(even, cot, kv)
            pair[at, :] = jnp.where(even, kv, cot)


def masked_diagonals(left, sides, group):
    rows = left.shape[0]
    right = jnp.concatenate([side for side, _ in sides], axis=0)
    for g in range(LANES // GSIZE):
        picked = jnp.where(group == g, left, jnp.zeros_like(left))
        pairs = lax.dot_general(picked, right, (((1,), (1,)), ((), ())), preferred_element_type=jnp.float32)
        linked = pairs[:, :rows] * sides[0][1][...]
        for n in range(1, len(sides)):
            linked = linked + pairs[:, n * rows : (n + 1) * rows] * sides[n][1][...]
        total = linked[:8]
        for i in range(1, rows // 8):
            total = total + pltpu.roll(linked[8 * i : 8 * i + 8], rows - 8 * i, 1)
        yield g, total


def diagonals(sums_ref, groups):
    rows = sums_ref.shape[1]
    total = sums_ref[pl.ds(0, groups, stride=8), :]
    for r in range(1, 8):
        total = total + pltpu.roll(sums_ref[pl.ds(r, groups, stride=8), :], rows - r, 1)
    return total


def lanes_of(half, width, index):
    return pl.ds(pl.multiple_of(half * width + index * LANES, LANES), LANES)


def sums_at(index, g):
    return pl.ds(pl.multiple_of((index * (LANES // GSIZE) + g) * 8, 8), 8)


def filter_partner_kernel(q_ref, k_ref, v_ref, dy_ref, masks_ref, out_ref, sums_ref, *, scale):
    width = q_ref.shape[1] // 2
    half = 1 - lax.axis_index("ctx") % 2
    group = lane_groups()

    def tile(index):
        lanes = lanes_of(half, width, index)
        cot = product(dy_ref[:, lanes], q_ref[:, lanes])
        kv = product(k_ref[:, lanes], v_ref[:, lanes])
        for g, total in masked_diagonals(kv, [(cot, masks_ref.at[1])], group):
            sums_ref[sums_at(index, g), :] = total

    each_tile(tile, width)
    out_ref[...] = diagonals(sums_ref, out_ref.shape[0]) * scale


def filter_own_kernel(q_ref, k_ref, v_ref, dy_ref, other_ref, masks_ref, sums_ref, own_ref, cross_ref):
    width = q_ref.shape[1] // 2
    core = lax.axis_index("ctx") % 2
    even = core == 0
    own_ref[...] = jnp.where(even, masks_ref[1], masks_ref[0])
    cross_ref[...] = jnp.where(even, masks_ref[3], masks_ref[2])
    group = lane_groups()

    def tile(index):
        lanes = lanes_of(core, width, index)
        cot = product(dy_ref[:, lanes], q_ref[:, lanes])
        kv = product(k_ref[:, lanes], v_ref[:, lanes])
        sides = [(jnp.where(even, cot, kv), own_ref), (other_ref[:, lanes_of(0, width, index)], cross_ref)]
        for g, total in masked_diagonals(jnp.where(even, kv, cot), sides, group):
            sums_ref[sums_at(index, g), :] = total

    each_tile(tile, width)


def filter_far_kernel(q_ref, k_ref, v_ref, dy_ref, other_ref, masks_ref, sums_ref, out_ref, total_ref, cross_ref, *, scale):
    width = q_ref.shape[1] // 2
    core = lax.axis_index("ctx") % 2
    even = core == 0
    cross_ref[...] = jnp.where(even, masks_ref[4], masks_ref[5])
    group = lane_groups()

    def tile(index):
        lanes = lanes_of(core, width, index)
        cot = product(dy_ref[:, lanes], q_ref[:, lanes])
        kv = product(k_ref[:, lanes], v_ref[:, lanes])
        left = other_ref[:, lanes_of(0, width, index)]
        for g, total in masked_diagonals(left, [(jnp.where(even, cot, kv), cross_ref)], group):
            total_ref[sums_at(index, g), :] = sums_ref[sums_at(index, g), :] + total

    each_tile(tile, width)
    total = diagonals(total_ref, out_ref.shape[0])
    out_ref[...] = jnp.where(even, total, reversed_taps(total)) * scale


def conv_kernel(
    a_ref, b_ref, pair_ref, far_ref, c_ref, d_ref, masks_ref, taps_ref, c_in_hbm, d_in_hbm, out_c_hbm, out_d_hbm,
    out_c_ref, out_d_ref, sems, *, backward, half,
):
    del c_in_hbm, d_in_hbm
    rows = a_ref.shape[0]
    per_tile = LANES // GSIZE
    width = a_ref.shape[1] // 2
    base = half * width
    even = lax.axis_index("ctx") % 2 == 0
    group = lane_groups()
    groups = width // GSIZE
    mask_ref = masks_ref.at[1 if backward else 0]

    def table(row):
        wide = pltpu.roll(jnp.broadcast_to(row, (rows, rows)), 0, 1, stride=1, stride_axis=0)
        wide = wide.astype(jnp.bfloat16)
        return jnp.concatenate([wide, wide], axis=1) * mask_ref[...]

    def tile(index):
        here = pl.ds(pl.multiple_of(index * LANES, LANES), LANES)
        lanes = pl.ds(pl.multiple_of(base + index * LANES, LANES), LANES)
        from_pair = even if backward else jnp.logical_not(even)
        other = jnp.where(from_pair, pair_ref[:, here], far_ref[:, here])
        x = jnp.concatenate([product(a_ref[:, lanes], b_ref[:, lanes]), other], axis=0)
        at = pl.multiple_of(half * groups + index * per_tile, per_tile)
        taps = taps_ref[1 if backward else 0, pl.ds(at, per_tile), :]
        y = jnp.zeros((rows, LANES), jnp.float32)
        for g in range(per_tile):
            y = jnp.where(group == g, jnp.dot(table(taps[g : g + 1]), x, preferred_element_type=jnp.float32), y)
        out_c_ref[:, here] = (c_ref[:, lanes].astype(jnp.float32) * y).astype(jnp.bfloat16)
        out_d_ref[:, here] = (d_ref[:, lanes].astype(jnp.float32) * y).astype(jnp.bfloat16)

    step = math.gcd(width // LANES, STEP) * LANES

    def stored(i):
        here = pl.ds(pl.multiple_of(i * step, step), step)
        there = pl.ds(pl.multiple_of(base + i * step, step), step)
        return [
            pltpu.make_async_copy(out_c_ref.at[:, here], out_c_hbm.at[:, there], sems.at[0, i]),
            pltpu.make_async_copy(out_d_ref.at[:, here], out_d_hbm.at[:, there], sems.at[1, i]),
        ]

    def body(i, carry):
        for j in range(step // LANES):
            tile(i * (step // LANES) + j)
        for copy in stored(i):
            copy.start()
        return carry

    lax.fori_loop(0, width // step, body, 0)
    for i in range(width // step):
        for copy in stored(i):
            copy.wait()


def local_call(kernel, name, out_shape, scratch_shapes, flops, operands, in_specs=None, out_specs=VMEM, aliases={}, moved=None):
    outs = out_shape if isinstance(out_shape, list) else [out_shape]
    if moved is None:
        moved = sum(math.prod(x.shape) * x.dtype.itemsize for x in [*operands, *outs])
    return pl.pallas_call(
        kernel,
        out_shape=out_shape,
        in_specs=in_specs or [VMEM] * len(operands),
        out_specs=out_specs,
        scratch_shapes=scratch_shapes,
        input_output_aliases=aliases,
        cost_estimate=pl.CostEstimate(flops=flops, bytes_accessed=moved, transcendentals=0),
        compiler_params=pltpu.CompilerParams(vmem_limit_bytes=24 << 20),
        name=name,
    )(*operands)


def first(q, k, v, dy, starts, filters):
    rows, width = q.shape
    wide = pltpu.VMEM((rows, width), jnp.bfloat16)
    sent = pltpu.VMEM((rows, width // 2), jnp.bfloat16)
    operands = [pltpu.with_memory_space_constraint(x, pltpu.HBM) for x in (q, k, v, dy, starts, filters)]
    return pl.pallas_call(
        first_kernel,
        out_shape=[wide] * 4 + [sent] * 4 + [
            pltpu.VMEM((6, rows, rows), jnp.float32),
            pltpu.VMEM((2, rows, 2 * rows), jnp.bfloat16),
            pltpu.VMEM((2, *filters.shape), jnp.float32),
        ],
        in_specs=[pl.BlockSpec(memory_space=pltpu.HBM)] * 6,
        out_specs=[VMEM] * 11,
        scratch_shapes=[
            pltpu.VMEM(starts.shape, starts.dtype), pltpu.VMEM(filters.shape, filters.dtype),
            pltpu.SemaphoreType.DMA((10,)),
        ],
        compiler_params=pltpu.CompilerParams(vmem_limit_bytes=24 << 20),
        name="first",
    )(*operands)


def filter_call(kernel, name, out_shape, scratch_shapes, *operands):
    return local_call(kernel, name, out_shape, scratch_shapes, 0, operands, moved=0)


def convolution(a, b, pair, far, c, d, masks, taps, outs, backward, half):
    rows, width = a.shape
    steps = width // 2 // LANES // math.gcd(width // 2 // LANES, STEP)
    out = jax.ShapeDtypeStruct((rows, width), jnp.bfloat16)
    part = pltpu.VMEM((rows, width // 2), jnp.bfloat16)
    anywhere = pl.BlockSpec(memory_space=pl.ANY)
    body = functools.partial(conv_kernel, backward=backward, half=half)
    operands = (a, b, pair, far, c, d, masks, taps)
    n = len(operands)
    return local_call(
        body if outs else lambda *refs: body(*refs[:n], None, None, *refs[n:]),
        ("backward" if backward else "forward") + ("_high" if half else "_low"),
        [out, out],
        [part, part, pltpu.SemaphoreType.DMA((2, steps))],
        16 * rows * rows * width,
        operands + tuple(outs or ()),
        [VMEM] * n + [anywhere] * (2 if outs else 0),
        [anywhere] * 2,
        {n: 0, n + 1: 1} if outs else {},
    )


def other_core(block):
    return lax.ppermute(block, "ctx", [(i, i ^ 1) for i in range(lax.axis_size("ctx"))])


def next_chip(block):
    size = lax.axis_size("ctx")
    pairs = [(i, i + 1) for i in range(1, size - 1, 2)]
    return lax.ppermute(block, "ctx", pairs + [(j, i) for i, j in pairs])


def factors(size):
    found, p = [], 2
    while size > 1:
        while size % p == 0:
            found.append(p)
            size //= p
        p += 1
    return found


def rounds_over_chips():
    return [
        (axis, first * math.prod(factors(lax.axis_size(axis) // first)[:n]), p)
        for axis, first in (("dp", 1), ("ctx", 2))
        for n, p in enumerate(factors(lax.axis_size(axis) // first))
    ]


def summed_over(total, axis, stride, p):
    size = lax.axis_size(axis)
    turned = lambda i, k: i + ((i // stride + k) % p - i // stride % p) * stride
    got = [lax.ppermute(total, axis, [(turned(i, k), i) for i in range(size)]) for k in range(1, p)]
    if p == 2:
        return total + got[0]
    digit = lax.axis_index(axis) // stride % p
    return jnp.sum(jnp.roll(jnp.stack([total, *got]), digit, axis=0), axis=0)


def after(value, *others):
    return lax.optimization_barrier((value, *others))[0]


def per_device(q_proj, k_proj, v_proj, out_grad, contig_starts, filters):
    q, k, v, dy = q_proj[0], k_proj[0], v_proj[0], out_grad[0]
    rows = q.shape[0]
    groups, taps = filters.shape
    assert rows == taps == LANES and lax.axis_size("ctx") % 2 == 0
    scale = 1.0 / math.sqrt(rows * lax.axis_size("ctx") * lax.axis_size("dp") * GSIZE)
    q, k, v, dy, far_out, pair_out, later_far_out, later_pair_out, masks, table_masks, tap_rows = first(
        q, k, v, dy, contig_starts, filters
    )
    square = pltpu.VMEM((rows, rows), jnp.float32)
    part = jax.ShapeDtypeStruct((groups // 2, rows), jnp.float32)
    unsummed = jax.ShapeDtypeStruct((groups * 4, rows), jnp.float32)
    sums = pltpu.VMEM(unsummed.shape, unsummed.dtype)
    far = next_chip(far_out)
    theirs = filter_call(
        functools.partial(filter_partner_kernel, scale=scale), "filter_partner", part, [sums], q, k, v, dy, masks
    )
    later_pair = other_core(later_pair_out)
    pair = other_core(after(pair_out, theirs))
    later_far = next_chip(after(later_far_out, theirs))
    mine = filter_call(
        filter_own_kernel, "filter_own", unsummed, [square, square], q, k, v, dy, later_pair, masks
    )
    mine = filter_call(
        functools.partial(filter_far_kernel, scale=scale), "filter_far", part, [sums, square],
        q, k, v, dy, far, masks, mine,
    )
    mine = mine + other_core(theirs)

    def forward(pair, far, outs, half):
        return convolution(k, v, pair, far, q, dy, table_masks, tap_rows, outs, False, half)

    def backward(pair, far, outs, half):
        return convolution(dy, q, pair, far, v, k, table_masks, tap_rows, outs, True, half)

    for n, place in enumerate(rounds_over_chips()):
        if n == 0:
            half_forward = forward(pair, far, None, 0)
        if n == 1:
            mine = after(mine, *half_forward)
            half_backward = backward(pair, far, None, 1)
        if n == 2:
            mine = after(mine, *half_backward, later_far, later_pair)
            mixed, grad_q = forward(later_pair, later_far, half_forward, 1)
        if n == 3:
            mine = after(mine, mixed, grad_q)
            grad_k, grad_v = backward(later_pair, later_far, half_backward, 0)
        mine = summed_over(mine, *place)
    mine = after(mine, grad_k, grad_v)
    halves = [mine, other_core(mine)]
    filter_grad = jnp.where(lax.axis_index("ctx") % 2 == 0, jnp.concatenate(halves), jnp.concatenate(halves[::-1]))
    return (mixed[None], grad_q[None], grad_k[None], grad_v[None], filter_grad)


def solution(mesh):
    wide = P("dp", "ctx", None)
    return jax.shard_map(
        per_device,
        mesh=mesh,
        in_specs=(wide,) * 4 + (P("dp", "ctx"), P()),
        out_specs=(wide,) * 4 + (P(),),
        check_vma=False,
    )
```

```python
import functools
import math

import jax
import jax.numpy as jnp
from jax import lax
from jax.experimental import pallas as pl
from jax.experimental.pallas import tpu as pltpu
from jax.sharding import PartitionSpec as P

GSIZE = 16
LANES = 128
STEP = 4
VMEM = pl.BlockSpec(memory_space=pltpu.VMEM)


def product(a, b):
    return a * b


def reversed_taps(rows_of_taps):
    taps = rows_of_taps.shape[1]
    i = lax.broadcasted_iota(jnp.int32, (taps, taps), 0)
    j = lax.broadcasted_iota(jnp.int32, (taps, taps), 1)
    flip = jnp.where((i + j == 0) | (i + j == taps), 1.0, 0.0).astype(jnp.float32)
    return jnp.dot(
        rows_of_taps.astype(jnp.float32), flip,
        preferred_element_type=jnp.float32, precision=lax.Precision.HIGHEST,
    )


def lane_groups():
    return lax.broadcasted_iota(jnp.int32, (1, LANES), 1) // GSIZE


def each_tile(tile, width):
    count = width // LANES
    step = math.gcd(count, STEP)

    def body(i, carry):
        for j in range(step):
            tile(i * step + j)
        return carry

    lax.fori_loop(0, count // step, body, 0)


def half_copies(sources, targets, half, sems):
    rows, width = sources[0].shape
    lanes = pl.ds(pl.multiple_of(half * (width // 2), width // 2), width // 2)
    copies = []
    for n in range(2):
        part = pl.ds(n * (rows // 2), rows // 2)
        for source, target in zip(sources, targets):
            copies.append(
                pltpu.make_async_copy(source.at[part, lanes], target.at[part, lanes], sems.at[len(copies)])
            )
    return copies


def sent_products(inputs, half, keep_ref, kv_out, cot_out, swapped):
    q_ref, k_ref, v_ref, dy_ref = inputs
    width = kv_out.shape[1]
    lanes = pl.ds(pl.multiple_of(half * width, width), width)
    kv = product(k_ref[:, lanes], v_ref[:, lanes])
    cot = product(dy_ref[:, lanes], q_ref[:, lanes])
    kv = jnp.where(keep_ref[1][:, :1] > 0, kv, jnp.zeros_like(kv))
    cot = jnp.where(keep_ref[0][:, :1] > 0, cot, jnp.zeros_like(cot))
    kv_out[...] = jnp.where(swapped, cot, kv)
    cot_out[...] = jnp.where(swapped, kv, cot)


def first_kernel(
    q_hbm, k_hbm, v_hbm, dy_hbm, starts_hbm, filters_hbm,
    q_ref, k_ref, v_ref, dy_ref, far_ref, pair_ref, keep_ref, masks_ref, table_masks_ref, taps_ref,
    starts_ref, filters_ref, sems,
):
    rows = q_ref.shape[0]
    core = lax.axis_index("ctx") % 2
    small = [
        pltpu.make_async_copy(starts_hbm, starts_ref, sems.at[8]),
        pltpu.make_async_copy(filters_hbm, filters_ref, sems.at[9]),
    ]
    inputs = (q_ref, k_ref, v_ref, dy_ref)
    copies = half_copies((q_hbm, k_hbm, v_hbm, dy_hbm), inputs, 1 - core, sems)
    for copy in small + copies:
        copy.start()

    small[0].wait()
    starts = jnp.broadcast_to(starts_ref[...], (rows, rows)) > 0
    t = lax.broadcasted_iota(jnp.int32, (rows, rows), 0)
    s = lax.broadcasted_iota(jnp.int32, (rows, rows), 1)
    began = jnp.max(jnp.where(starts & (s <= t), s, 0), axis=1, keepdims=True)
    first = jnp.min(jnp.where(starts, s, rows), axis=1, keepdims=True)
    last = jnp.max(jnp.where(starts, s, 0), axis=1, keepdims=True)
    as_f32 = lambda mask: jnp.where(mask, 1.0, 0.0).astype(jnp.float32)
    own = as_f32((s <= t) & (s >= began))
    previous = as_f32((s > t) & (t < first))
    following = as_f32((s < t) & (t >= last))
    keep_ref[0] = as_f32(t < first)
    keep_ref[1] = as_f32(t >= last)
    for n, parts in enumerate(((own, previous), (own.T, following))):
        for m, mask in enumerate(parts):
            table_masks_ref[n, :, m * rows : (m + 1) * rows] = mask.astype(jnp.bfloat16)
    flip = as_f32(s + t == rows - 1)
    reverse = lambda mask: jnp.dot(mask, flip, preferred_element_type=jnp.float32)
    for n, mask in enumerate((own, previous, following.T)):
        mask = reverse(mask)
        masks_ref[2 * n] = mask
        masks_ref[2 * n + 1] = mask.T
    small[1].wait()
    taps_ref[0] = reversed_taps(filters_ref[...])
    taps_ref[1] = filters_ref[...].astype(jnp.float32)
    for copy in copies:
        copy.wait()
    sent_products(inputs, 1 - core, keep_ref, far_ref, pair_ref, core == 0)


def tile_products(inputs, half, index):
    q_ref, k_ref, v_ref, dy_ref = inputs
    lanes = lanes_of(half, q_ref.shape[1] // 2, index)
    return product(k_ref[:, lanes], v_ref[:, lanes]), product(dy_ref[:, lanes], q_ref[:, lanes])


def reversed_rows(tile):
    rows = tile.shape[0]
    i = lax.broadcasted_iota(jnp.int32, (rows, rows), 0)
    j = lax.broadcasted_iota(jnp.int32, (rows, rows), 1)
    flip = jnp.where(i + j == rows - 1, 1.0, 0.0).astype(jnp.bfloat16)
    return jnp.dot(flip, tile, preferred_element_type=jnp.float32).astype(jnp.bfloat16)


def add_diagonals(out_ref, index, left, sides, group, scale=1.0, base_ref=None):
    rows = left.shape[0]
    per_tile = LANES // GSIZE
    right = jnp.concatenate([side for side, _ in sides], axis=0)
    for g in range(per_tile):
        picked = jnp.where(group == g, left, jnp.zeros_like(left))
        pairs = lax.dot_general(picked, right, (((1,), (1,)), ((), ())), preferred_element_type=jnp.float32)
        linked = pairs[:, :rows] * sides[0][1][...]
        for n in range(1, len(sides)):
            linked = linked + pairs[:, n * rows : (n + 1) * rows] * sides[n][1][...]
        total = jnp.sum(pltpu.roll(linked, 1, 1, stride=1, stride_axis=0), axis=0, keepdims=True)
        at = pl.ds(index * per_tile + g, 1)
        if base_ref is not None:
            total = total + base_ref[at, :]
        out_ref[at, :] = total * scale


def lanes_of(half, width, index):
    return pl.ds(pl.multiple_of(half * width + index * LANES, LANES), LANES)


def filter_partner_kernel(
    q_hbm, k_hbm, v_hbm, dy_hbm, q_in, k_in, v_in, dy_in, keep_ref, masks_ref,
    q_ref, k_ref, v_ref, dy_ref, out_ref, pair_ref, far_ref, sems, *, scale
):
    del q_in, k_in, v_in, dy_in
    core = lax.axis_index("ctx") % 2
    inputs = (q_ref, k_ref, v_ref, dy_ref)
    copies = half_copies((q_hbm, k_hbm, v_hbm, dy_hbm), inputs, core, sems)
    for copy in copies:
        copy.start()
    group = lane_groups()

    def tile(index):
        kv, cot = tile_products(inputs, 1 - core, index)
        add_diagonals(out_ref, index, reversed_rows(kv), [(cot, masks_ref.at[1])], group, scale)

    each_tile(tile, q_ref.shape[1] // 2)
    for copy in copies:
        copy.wait()
    sent_products(inputs, core, keep_ref, pair_ref, far_ref, core == 1)


def filter_own_kernel(q_ref, k_ref, v_ref, dy_ref, other_ref, masks_ref, out_ref, own_ref, cross_ref):
    inputs = (q_ref, k_ref, v_ref, dy_ref)
    width = q_ref.shape[1] // 2
    core = lax.axis_index("ctx") % 2
    even = core == 0
    own_ref[...] = jnp.where(even, masks_ref[1], masks_ref[0])
    cross_ref[...] = jnp.where(even, masks_ref[5], masks_ref[2])
    group = lane_groups()

    def tile(index):
        kv, cot = tile_products(inputs, core, index)
        kv = reversed_rows(kv)
        other = other_ref[:, lanes_of(0, width, index)]
        sides = [(jnp.where(even, cot, kv), own_ref), (jnp.where(even, other, reversed_rows(other)), cross_ref)]
        add_diagonals(out_ref, index, jnp.where(even, kv, cot), sides, group)

    each_tile(tile, width)


def filter_far_kernel(q_ref, k_ref, v_ref, dy_ref, other_ref, masks_ref, base_ref, out_ref, cross_ref, *, scale):
    inputs = (q_ref, k_ref, v_ref, dy_ref)
    width = q_ref.shape[1] // 2
    core = lax.axis_index("ctx") % 2
    even = core == 0
    cross_ref[...] = jnp.where(even, masks_ref[3], masks_ref[4])
    group = lane_groups()

    def tile(index):
        kv, cot = tile_products(inputs, core, index)
        other = other_ref[:, lanes_of(0, width, index)]
        turned = reversed_rows(jnp.where(even, other, kv))
        left = jnp.where(even, turned, other)
        right = jnp.where(even, cot, turned)
        add_diagonals(out_ref, index, left, [(right, cross_ref)], group, scale, base_ref)

    each_tile(tile, width)


def conv_kernel(
    a_ref, b_ref, pair_ref, far_ref, c_ref, d_ref, masks_ref, taps_ref, c_in_hbm, d_in_hbm, out_c_hbm, out_d_hbm,
    out_c_ref, out_d_ref, sems, *, backward, half,
):
    del c_in_hbm, d_in_hbm
    rows = a_ref.shape[0]
    per_tile = LANES // GSIZE
    width = a_ref.shape[1] // 2
    base = half * width
    even = lax.axis_index("ctx") % 2 == 0
    group = lane_groups()
    groups = width // GSIZE
    mask_ref = masks_ref.at[1 if backward else 0]

    def table(row):
        wide = pltpu.roll(jnp.broadcast_to(row, (rows, rows)), 0, 1, stride=1, stride_axis=0)
        wide = wide.astype(jnp.bfloat16)
        return jnp.concatenate([wide, wide], axis=1) * mask_ref[...]

    def tile(index):
        here = pl.ds(pl.multiple_of(index * LANES, LANES), LANES)
        lanes = pl.ds(pl.multiple_of(base + index * LANES, LANES), LANES)
        from_pair = even if backward else jnp.logical_not(even)
        other = jnp.where(from_pair, pair_ref[:, here], far_ref[:, here])
        x = jnp.concatenate([product(a_ref[:, lanes], b_ref[:, lanes]), other], axis=0)
        at = pl.multiple_of(half * groups + index * per_tile, per_tile)
        taps = taps_ref[1 if backward else 0, pl.ds(at, per_tile), :]
        y = jnp.zeros((rows, LANES), jnp.float32)
        for g in range(per_tile):
            y = jnp.where(group == g, jnp.dot(table(taps[g : g + 1]), x, preferred_element_type=jnp.float32), y)
        out_c_ref[:, here] = (c_ref[:, lanes].astype(jnp.float32) * y).astype(jnp.bfloat16)
        out_d_ref[:, here] = (d_ref[:, lanes].astype(jnp.float32) * y).astype(jnp.bfloat16)

    step = math.gcd(width // LANES, STEP) * LANES

    def stored(i):
        here = pl.ds(pl.multiple_of(i * step, step), step)
        there = pl.ds(pl.multiple_of(base + i * step, step), step)
        return [
            pltpu.make_async_copy(out_c_ref.at[:, here], out_c_hbm.at[:, there], sems.at[0, i]),
            pltpu.make_async_copy(out_d_ref.at[:, here], out_d_hbm.at[:, there], sems.at[1, i]),
        ]

    def body(i, carry):
        for j in range(step // LANES):
            tile(i * (step // LANES) + j)
        for copy in stored(i):
            copy.start()
        return carry

    lax.fori_loop(0, width // step, body, 0)
    for i in range(width // step):
        for copy in stored(i):
            copy.wait()


def local_call(kernel, name, out_shape, scratch_shapes, flops, operands, in_specs=None, out_specs=VMEM, aliases={}, moved=None):
    outs = out_shape if isinstance(out_shape, list) else [out_shape]
    if moved is None:
        moved = sum(math.prod(x.shape) * x.dtype.itemsize for x in [*operands, *outs])
    return pl.pallas_call(
        kernel,
        out_shape=out_shape,
        in_specs=in_specs or [VMEM] * len(operands),
        out_specs=out_specs,
        scratch_shapes=scratch_shapes,
        input_output_aliases=aliases,
        cost_estimate=pl.CostEstimate(flops=flops, bytes_accessed=moved, transcendentals=0),
        compiler_params=pltpu.CompilerParams(vmem_limit_bytes=24 << 20),
        name=name,
    )(*operands)


def in_hbm(*arrays):
    return [pltpu.with_memory_space_constraint(x, pltpu.HBM) for x in arrays]


def own_call(kernel, name, out_shape, scratch_shapes, hbm_operands, operands, aliases={}):
    return pl.pallas_call(
        kernel,
        out_shape=out_shape,
        in_specs=[pl.BlockSpec(memory_space=pltpu.HBM)] * len(hbm_operands) + [VMEM] * len(operands),
        out_specs=[VMEM] * len(out_shape) if isinstance(out_shape, list) else VMEM,
        scratch_shapes=scratch_shapes,
        input_output_aliases=aliases,
        cost_estimate=pl.CostEstimate(flops=0, bytes_accessed=0, transcendentals=0),
        compiler_params=pltpu.CompilerParams(vmem_limit_bytes=24 << 20),
        name=name,
    )(*in_hbm(*hbm_operands), *operands)


def first(q, k, v, dy, starts, filters):
    rows, width = q.shape
    wide = pltpu.VMEM((rows, width), jnp.bfloat16)
    sent = pltpu.VMEM((rows, width // 2), jnp.bfloat16)
    return own_call(
        first_kernel, "first",
        [wide] * 4 + [sent] * 2 + [
            pltpu.VMEM((2, rows, rows), jnp.float32),
            pltpu.VMEM((6, rows, rows), jnp.float32),
            pltpu.VMEM((2, rows, 2 * rows), jnp.bfloat16),
            pltpu.VMEM((2, *filters.shape), jnp.float32),
        ],
        [
            pltpu.VMEM(starts.shape, starts.dtype), pltpu.VMEM(filters.shape, filters.dtype),
            pltpu.SemaphoreType.DMA((10,)),
        ],
        (q, k, v, dy, starts, filters), (),
    )


def convolution(a, b, pair, far, c, d, masks, taps, outs, backward, half):
    rows, width = a.shape
    steps = width // 2 // LANES // math.gcd(width // 2 // LANES, STEP)
    out = jax.ShapeDtypeStruct((rows, width), jnp.bfloat16)
    part = pltpu.VMEM((rows, width // 2), jnp.bfloat16)
    anywhere = pl.BlockSpec(memory_space=pl.ANY)
    body = functools.partial(conv_kernel, backward=backward, half=half)
    operands = (a, b, pair, far, c, d, masks, taps)
    n = len(operands)
    return local_call(
        body if outs else lambda *refs: body(*refs[:n], None, None, *refs[n:]),
        ("backward" if backward else "forward") + ("_high" if half else "_low"),
        [out, out],
        [part, part, pltpu.SemaphoreType.DMA((2, steps))],
        16 * rows * rows * width,
        operands + tuple(outs or ()),
        [VMEM] * n + [anywhere] * (2 if outs else 0),
        [anywhere] * 2,
        {n: 0, n + 1: 1} if outs else {},
    )


def other_core(block):
    return lax.ppermute(block, "ctx", [(i, i ^ 1) for i in range(lax.axis_size("ctx"))])


def next_chip(block):
    size = lax.axis_size("ctx")
    pairs = [(i, i + 1) for i in range(1, size - 1, 2)]
    return lax.ppermute(block, "ctx", pairs + [(j, i) for i, j in pairs])


def factors(size):
    found, p = [], 2
    while size > 1:
        while size % p == 0:
            found.append(p)
            size //= p
        p += 1
    return found


def rounds_over_chips():
    return [
        (axis, first * math.prod(factors(lax.axis_size(axis) // first)[:n]), p)
        for axis, first in (("dp", 1), ("ctx", 2))
        for n, p in enumerate(factors(lax.axis_size(axis) // first))
    ]


def summed_over(total, axis, stride, p):
    size = lax.axis_size(axis)
    turned = lambda i, k: i + ((i // stride + k) % p - i // stride % p) * stride
    got = [lax.ppermute(total, axis, [(turned(i, k), i) for i in range(size)]) for k in range(1, p)]
    if p == 2:
        return total + got[0]
    digit = lax.axis_index(axis) // stride % p
    return jnp.sum(jnp.roll(jnp.stack([total, *got]), digit, axis=0), axis=0)


def after(value, *others):
    return lax.optimization_barrier((value, *others))[0]


def per_device(q_proj, k_proj, v_proj, out_grad, contig_starts, filters):
    q, k, v, dy = q_proj[0], k_proj[0], v_proj[0], out_grad[0]
    rows = q.shape[0]
    groups, taps = filters.shape
    assert rows == taps == LANES and lax.axis_size("ctx") % 2 == 0
    scale = 1.0 / math.sqrt(rows * lax.axis_size("ctx") * lax.axis_size("dp") * GSIZE)
    inputs = q, k, v, dy
    *partly, far_out, pair_out, keep, masks, table_masks, tap_rows = first(*inputs, contig_starts, filters)
    square = pltpu.VMEM((rows, rows), jnp.float32)
    part = pltpu.VMEM((groups // 2, rows), jnp.float32)
    wide = pltpu.VMEM(q.shape, q.dtype)
    sent = pltpu.VMEM((rows, q.shape[1] // 2), q.dtype)
    far = next_chip(far_out)
    later_pair = other_core(pair_out)
    q, k, v, dy, theirs, pair_out, far_out = own_call(
        functools.partial(filter_partner_kernel, scale=scale), "filter_partner",
        [wide] * 4 + [part, sent, sent], [pltpu.SemaphoreType.DMA((8,))],
        inputs, (*partly, keep, masks), {4: 0, 5: 1, 6: 2, 7: 3},
    )
    pair = other_core(pair_out)
    mine = own_call(
        filter_own_kernel, "filter_own", part, [square, square],
        (), (q, k, v, dy, later_pair, masks),
    )
    later_far = next_chip(after(far_out, mine))
    mine = own_call(
        functools.partial(filter_far_kernel, scale=scale), "filter_far", part, [square],
        (), (q, k, v, dy, far, masks, mine),
    )
    mine = mine + other_core(theirs)

    def forward(pair, far, outs, half):
        return convolution(k, v, pair, far, q, dy, table_masks, tap_rows, outs, False, half)

    def backward(pair, far, outs, half):
        return convolution(dy, q, pair, far, v, k, table_masks, tap_rows, outs, True, half)

    for n, place in enumerate(rounds_over_chips()):
        if n == 0:
            half_forward = forward(pair, far, None, 0)
        if n == 1:
            mine = after(mine, *half_forward)
            half_backward = backward(pair, far, None, 1)
        if n == 2:
            mine = after(mine, *half_backward, later_far, later_pair)
            mixed, grad_q = forward(later_pair, later_far, half_forward, 1)
        if n == 3:
            mine = after(mine, mixed, grad_q)
            grad_k, grad_v = backward(later_pair, later_far, half_backward, 0)
        mine = summed_over(mine, *place)
    mine = after(mine, grad_k, grad_v)
    halves = [mine, other_core(mine)]
    filter_grad = jnp.where(lax.axis_index("ctx") % 2 == 0, jnp.concatenate(halves), jnp.concatenate(halves[::-1]))
    return (mixed[None], grad_q[None], grad_k[None], grad_v[None], filter_grad)


def solution(mesh):
    wide = P("dp", "ctx", None)
    return jax.shard_map(
        per_device,
        mesh=mesh,
        in_specs=(wide,) * 4 + (P("dp", "ctx"), P()),
        out_specs=(wide,) * 4 + (P(),),
        check_vma=False,
    )
```

```python
import functools
import math

import jax
import jax.numpy as jnp
from jax import lax
from jax.experimental import pallas as pl
from jax.experimental.pallas import tpu as pltpu
from jax.sharding import PartitionSpec as P

GSIZE = 16
LANES = 128
STEP = 4
VMEM = pl.BlockSpec(memory_space=pltpu.VMEM)


def product(a, b):
    return a * b


def reversed_taps(rows_of_taps):
    taps = rows_of_taps.shape[1]
    i = lax.broadcasted_iota(jnp.int32, (taps, taps), 0)
    j = lax.broadcasted_iota(jnp.int32, (taps, taps), 1)
    flip = jnp.where((i + j == 0) | (i + j == taps), 1.0, 0.0).astype(jnp.float32)
    return jnp.dot(
        rows_of_taps.astype(jnp.float32), flip,
        preferred_element_type=jnp.float32, precision=lax.Precision.HIGHEST,
    )


def lane_groups():
    return lax.broadcasted_iota(jnp.int32, (1, LANES), 1) // GSIZE


def each_tile(tile, width):
    count = width // LANES
    step = math.gcd(count, STEP)

    def body(i, carry):
        for j in range(step):
            tile(i * step + j)
        return carry

    lax.fori_loop(0, count // step, body, 0)


def half_copies(sources, targets, half, sems):
    rows, width = sources[0].shape
    lanes = pl.ds(pl.multiple_of(half * (width // 2), width // 2), width // 2)
    copies = []
    for n in range(2):
        part = pl.ds(n * (rows // 2), rows // 2)
        for source, target in zip(sources, targets):
            copies.append(
                pltpu.make_async_copy(source.at[part, lanes], target.at[part, lanes], sems.at[len(copies)])
            )
    return copies


def sent_products(inputs, half, keep_ref, kv_out, cot_out, swapped):
    q_ref, k_ref, v_ref, dy_ref = inputs
    width = kv_out.shape[1]
    lanes = pl.ds(pl.multiple_of(half * width, width), width)
    kv = product(k_ref[:, lanes], v_ref[:, lanes])
    cot = product(dy_ref[:, lanes], q_ref[:, lanes])
    kv = jnp.where(keep_ref[1][:, :1] > 0, kv, jnp.zeros_like(kv))
    cot = jnp.where(keep_ref[0][:, :1] > 0, cot, jnp.zeros_like(cot))
    kv_out[...] = jnp.where(swapped, cot, kv)
    cot_out[...] = jnp.where(swapped, kv, cot)


def first_kernel(
    q_hbm, k_hbm, v_hbm, dy_hbm, starts_hbm, filters_hbm,
    q_ref, k_ref, v_ref, dy_ref, far_ref, pair_ref, keep_ref, masks_ref, table_masks_ref, taps_ref,
    starts_ref, filters_ref, sems,
):
    rows = q_ref.shape[0]
    core = lax.axis_index("ctx") % 2
    small = [
        pltpu.make_async_copy(starts_hbm, starts_ref, sems.at[8]),
        pltpu.make_async_copy(filters_hbm, filters_ref, sems.at[9]),
    ]
    inputs = (q_ref, k_ref, v_ref, dy_ref)
    copies = half_copies((q_hbm, k_hbm, v_hbm, dy_hbm), inputs, 1 - core, sems)
    for copy in small + copies:
        copy.start()

    small[0].wait()
    starts = jnp.broadcast_to(starts_ref[...], (rows, rows)) > 0
    t = lax.broadcasted_iota(jnp.int32, (rows, rows), 0)
    s = lax.broadcasted_iota(jnp.int32, (rows, rows), 1)
    began = jnp.max(jnp.where(starts & (s <= t), s, 0), axis=1, keepdims=True)
    first = jnp.min(jnp.where(starts, s, rows), axis=1, keepdims=True)
    last = jnp.max(jnp.where(starts, s, 0), axis=1, keepdims=True)
    as_f32 = lambda mask: jnp.where(mask, 1.0, 0.0).astype(jnp.float32)
    own = as_f32((s <= t) & (s >= began))
    previous = as_f32((s > t) & (t < first))
    following = as_f32((s < t) & (t >= last))
    keep_ref[0] = as_f32(t < first)
    keep_ref[1] = as_f32(t >= last)
    for n, parts in enumerate(((own, previous), (own.T, following))):
        for m, mask in enumerate(parts):
            table_masks_ref[n, :, m * rows : (m + 1) * rows] = mask.astype(jnp.bfloat16)
    for n, mask in enumerate((own, own.T, previous, following, previous.T, following.T)):
        masks_ref[n] = mask
    small[1].wait()
    taps_ref[0] = reversed_taps(filters_ref[...])
    taps_ref[1] = filters_ref[...].astype(jnp.float32)
    for copy in copies:
        copy.wait()
    sent_products(inputs, 1 - core, keep_ref, far_ref, pair_ref, core == 0)


def tile_products(inputs, half, index):
    q_ref, k_ref, v_ref, dy_ref = inputs
    lanes = lanes_of(half, q_ref.shape[1] // 2, index)
    return product(k_ref[:, lanes], v_ref[:, lanes]), product(dy_ref[:, lanes], q_ref[:, lanes])


def wrapped(linked):
    rows = linked.shape[0]
    total = linked[:8]
    for i in range(1, rows // 8):
        total = total + pltpu.roll(linked[8 * i : 8 * i + 8], rows - 8 * i, 1)
    return total


def products(left, right):
    return lax.dot_general(left, right, (((1,), (1,)), ((), ())), preferred_element_type=jnp.float32)


def picked(group, g, *tiles):
    return jnp.concatenate([jnp.where(group == g, tile, jnp.zeros_like(tile)) for tile in tiles], axis=1)


def diagonals(sums_ref, groups):
    rows = sums_ref.shape[1]
    total = sums_ref[pl.ds(0, groups, stride=8), :]
    for r in range(1, 8):
        total = total + pltpu.roll(sums_ref[pl.ds(r, groups, stride=8), :], rows - r, 1)
    return total


def sums_at(index, g):
    return pl.ds(pl.multiple_of((index * (LANES // GSIZE) + g) * 8, 8), 8)


def two_tiles(index, sides, mask_ref, store, group):
    rows = mask_ref.shape[0]
    (left_a, right_a), (left_b, right_b) = sides(index), sides(index + 1)
    zeros = jnp.zeros_like(right_a)
    right = jnp.concatenate(
        [jnp.concatenate([right_a, zeros], axis=1), jnp.concatenate([zeros, right_b], axis=1)], axis=0
    )
    for g in range(LANES // GSIZE):
        pairs = products(picked(group, g, left_a, left_b), right)
        for n in range(2):
            store(sums_at(index + n, g), wrapped(pairs[:, n * rows : (n + 1) * rows] * mask_ref[...]))


def lanes_of(half, width, index):
    return pl.ds(pl.multiple_of(half * width + index * LANES, LANES), LANES)


def filter_partner_kernel(
    q_hbm, k_hbm, v_hbm, dy_hbm, q_in, k_in, v_in, dy_in, keep_ref, masks_ref,
    q_ref, k_ref, v_ref, dy_ref, out_ref, pair_ref, far_ref, sums_ref, sems, *, scale
):
    del q_in, k_in, v_in, dy_in
    core = lax.axis_index("ctx") % 2
    inputs = (q_ref, k_ref, v_ref, dy_ref)
    copies = half_copies((q_hbm, k_hbm, v_hbm, dy_hbm), inputs, core, sems)
    for copy in copies:
        copy.start()
    group = lane_groups()

    def store(at, total):
        sums_ref[at, :] = total

    def tiles(index):
        two_tiles(2 * index, lambda i: tile_products(inputs, 1 - core, i), masks_ref.at[1], store, group)

    each_tile(tiles, q_ref.shape[1] // 4)
    out_ref[...] = diagonals(sums_ref, out_ref.shape[0]) * scale
    for copy in copies:
        copy.wait()
    sent_products(inputs, core, keep_ref, pair_ref, far_ref, core == 1)


def filter_own_kernel(q_ref, k_ref, v_ref, dy_ref, other_ref, masks_ref, sums_ref, own_ref, cross_ref):
    inputs = (q_ref, k_ref, v_ref, dy_ref)
    rows, width = q_ref.shape[0], q_ref.shape[1] // 2
    core = lax.axis_index("ctx") % 2
    even = core == 0
    own_ref[...] = jnp.where(even, masks_ref[1], masks_ref[0])
    cross_ref[...] = jnp.where(even, masks_ref[3], masks_ref[2])
    group = lane_groups()

    def tile(index):
        kv, cot = tile_products(inputs, core, index)
        left = jnp.where(even, kv, cot)
        right = jnp.concatenate([jnp.where(even, cot, kv), other_ref[:, lanes_of(0, width, index)]], axis=0)
        for g in range(LANES // GSIZE):
            pairs = products(picked(group, g, left), right)
            linked = pairs[:, :rows] * own_ref[...] + pairs[:, rows:] * cross_ref[...]
            sums_ref[sums_at(index, g), :] = wrapped(linked)

    each_tile(tile, width)


def filter_far_kernel(q_ref, k_ref, v_ref, dy_ref, other_ref, masks_ref, base_ref, out_ref, total_ref, cross_ref, *, scale):
    inputs = (q_ref, k_ref, v_ref, dy_ref)
    width = q_ref.shape[1] // 2
    core = lax.axis_index("ctx") % 2
    even = core == 0
    cross_ref[...] = jnp.where(even, masks_ref[4], masks_ref[5])
    group = lane_groups()

    def sides(index):
        kv, cot = tile_products(inputs, core, index)
        return other_ref[:, lanes_of(0, width, index)], jnp.where(even, cot, kv)

    def store(at, total):
        total_ref[at, :] = base_ref[at, :] + total

    each_tile(lambda index: two_tiles(2 * index, sides, cross_ref, store, group), width // 2)
    total = diagonals(total_ref, out_ref.shape[0])
    out_ref[...] = jnp.where(even, total, reversed_taps(total)) * scale


def conv_kernel(
    a_ref, b_ref, pair_ref, far_ref, c_ref, d_ref, masks_ref, taps_ref, c_in_hbm, d_in_hbm, out_c_hbm, out_d_hbm,
    out_c_ref, out_d_ref, sems, *, backward, half,
):
    del c_in_hbm, d_in_hbm
    rows = a_ref.shape[0]
    per_tile = LANES // GSIZE
    width = a_ref.shape[1] // 2
    base = half * width
    even = lax.axis_index("ctx") % 2 == 0
    group = lane_groups()
    groups = width // GSIZE
    mask_ref = masks_ref.at[1 if backward else 0]

    def table(row):
        first = pltpu.roll(jnp.broadcast_to(row, (8, rows)), 0, 1, stride=1, stride_axis=0)
        wide = jnp.concatenate([first] + [pltpu.roll(first, 8 * i, 1) for i in range(1, rows // 8)], axis=0)
        wide = wide.astype(jnp.bfloat16)
        return jnp.concatenate([wide, wide], axis=1) * mask_ref[...]

    def tile(index):
        here = pl.ds(pl.multiple_of(index * LANES, LANES), LANES)
        lanes = pl.ds(pl.multiple_of(base + index * LANES, LANES), LANES)
        from_pair = even if backward else jnp.logical_not(even)
        other = jnp.where(from_pair, pair_ref[:, here], far_ref[:, here])
        x = jnp.concatenate([product(a_ref[:, lanes], b_ref[:, lanes]), other], axis=0)
        at = pl.multiple_of(half * groups + index * per_tile, per_tile)
        taps = taps_ref[1 if backward else 0, pl.ds(at, per_tile), :]
        tables = [table(taps[g : g + 1]) for g in range(per_tile)]
        if backward:
            each = [jnp.dot(one, x, preferred_element_type=jnp.float32) for one in tables]
        else:
            every = jnp.dot(jnp.concatenate(tables, axis=0), x, preferred_element_type=jnp.float32)
            each = [every[g * rows : (g + 1) * rows] for g in range(per_tile)]
        y = each[0]
        for g in range(1, per_tile):
            y = jnp.where(group == g, each[g], y)
        out_c_ref[:, here] = (c_ref[:, lanes].astype(jnp.float32) * y).astype(jnp.bfloat16)
        out_d_ref[:, here] = (d_ref[:, lanes].astype(jnp.float32) * y).astype(jnp.bfloat16)

    step = math.gcd(width // LANES, STEP) * LANES

    def stored(i):
        here = pl.ds(pl.multiple_of(i * step, step), step)
        there = pl.ds(pl.multiple_of(base + i * step, step), step)
        return [
            pltpu.make_async_copy(out_c_ref.at[:, here], out_c_hbm.at[:, there], sems.at[0, i]),
            pltpu.make_async_copy(out_d_ref.at[:, here], out_d_hbm.at[:, there], sems.at[1, i]),
        ]

    def body(i, carry):
        for j in range(step // LANES):
            tile(i * (step // LANES) + j)
        for copy in stored(i):
            copy.start()
        return carry

    lax.fori_loop(0, width // step, body, 0)
    for i in range(width // step):
        for copy in stored(i):
            copy.wait()


def local_call(kernel, name, out_shape, scratch_shapes, flops, operands, in_specs=None, out_specs=VMEM, aliases={}, moved=None):
    outs = out_shape if isinstance(out_shape, list) else [out_shape]
    if moved is None:
        moved = sum(math.prod(x.shape) * x.dtype.itemsize for x in [*operands, *outs])
    return pl.pallas_call(
        kernel,
        out_shape=out_shape,
        in_specs=in_specs or [VMEM] * len(operands),
        out_specs=out_specs,
        scratch_shapes=scratch_shapes,
        input_output_aliases=aliases,
        cost_estimate=pl.CostEstimate(flops=flops, bytes_accessed=moved, transcendentals=0),
        compiler_params=pltpu.CompilerParams(vmem_limit_bytes=24 << 20),
        name=name,
    )(*operands)


def in_hbm(*arrays):
    return [pltpu.with_memory_space_constraint(x, pltpu.HBM) for x in arrays]


def own_call(kernel, name, out_shape, scratch_shapes, hbm_operands, operands, aliases={}):
    return pl.pallas_call(
        kernel,
        out_shape=out_shape,
        in_specs=[pl.BlockSpec(memory_space=pltpu.HBM)] * len(hbm_operands) + [VMEM] * len(operands),
        out_specs=[VMEM] * len(out_shape) if isinstance(out_shape, list) else VMEM,
        scratch_shapes=scratch_shapes,
        input_output_aliases=aliases,
        cost_estimate=pl.CostEstimate(flops=0, bytes_accessed=0, transcendentals=0),
        compiler_params=pltpu.CompilerParams(vmem_limit_bytes=24 << 20),
        name=name,
    )(*in_hbm(*hbm_operands), *operands)


def first(q, k, v, dy, starts, filters):
    rows, width = q.shape
    wide = pltpu.VMEM((rows, width), jnp.bfloat16)
    sent = pltpu.VMEM((rows, width // 2), jnp.bfloat16)
    return own_call(
        first_kernel, "first",
        [wide] * 4 + [sent] * 2 + [
            pltpu.VMEM((2, rows, rows), jnp.float32),
            pltpu.VMEM((6, rows, rows), jnp.float32),
            pltpu.VMEM((2, rows, 2 * rows), jnp.bfloat16),
            pltpu.VMEM((2, *filters.shape), jnp.float32),
        ],
        [
            pltpu.VMEM(starts.shape, starts.dtype), pltpu.VMEM(filters.shape, filters.dtype),
            pltpu.SemaphoreType.DMA((10,)),
        ],
        (q, k, v, dy, starts, filters), (),
    )


def convolution(a, b, pair, far, c, d, masks, taps, outs, backward, half):
    rows, width = a.shape
    steps = width // 2 // LANES // math.gcd(width // 2 // LANES, STEP)
    out = jax.ShapeDtypeStruct((rows, width), jnp.bfloat16)
    part = pltpu.VMEM((rows, width // 2), jnp.bfloat16)
    anywhere = pl.BlockSpec(memory_space=pl.ANY)
    body = functools.partial(conv_kernel, backward=backward, half=half)
    operands = (a, b, pair, far, c, d, masks, taps)
    n = len(operands)
    return local_call(
        body if outs else lambda *refs: body(*refs[:n], None, None, *refs[n:]),
        ("backward" if backward else "forward") + ("_high" if half else "_low"),
        [out, out],
        [part, part, pltpu.SemaphoreType.DMA((2, steps))],
        16 * rows * rows * width,
        operands + tuple(outs or ()),
        [VMEM] * n + [anywhere] * (2 if outs else 0),
        [anywhere] * 2,
        {n: 0, n + 1: 1} if outs else {},
    )


def other_core(block):
    return lax.ppermute(block, "ctx", [(i, i ^ 1) for i in range(lax.axis_size("ctx"))])


def next_chip(block):
    size = lax.axis_size("ctx")
    pairs = [(i, i + 1) for i in range(1, size - 1, 2)]
    return lax.ppermute(block, "ctx", pairs + [(j, i) for i, j in pairs])


def factors(size):
    found, p = [], 2
    while size > 1:
        while size % p == 0:
            found.append(p)
            size //= p
        p += 1
    return found


def rounds_over_chips():
    return [
        (axis, first * math.prod(factors(lax.axis_size(axis) // first)[:n]), p)
        for axis, first in (("dp", 1), ("ctx", 2))
        for n, p in enumerate(factors(lax.axis_size(axis) // first))
    ]


def summed_over(total, axis, stride, p):
    size = lax.axis_size(axis)
    turned = lambda i, k: i + ((i // stride + k) % p - i // stride % p) * stride
    got = [lax.ppermute(total, axis, [(turned(i, k), i) for i in range(size)]) for k in range(1, p)]
    if p == 2:
        return total + got[0]
    digit = lax.axis_index(axis) // stride % p
    return jnp.sum(jnp.roll(jnp.stack([total, *got]), digit, axis=0), axis=0)


def after(value, *others):
    return lax.optimization_barrier((value, *others))[0]


def per_device(q_proj, k_proj, v_proj, out_grad, contig_starts, filters):
    q, k, v, dy = q_proj[0], k_proj[0], v_proj[0], out_grad[0]
    rows = q.shape[0]
    groups, taps = filters.shape
    assert rows == taps == LANES and lax.axis_size("ctx") % 2 == 0
    scale = 1.0 / math.sqrt(rows * lax.axis_size("ctx") * lax.axis_size("dp") * GSIZE)
    inputs = q, k, v, dy
    *partly, far_out, pair_out, keep, masks, table_masks, tap_rows = first(*inputs, contig_starts, filters)
    square = pltpu.VMEM((rows, rows), jnp.float32)
    part = pltpu.VMEM((groups // 2, rows), jnp.float32)
    unsummed = pltpu.VMEM((groups * 4, rows), jnp.float32)
    wide = pltpu.VMEM(q.shape, q.dtype)
    sent = pltpu.VMEM((rows, q.shape[1] // 2), q.dtype)
    far = next_chip(far_out)
    later_pair = other_core(pair_out)
    q, k, v, dy, theirs, pair_out, far_out = own_call(
        functools.partial(filter_partner_kernel, scale=scale), "filter_partner",
        [wide] * 4 + [part, sent, sent], [unsummed, pltpu.SemaphoreType.DMA((8,))],
        inputs, (*partly, keep, masks), {4: 0, 5: 1, 6: 2, 7: 3},
    )
    pair = other_core(pair_out)
    mine = own_call(
        filter_own_kernel, "filter_own", unsummed, [square, square],
        (), (q, k, v, dy, later_pair, masks),
    )
    later_far = next_chip(after(far_out, mine))
    mine = own_call(
        functools.partial(filter_far_kernel, scale=scale), "filter_far", part, [unsummed, square],
        (), (q, k, v, dy, far, masks, mine),
    )
    mine = mine + other_core(theirs)

    def forward(pair, far, outs, half):
        return convolution(k, v, pair, far, q, dy, table_masks, tap_rows, outs, False, half)

    def backward(pair, far, outs, half):
        return convolution(dy, q, pair, far, v, k, table_masks, tap_rows, outs, True, half)

    for n, place in enumerate(rounds_over_chips()):
        if n == 0:
            half_forward = forward(pair, far, None, 0)
        if n == 1:
            mine = after(mine, *half_forward)
            half_backward = backward(pair, far, None, 1)
        if n == 2:
            mine = after(mine, *half_backward, later_far, later_pair)
            mixed, grad_q = forward(later_pair, later_far, half_forward, 1)
        if n == 3:
            mine = after(mine, mixed, grad_q)
            grad_k, grad_v = backward(later_pair, later_far, half_backward, 0)
        mine = summed_over(mine, *place)
    mine = after(mine, grad_k, grad_v)
    halves = [mine, other_core(mine)]
    filter_grad = jnp.where(lax.axis_index("ctx") % 2 == 0, jnp.concatenate(halves), jnp.concatenate(halves[::-1]))
    return (mixed[None], grad_q[None], grad_k[None], grad_v[None], filter_grad)


def solution(mesh):
    wide = P("dp", "ctx", None)
    return jax.shard_map(
        per_device,
        mesh=mesh,
        in_specs=(wide,) * 4 + (P("dp", "ctx"), P()),
        out_specs=(wide,) * 4 + (P(),),
        check_vma=False,
    )
```

```python
import functools
import math

import jax
import jax.numpy as jnp
from jax import lax
from jax.experimental import pallas as pl
from jax.experimental.pallas import tpu as pltpu
from jax.sharding import PartitionSpec as P

GSIZE = 16
LANES = 128
BLOCK = 16
STEP = 4
VMEM = pl.BlockSpec(memory_space=pltpu.VMEM)


def product(a, b):
    return a * b


def reversed_taps(rows_of_taps):
    taps = rows_of_taps.shape[1]
    i = lax.broadcasted_iota(jnp.int32, (taps, taps), 0)
    j = lax.broadcasted_iota(jnp.int32, (taps, taps), 1)
    flip = jnp.where((i + j == 0) | (i + j == taps), 1.0, 0.0).astype(jnp.float32)
    return jnp.dot(
        rows_of_taps.astype(jnp.float32), flip,
        preferred_element_type=jnp.float32, precision=lax.Precision.HIGHEST,
    )


def lane_groups():
    return lax.broadcasted_iota(jnp.int32, (1, LANES), 1) // GSIZE


def each_tile(tile, width):
    count = width // LANES
    step = math.gcd(count, STEP)

    def body(i, carry):
        for j in range(step):
            tile(i * step + j)
        return carry

    lax.fori_loop(0, count // step, body, 0)


def aligned(mask):
    rows = mask.shape[0]
    blocks = [mask[at : at + BLOCK] for at in range(0, rows, BLOCK)]
    return jnp.concatenate(
        blocks[:1] + [pltpu.roll(block, rows - BLOCK * (i + 1), 1) for i, block in enumerate(blocks[1:])], axis=0
    )


def turned(tile, at):
    return jnp.concatenate([tile[at:], tile[:at]], axis=0) if at else tile


def for_groups(block):
    return jnp.concatenate([block] * (LANES // GSIZE), axis=0)


def half_copies(sources, targets, half, sems):
    rows, width = sources[0].shape
    lanes = pl.ds(pl.multiple_of(half * (width // 2), width // 2), width // 2)
    copies = []
    for n in range(2):
        part = pl.ds(n * (rows // 2), rows // 2)
        for source, target in zip(sources, targets):
            copies.append(
                pltpu.make_async_copy(source.at[part, lanes], target.at[part, lanes], sems.at[len(copies)])
            )
    return copies


def sent_products(inputs, half, keep_ref, kv_out, cot_out, swapped):
    q_ref, k_ref, v_ref, dy_ref = inputs
    width = kv_out.shape[1]
    lanes = pl.ds(pl.multiple_of(half * width, width), width)
    kv = product(k_ref[:, lanes], v_ref[:, lanes])
    cot = product(dy_ref[:, lanes], q_ref[:, lanes])
    kv = jnp.where(keep_ref[1][:, :1] > 0, kv, jnp.zeros_like(kv))
    cot = jnp.where(keep_ref[0][:, :1] > 0, cot, jnp.zeros_like(cot))
    kv_out[...] = jnp.where(swapped, cot, kv)
    cot_out[...] = jnp.where(swapped, kv, cot)


def first_kernel(
    q_hbm, k_hbm, v_hbm, dy_hbm, starts_hbm, filters_hbm,
    q_ref, k_ref, v_ref, dy_ref, far_ref, pair_ref, keep_ref, masks_ref, table_masks_ref, taps_ref,
    starts_ref, filters_ref, sems,
):
    rows = q_ref.shape[0]
    core = lax.axis_index("ctx") % 2
    small = [
        pltpu.make_async_copy(starts_hbm, starts_ref, sems.at[8]),
        pltpu.make_async_copy(filters_hbm, filters_ref, sems.at[9]),
    ]
    inputs = (q_ref, k_ref, v_ref, dy_ref)
    copies = half_copies((q_hbm, k_hbm, v_hbm, dy_hbm), inputs, 1 - core, sems)
    for copy in small + copies:
        copy.start()

    small[0].wait()
    starts = jnp.broadcast_to(starts_ref[...], (rows, rows)) > 0
    t = lax.broadcasted_iota(jnp.int32, (rows, rows), 0)
    s = lax.broadcasted_iota(jnp.int32, (rows, rows), 1)
    began = jnp.max(jnp.where(starts & (s <= t), s, 0), axis=1, keepdims=True)
    first = jnp.min(jnp.where(starts, s, rows), axis=1, keepdims=True)
    last = jnp.max(jnp.where(starts, s, 0), axis=1, keepdims=True)
    as_f32 = lambda mask: jnp.where(mask, 1.0, 0.0).astype(jnp.float32)
    own = as_f32((s <= t) & (s >= began))
    previous = as_f32((s > t) & (t < first))
    following = as_f32((s < t) & (t >= last))
    keep_ref[0] = as_f32(t < first)
    keep_ref[1] = as_f32(t >= last)
    for n, parts in enumerate(((own, previous), (own.T, following))):
        for m, mask in enumerate(parts):
            table_masks_ref[n, :, m * rows : (m + 1) * rows] = aligned(mask).astype(jnp.bfloat16)
    for n, mask in enumerate((own, own.T, previous, following, previous.T, following.T)):
        masks_ref[n] = aligned(mask)
    small[1].wait()
    taps_ref[0] = reversed_taps(filters_ref[...])
    taps_ref[1] = filters_ref[...].astype(jnp.float32)
    for copy in copies:
        copy.wait()
    sent_products(inputs, 1 - core, keep_ref, far_ref, pair_ref, core == 0)


def tile_products(inputs, half, index):
    q_ref, k_ref, v_ref, dy_ref = inputs
    lanes = lanes_of(half, q_ref.shape[1] // 2, index)
    return product(k_ref[:, lanes], v_ref[:, lanes]), product(dy_ref[:, lanes], q_ref[:, lanes])


def wrapped_products(left, rights, masks, group):
    rows = left[0].shape[0]
    zeros = jnp.zeros_like(left[0])
    totals = [None] * len(masks)
    for at in range(0, rows, BLOCK):
        picked = jnp.concatenate(
            [
                jnp.concatenate([jnp.where(group == g, tile[at : at + BLOCK], zeros[:BLOCK]) for tile in left], axis=1)
                for g in range(LANES // GSIZE)
            ],
            axis=0,
        )
        right = jnp.concatenate(
            [
                jnp.concatenate([zeros if tile is None else turned(tile, at) for tile in tiles], axis=1)
                for tiles in rights
            ],
            axis=0,
        )
        pairs = lax.dot_general(picked, right, (((1,), (1,)), ((), ())), preferred_element_type=jnp.float32)
        for n, columns in enumerate(masks):
            for column, mask_ref in columns:
                piece = pairs[:, column * rows : (column + 1) * rows] * for_groups(mask_ref[at : at + BLOCK, :])
                totals[n] = piece if totals[n] is None else totals[n] + piece
    for total in totals:
        yield jnp.concatenate(
            [
                total[at : at + 8] + pltpu.roll(total[at + 8 : at + 16], rows - 8, 1)
                for at in range(0, total.shape[0], BLOCK)
            ],
            axis=0,
        )


def diagonals(sums_ref, groups):
    rows = sums_ref.shape[1]
    total = sums_ref[pl.ds(0, groups, stride=8), :]
    for r in range(1, 8):
        total = total + pltpu.roll(sums_ref[pl.ds(r, groups, stride=8), :], rows - r, 1)
    return total


def sums_at(index):
    count = LANES // GSIZE * 8
    return pl.ds(pl.multiple_of(index * count, count), count)


def two_tiles(index, sides, mask_ref, store, group):
    (left_a, right_a), (left_b, right_b) = sides(index), sides(index + 1)
    masks = [[(0, mask_ref)], [(1, mask_ref)]]
    rights = [[right_a, None], [None, right_b]]
    for n, total in enumerate(wrapped_products([left_a, left_b], rights, masks, group)):
        store(sums_at(index + n), total)


def lanes_of(half, width, index):
    return pl.ds(pl.multiple_of(half * width + index * LANES, LANES), LANES)


def filter_partner_kernel(
    q_hbm, k_hbm, v_hbm, dy_hbm, q_in, k_in, v_in, dy_in, keep_ref, masks_ref,
    q_ref, k_ref, v_ref, dy_ref, out_ref, pair_ref, far_ref, sums_ref, sems, *, scale
):
    del q_in, k_in, v_in, dy_in
    core = lax.axis_index("ctx") % 2
    inputs = (q_ref, k_ref, v_ref, dy_ref)
    copies = half_copies((q_hbm, k_hbm, v_hbm, dy_hbm), inputs, core, sems)
    for copy in copies:
        copy.start()
    group = lane_groups()

    def store(at, total):
        sums_ref[at, :] = total

    def tiles(index):
        two_tiles(2 * index, lambda i: tile_products(inputs, 1 - core, i), masks_ref.at[1], store, group)

    each_tile(tiles, q_ref.shape[1] // 4)
    out_ref[...] = diagonals(sums_ref, out_ref.shape[0]) * scale
    for copy in copies:
        copy.wait()
    sent_products(inputs, core, keep_ref, pair_ref, far_ref, core == 1)


def filter_own_kernel(q_ref, k_ref, v_ref, dy_ref, other_ref, masks_ref, sums_ref, own_ref, cross_ref):
    inputs = (q_ref, k_ref, v_ref, dy_ref)
    width = q_ref.shape[1] // 2
    core = lax.axis_index("ctx") % 2
    even = core == 0
    own_ref[...] = jnp.where(even, masks_ref[1], masks_ref[0])
    cross_ref[...] = jnp.where(even, masks_ref[3], masks_ref[2])
    group = lane_groups()

    def tile(index):
        kv, cot = tile_products(inputs, core, index)
        left = jnp.where(even, kv, cot)
        rights = [[jnp.where(even, cot, kv)], [other_ref[:, lanes_of(0, width, index)]]]
        for total in wrapped_products([left], rights, [[(0, own_ref), (1, cross_ref)]], group):
            sums_ref[sums_at(index), :] = total

    each_tile(tile, width)


def filter_far_kernel(q_ref, k_ref, v_ref, dy_ref, other_ref, masks_ref, base_ref, out_ref, total_ref, cross_ref, *, scale):
    inputs = (q_ref, k_ref, v_ref, dy_ref)
    width = q_ref.shape[1] // 2
    core = lax.axis_index("ctx") % 2
    even = core == 0
    cross_ref[...] = jnp.where(even, masks_ref[4], masks_ref[5])
    group = lane_groups()

    def sides(index):
        kv, cot = tile_products(inputs, core, index)
        return other_ref[:, lanes_of(0, width, index)], jnp.where(even, cot, kv)

    def store(at, total):
        total_ref[at, :] = base_ref[at, :] + total

    each_tile(lambda index: two_tiles(2 * index, sides, cross_ref, store, group), width // 2)
    total = diagonals(total_ref, out_ref.shape[0])
    out_ref[...] = jnp.where(even, total, reversed_taps(total)) * scale


def conv_kernel(
    a_ref, b_ref, pair_ref, far_ref, c_ref, d_ref, masks_ref, taps_ref, c_in_hbm, d_in_hbm, out_c_hbm, out_d_hbm,
    out_c_ref, out_d_ref, sems, *, backward, half,
):
    del c_in_hbm, d_in_hbm
    rows = a_ref.shape[0]
    per_tile = LANES // GSIZE
    width = a_ref.shape[1] // 2
    base = half * width
    even = lax.axis_index("ctx") % 2 == 0
    group = lane_groups()
    groups = width // GSIZE
    mask_ref = masks_ref.at[1 if backward else 0]

    def table_start(row):
        start = pltpu.roll(jnp.broadcast_to(row, (BLOCK, rows)), 0, 1, stride=1, stride_axis=0).astype(jnp.bfloat16)
        return jnp.concatenate([start, start], axis=1)

    def tile(index):
        here = pl.ds(pl.multiple_of(index * LANES, LANES), LANES)
        lanes = pl.ds(pl.multiple_of(base + index * LANES, LANES), LANES)
        from_pair = even if backward else jnp.logical_not(even)
        own = product(a_ref[:, lanes], b_ref[:, lanes])
        other = jnp.where(from_pair, pair_ref[:, here], far_ref[:, here])
        at = pl.multiple_of(half * groups + index * per_tile, per_tile)
        taps = taps_ref[1 if backward else 0, pl.ds(at, per_tile), :]
        tables = jnp.concatenate([table_start(taps[g : g + 1]) for g in range(per_tile)], axis=0)
        for at in range(0, rows, BLOCK):
            x = jnp.concatenate([turned(own, at), turned(other, at)], axis=0)
            masked = tables * for_groups(mask_ref[at : at + BLOCK, :])
            every = jnp.dot(masked, x, preferred_element_type=jnp.float32)
            y = every[:BLOCK]
            for g in range(1, per_tile):
                y = jnp.where(group == g, every[g * BLOCK : (g + 1) * BLOCK], y)
            block = slice(at, at + BLOCK)
            out_c_ref[block, here] = (c_ref[block, lanes].astype(jnp.float32) * y).astype(jnp.bfloat16)
            out_d_ref[block, here] = (d_ref[block, lanes].astype(jnp.float32) * y).astype(jnp.bfloat16)

    step = math.gcd(width // LANES, STEP) * LANES

    def stored(i):
        here = pl.ds(pl.multiple_of(i * step, step), step)
        there = pl.ds(pl.multiple_of(base + i * step, step), step)
        return [
            pltpu.make_async_copy(out_c_ref.at[:, here], out_c_hbm.at[:, there], sems.at[0, i]),
            pltpu.make_async_copy(out_d_ref.at[:, here], out_d_hbm.at[:, there], sems.at[1, i]),
        ]

    def body(i, carry):
        for j in range(step // LANES):
            tile(i * (step // LANES) + j)
        for copy in stored(i):
            copy.start()
        return carry

    lax.fori_loop(0, width // step, body, 0)
    for i in range(width // step):
        for copy in stored(i):
            copy.wait()


def local_call(kernel, name, out_shape, scratch_shapes, flops, operands, in_specs=None, out_specs=VMEM, aliases={}, moved=None):
    outs = out_shape if isinstance(out_shape, list) else [out_shape]
    if moved is None:
        moved = sum(math.prod(x.shape) * x.dtype.itemsize for x in [*operands, *outs])
    return pl.pallas_call(
        kernel,
        out_shape=out_shape,
        in_specs=in_specs or [VMEM] * len(operands),
        out_specs=out_specs,
        scratch_shapes=scratch_shapes,
        input_output_aliases=aliases,
        cost_estimate=pl.CostEstimate(flops=flops, bytes_accessed=moved, transcendentals=0),
        compiler_params=pltpu.CompilerParams(vmem_limit_bytes=24 << 20),
        name=name,
    )(*operands)


def in_hbm(*arrays):
    return [pltpu.with_memory_space_constraint(x, pltpu.HBM) for x in arrays]


def own_call(kernel, name, out_shape, scratch_shapes, hbm_operands, operands, aliases={}):
    return pl.pallas_call(
        kernel,
        out_shape=out_shape,
        in_specs=[pl.BlockSpec(memory_space=pltpu.HBM)] * len(hbm_operands) + [VMEM] * len(operands),
        out_specs=[VMEM] * len(out_shape) if isinstance(out_shape, list) else VMEM,
        scratch_shapes=scratch_shapes,
        input_output_aliases=aliases,
        cost_estimate=pl.CostEstimate(flops=0, bytes_accessed=0, transcendentals=0),
        compiler_params=pltpu.CompilerParams(vmem_limit_bytes=24 << 20),
        name=name,
    )(*in_hbm(*hbm_operands), *operands)


def first(q, k, v, dy, starts, filters):
    rows, width = q.shape
    wide = pltpu.VMEM((rows, width), jnp.bfloat16)
    sent = pltpu.VMEM((rows, width // 2), jnp.bfloat16)
    return own_call(
        first_kernel, "first",
        [wide] * 4 + [sent] * 2 + [
            pltpu.VMEM((2, rows, rows), jnp.float32),
            pltpu.VMEM((6, rows, rows), jnp.float32),
            pltpu.VMEM((2, rows, 2 * rows), jnp.bfloat16),
            pltpu.VMEM((2, *filters.shape), jnp.float32),
        ],
        [
            pltpu.VMEM(starts.shape, starts.dtype), pltpu.VMEM(filters.shape, filters.dtype),
            pltpu.SemaphoreType.DMA((10,)),
        ],
        (q, k, v, dy, starts, filters), (),
    )


def convolution(a, b, pair, far, c, d, masks, taps, outs, backward, half):
    rows, width = a.shape
    steps = width // 2 // LANES // math.gcd(width // 2 // LANES, STEP)
    out = jax.ShapeDtypeStruct((rows, width), jnp.bfloat16)
    part = pltpu.VMEM((rows, width // 2), jnp.bfloat16)
    anywhere = pl.BlockSpec(memory_space=pl.ANY)
    body = functools.partial(conv_kernel, backward=backward, half=half)
    operands = (a, b, pair, far, c, d, masks, taps)
    n = len(operands)
    return local_call(
        body if outs else lambda *refs: body(*refs[:n], None, None, *refs[n:]),
        ("backward" if backward else "forward") + ("_high" if half else "_low"),
        [out, out],
        [part, part, pltpu.SemaphoreType.DMA((2, steps))],
        16 * rows * rows * width,
        operands + tuple(outs or ()),
        [VMEM] * n + [anywhere] * (2 if outs else 0),
        [anywhere] * 2,
        {n: 0, n + 1: 1} if outs else {},
    )


def other_core(block):
    return lax.ppermute(block, "ctx", [(i, i ^ 1) for i in range(lax.axis_size("ctx"))])


def next_chip(block):
    size = lax.axis_size("ctx")
    pairs = [(i, i + 1) for i in range(1, size - 1, 2)]
    return lax.ppermute(block, "ctx", pairs + [(j, i) for i, j in pairs])


def factors(size):
    found, p = [], 2
    while size > 1:
        while size % p == 0:
            found.append(p)
            size //= p
        p += 1
    return found


def rounds_over_chips():
    return [
        (axis, first * math.prod(factors(lax.axis_size(axis) // first)[:n]), p)
        for axis, first in (("dp", 1), ("ctx", 2))
        for n, p in enumerate(factors(lax.axis_size(axis) // first))
    ]


def summed_over(total, axis, stride, p):
    size = lax.axis_size(axis)
    turned = lambda i, k: i + ((i // stride + k) % p - i // stride % p) * stride
    got = [lax.ppermute(total, axis, [(turned(i, k), i) for i in range(size)]) for k in range(1, p)]
    if p == 2:
        return total + got[0]
    digit = lax.axis_index(axis) // stride % p
    return jnp.sum(jnp.roll(jnp.stack([total, *got]), digit, axis=0), axis=0)


def after(value, *others):
    return lax.optimization_barrier((value, *others))[0]


def per_device(q_proj, k_proj, v_proj, out_grad, contig_starts, filters):
    q, k, v, dy = q_proj[0], k_proj[0], v_proj[0], out_grad[0]
    rows = q.shape[0]
    groups, taps = filters.shape
    assert rows == taps == LANES and lax.axis_size("ctx") % 2 == 0
    scale = 1.0 / math.sqrt(rows * lax.axis_size("ctx") * lax.axis_size("dp") * GSIZE)
    inputs = q, k, v, dy
    *partly, far_out, pair_out, keep, masks, table_masks, tap_rows = first(*inputs, contig_starts, filters)
    square = pltpu.VMEM((rows, rows), jnp.float32)
    part = pltpu.VMEM((groups // 2, rows), jnp.float32)
    unsummed = pltpu.VMEM((groups * 4, rows), jnp.float32)
    wide = pltpu.VMEM(q.shape, q.dtype)
    sent = pltpu.VMEM((rows, q.shape[1] // 2), q.dtype)
    far = next_chip(far_out)
    later_pair = other_core(pair_out)
    q, k, v, dy, theirs, pair_out, far_out = own_call(
        functools.partial(filter_partner_kernel, scale=scale), "filter_partner",
        [wide] * 4 + [part, sent, sent], [unsummed, pltpu.SemaphoreType.DMA((8,))],
        inputs, (*partly, keep, masks), {4: 0, 5: 1, 6: 2, 7: 3},
    )
    pair = other_core(pair_out)
    mine = own_call(
        filter_own_kernel, "filter_own", unsummed, [square, square],
        (), (q, k, v, dy, later_pair, masks),
    )
    later_far = next_chip(after(far_out, mine))
    mine = own_call(
        functools.partial(filter_far_kernel, scale=scale), "filter_far", part, [unsummed, square],
        (), (q, k, v, dy, far, masks, mine),
    )
    mine = mine + other_core(theirs)

    def forward(pair, far, outs, half):
        return convolution(k, v, pair, far, q, dy, table_masks, tap_rows, outs, False, half)

    def backward(pair, far, outs, half):
        return convolution(dy, q, pair, far, v, k, table_masks, tap_rows, outs, True, half)

    for n, place in enumerate(rounds_over_chips()):
        if n == 0:
            half_forward = forward(pair, far, None, 0)
        if n == 1:
            mine = after(mine, *half_forward)
            half_backward = backward(pair, far, None, 1)
        if n == 2:
            mine = after(mine, *half_backward, later_far, later_pair)
            mixed, grad_q = forward(later_pair, later_far, half_forward, 1)
        if n == 3:
            mine = after(mine, mixed, grad_q)
            grad_k, grad_v = backward(later_pair, later_far, half_backward, 0)
        mine = summed_over(mine, *place)
    mine = after(mine, grad_k, grad_v)
    halves = [mine, other_core(mine)]
    filter_grad = jnp.where(lax.axis_index("ctx") % 2 == 0, jnp.concatenate(halves), jnp.concatenate(halves[::-1]))
    return (mixed[None], grad_q[None], grad_k[None], grad_v[None], filter_grad)


def solution(mesh):
    wide = P("dp", "ctx", None)
    return jax.shard_map(
        per_device,
        mesh=mesh,
        in_specs=(wide,) * 4 + (P("dp", "ctx"), P()),
        out_specs=(wide,) * 4 + (P(),),
        check_vma=False,
    )
```

```python
import functools
import math

import jax
import jax.numpy as jnp
from jax import lax
from jax.experimental import pallas as pl
from jax.experimental.pallas import tpu as pltpu
from jax.sharding import PartitionSpec as P

GSIZE = 16
LANES = 128
BLOCK = 16
STEP = 2
VMEM = pl.BlockSpec(memory_space=pltpu.VMEM)


def product(a, b):
    return a * b


def reversed_taps(rows_of_taps):
    taps = rows_of_taps.shape[1]
    i = lax.broadcasted_iota(jnp.int32, (taps, taps), 0)
    j = lax.broadcasted_iota(jnp.int32, (taps, taps), 1)
    flip = jnp.where((i + j == 0) | (i + j == taps), 1.0, 0.0).astype(jnp.float32)
    return jnp.dot(
        rows_of_taps.astype(jnp.float32), flip,
        preferred_element_type=jnp.float32, precision=lax.Precision.HIGHEST,
    )


def lane_groups():
    return lax.broadcasted_iota(jnp.int32, (1, LANES), 1) // GSIZE


def each_tile(tile, width):
    count = width // LANES
    step = math.gcd(count, STEP)

    def body(i, carry):
        for j in range(step):
            tile(i * step + j)
        return carry

    lax.fori_loop(0, count // step, body, 0)


def aligned(mask):
    rows = mask.shape[0]
    blocks = [mask[at : at + BLOCK] for at in range(0, rows, BLOCK)]
    return jnp.concatenate(
        blocks[:1] + [pltpu.roll(block, rows - BLOCK * (i + 1), 1) for i, block in enumerate(blocks[1:])], axis=0
    )


def turned(tile, at):
    return jnp.concatenate([tile[at:], tile[:at]], axis=0) if at else tile


def for_groups(block):
    return jnp.concatenate([block] * (LANES // GSIZE), axis=0)


def half_copies(sources, targets, half, sems):
    rows, width = sources[0].shape
    lanes = pl.ds(pl.multiple_of(half * (width // 2), width // 2), width // 2)
    copies = []
    for n in range(2):
        part = pl.ds(n * (rows // 2), rows // 2)
        for source, target in zip(sources, targets):
            copies.append(
                pltpu.make_async_copy(source.at[part, lanes], target.at[part, lanes], sems.at[len(copies)])
            )
    return copies


def sent_products(inputs, half, keep_ref, kv_out, cot_out, swapped):
    q_ref, k_ref, v_ref, dy_ref = inputs
    width = kv_out.shape[1]
    lanes = pl.ds(pl.multiple_of(half * width, width), width)
    kv = product(k_ref[:, lanes], v_ref[:, lanes])
    cot = product(dy_ref[:, lanes], q_ref[:, lanes])
    kv = jnp.where(keep_ref[1][:, :1] > 0, kv, jnp.zeros_like(kv))
    cot = jnp.where(keep_ref[0][:, :1] > 0, cot, jnp.zeros_like(cot))
    kv_out[...] = jnp.where(swapped, cot, kv)
    cot_out[...] = jnp.where(swapped, kv, cot)


def first_kernel(
    q_hbm, k_hbm, v_hbm, dy_hbm, starts_hbm, filters_hbm,
    q_ref, k_ref, v_ref, dy_ref, far_ref, pair_ref, keep_ref, masks_ref, table_masks_ref, taps_ref,
    starts_ref, filters_ref, sems,
):
    rows = q_ref.shape[0]
    core = lax.axis_index("ctx") % 2
    small = [
        pltpu.make_async_copy(starts_hbm, starts_ref, sems.at[8]),
        pltpu.make_async_copy(filters_hbm, filters_ref, sems.at[9]),
    ]
    inputs = (q_ref, k_ref, v_ref, dy_ref)
    copies = half_copies((q_hbm, k_hbm, v_hbm, dy_hbm), inputs, 1 - core, sems)
    for copy in small + copies:
        copy.start()

    small[0].wait()
    starts = jnp.broadcast_to(starts_ref[...], (rows, rows)) > 0
    t = lax.broadcasted_iota(jnp.int32, (rows, rows), 0)
    s = lax.broadcasted_iota(jnp.int32, (rows, rows), 1)
    began = jnp.max(jnp.where(starts & (s <= t), s, 0), axis=1, keepdims=True)
    first = jnp.min(jnp.where(starts, s, rows), axis=1, keepdims=True)
    last = jnp.max(jnp.where(starts, s, 0), axis=1, keepdims=True)
    as_f32 = lambda mask: jnp.where(mask, 1.0, 0.0).astype(jnp.float32)
    own = as_f32((s <= t) & (s >= began))
    previous = as_f32((s > t) & (t < first))
    following = as_f32((s < t) & (t >= last))
    keep_ref[0] = as_f32(t < first)
    keep_ref[1] = as_f32(t >= last)
    for n, parts in enumerate(((own, previous), (own.T, following))):
        for m, mask in enumerate(parts):
            table_masks_ref[n, :, m * rows : (m + 1) * rows] = aligned(mask).astype(jnp.bfloat16)
    for n, mask in enumerate((own, own.T, previous, following, previous.T, following.T)):
        masks_ref[n] = aligned(mask)
    small[1].wait()
    taps_ref[0] = reversed_taps(filters_ref[...])
    taps_ref[1] = filters_ref[...].astype(jnp.float32)
    for copy in copies:
        copy.wait()
    sent_products(inputs, 1 - core, keep_ref, far_ref, pair_ref, core == 0)


def tile_products(inputs, half, index):
    q_ref, k_ref, v_ref, dy_ref = inputs
    lanes = lanes_of(half, q_ref.shape[1] // 2, index)
    return product(k_ref[:, lanes], v_ref[:, lanes]), product(dy_ref[:, lanes], q_ref[:, lanes])


def wrapped_products(left, rights, masks, group):
    rows = left[0].shape[0]
    zeros = jnp.zeros_like(left[0])
    totals = [None] * len(masks)
    for at in range(0, rows, BLOCK):
        picked = jnp.concatenate(
            [
                jnp.concatenate([jnp.where(group == g, tile[at : at + BLOCK], zeros[:BLOCK]) for tile in left], axis=1)
                for g in range(LANES // GSIZE)
            ],
            axis=0,
        )
        right = jnp.concatenate(
            [
                jnp.concatenate([zeros if tile is None else turned(tile, at) for tile in tiles], axis=1)
                for tiles in rights
            ],
            axis=0,
        )
        pairs = lax.dot_general(picked, right, (((1,), (1,)), ((), ())), preferred_element_type=jnp.float32)
        for n, columns in enumerate(masks):
            for column, mask_ref in columns:
                piece = pairs[:, column * rows : (column + 1) * rows] * for_groups(mask_ref[at : at + BLOCK, :])
                totals[n] = piece if totals[n] is None else totals[n] + piece
    for total in totals:
        yield jnp.concatenate(
            [
                total[at : at + 8] + pltpu.roll(total[at + 8 : at + 16], rows - 8, 1)
                for at in range(0, total.shape[0], BLOCK)
            ],
            axis=0,
        )


def diagonals(sums_ref, groups):
    rows = sums_ref.shape[1]
    total = sums_ref[pl.ds(0, groups, stride=8), :]
    for r in range(1, 8):
        total = total + pltpu.roll(sums_ref[pl.ds(r, groups, stride=8), :], rows - r, 1)
    return total


def sums_at(index):
    count = LANES // GSIZE * 8
    return pl.ds(pl.multiple_of(index * count, count), count)


def two_tiles(index, sides, mask_ref, store, group):
    (left_a, right_a), (left_b, right_b) = sides(index), sides(index + 1)
    masks = [[(0, mask_ref)], [(1, mask_ref)]]
    rights = [[right_a, None], [None, right_b]]
    for n, total in enumerate(wrapped_products([left_a, left_b], rights, masks, group)):
        store(sums_at(index + n), total)


def lanes_of(half, width, index):
    return pl.ds(pl.multiple_of(half * width + index * LANES, LANES), LANES)


def filter_partner_kernel(
    q_hbm, k_hbm, v_hbm, dy_hbm, q_in, k_in, v_in, dy_in, keep_ref, masks_ref,
    q_ref, k_ref, v_ref, dy_ref, out_ref, pair_ref, far_ref, sums_ref, sems, *, scale
):
    del q_in, k_in, v_in, dy_in
    core = lax.axis_index("ctx") % 2
    inputs = (q_ref, k_ref, v_ref, dy_ref)
    copies = half_copies((q_hbm, k_hbm, v_hbm, dy_hbm), inputs, core, sems)
    for copy in copies:
        copy.start()
    group = lane_groups()

    def store(at, total):
        sums_ref[at, :] = total

    def tiles(index):
        two_tiles(2 * index, lambda i: tile_products(inputs, 1 - core, i), masks_ref.at[1], store, group)

    each_tile(tiles, q_ref.shape[1] // 4)
    out_ref[...] = diagonals(sums_ref, out_ref.shape[0]) * scale
    for copy in copies:
        copy.wait()
    sent_products(inputs, core, keep_ref, pair_ref, far_ref, core == 1)


def filter_own_kernel(q_ref, k_ref, v_ref, dy_ref, other_ref, masks_ref, sums_ref, own_ref, cross_ref):
    inputs = (q_ref, k_ref, v_ref, dy_ref)
    width = q_ref.shape[1] // 2
    core = lax.axis_index("ctx") % 2
    even = core == 0
    own_ref[...] = jnp.where(even, masks_ref[1], masks_ref[0])
    cross_ref[...] = jnp.where(even, masks_ref[3], masks_ref[2])
    group = lane_groups()

    def tile(index):
        kv, cot = tile_products(inputs, core, index)
        left = jnp.where(even, kv, cot)
        rights = [[jnp.where(even, cot, kv)], [other_ref[:, lanes_of(0, width, index)]]]
        for total in wrapped_products([left], rights, [[(0, own_ref), (1, cross_ref)]], group):
            sums_ref[sums_at(index), :] = total

    each_tile(tile, width)


def filter_far_kernel(q_ref, k_ref, v_ref, dy_ref, other_ref, masks_ref, base_ref, out_ref, total_ref, cross_ref, *, scale):
    inputs = (q_ref, k_ref, v_ref, dy_ref)
    width = q_ref.shape[1] // 2
    core = lax.axis_index("ctx") % 2
    even = core == 0
    cross_ref[...] = jnp.where(even, masks_ref[4], masks_ref[5])
    group = lane_groups()

    def sides(index):
        kv, cot = tile_products(inputs, core, index)
        return other_ref[:, lanes_of(0, width, index)], jnp.where(even, cot, kv)

    def store(at, total):
        total_ref[at, :] = base_ref[at, :] + total

    each_tile(lambda index: two_tiles(2 * index, sides, cross_ref, store, group), width // 2)
    total = diagonals(total_ref, out_ref.shape[0])
    out_ref[...] = jnp.where(even, total, reversed_taps(total)) * scale


def conv_kernel(
    a_ref, b_ref, pair_ref, far_ref, c_ref, d_ref, masks_ref, taps_ref, c_in_hbm, d_in_hbm, out_c_hbm, out_d_hbm,
    out_c_ref, out_d_ref, sems, *, backward, half,
):
    del c_in_hbm, d_in_hbm
    rows = a_ref.shape[0]
    per_tile = LANES // GSIZE
    width = a_ref.shape[1] // 2
    base = half * width
    even = lax.axis_index("ctx") % 2 == 0
    group = lane_groups()
    groups = width // GSIZE
    mask_ref = masks_ref.at[1 if backward else 0]

    def table_start(row):
        start = pltpu.roll(jnp.broadcast_to(row, (BLOCK, rows)), 0, 1, stride=1, stride_axis=0).astype(jnp.bfloat16)
        return jnp.concatenate([start, start], axis=1)

    def tile(index):
        here = pl.ds(pl.multiple_of(index * LANES, LANES), LANES)
        lanes = pl.ds(pl.multiple_of(base + index * LANES, LANES), LANES)
        from_pair = even if backward else jnp.logical_not(even)
        own = product(a_ref[:, lanes], b_ref[:, lanes])
        other = jnp.where(from_pair, pair_ref[:, here], far_ref[:, here])
        at = pl.multiple_of(half * groups + index * per_tile, per_tile)
        taps = taps_ref[1 if backward else 0, pl.ds(at, per_tile), :]
        tables = jnp.concatenate([table_start(taps[g : g + 1]) for g in range(per_tile)], axis=0)
        for at in range(0, rows, BLOCK):
            x = jnp.concatenate([turned(own, at), turned(other, at)], axis=0)
            masked = tables * for_groups(mask_ref[at : at + BLOCK, :])
            every = jnp.dot(masked, x, preferred_element_type=jnp.float32)
            y = every[:BLOCK]
            for g in range(1, per_tile):
                y = jnp.where(group == g, every[g * BLOCK : (g + 1) * BLOCK], y)
            block = slice(at, at + BLOCK)
            out_c_ref[block, here] = (c_ref[block, lanes].astype(jnp.float32) * y).astype(jnp.bfloat16)
            out_d_ref[block, here] = (d_ref[block, lanes].astype(jnp.float32) * y).astype(jnp.bfloat16)

    step = math.gcd(width // LANES, STEP) * LANES

    def stored(i):
        here = pl.ds(pl.multiple_of(i * step, step), step)
        there = pl.ds(pl.multiple_of(base + i * step, step), step)
        return [
            pltpu.make_async_copy(out_c_ref.at[:, here], out_c_hbm.at[:, there], sems.at[0, i]),
            pltpu.make_async_copy(out_d_ref.at[:, here], out_d_hbm.at[:, there], sems.at[1, i]),
        ]

    def body(i, carry):
        for j in range(step // LANES):
            tile(i * (step // LANES) + j)
        for copy in stored(i):
            copy.start()
        return carry

    lax.fori_loop(0, width // step, body, 0)
    for i in range(width // step):
        for copy in stored(i):
            copy.wait()


def local_call(kernel, name, out_shape, scratch_shapes, flops, operands, in_specs=None, out_specs=VMEM, aliases={}, moved=None):
    outs = out_shape if isinstance(out_shape, list) else [out_shape]
    if moved is None:
        moved = sum(math.prod(x.shape) * x.dtype.itemsize for x in [*operands, *outs])
    return pl.pallas_call(
        kernel,
        out_shape=out_shape,
        in_specs=in_specs or [VMEM] * len(operands),
        out_specs=out_specs,
        scratch_shapes=scratch_shapes,
        input_output_aliases=aliases,
        cost_estimate=pl.CostEstimate(flops=flops, bytes_accessed=moved, transcendentals=0),
        compiler_params=pltpu.CompilerParams(vmem_limit_bytes=24 << 20),
        name=name,
    )(*operands)


def in_hbm(*arrays):
    return [pltpu.with_memory_space_constraint(x, pltpu.HBM) for x in arrays]


def own_call(kernel, name, out_shape, scratch_shapes, hbm_operands, operands, aliases={}):
    return pl.pallas_call(
        kernel,
        out_shape=out_shape,
        in_specs=[pl.BlockSpec(memory_space=pltpu.HBM)] * len(hbm_operands) + [VMEM] * len(operands),
        out_specs=[VMEM] * len(out_shape) if isinstance(out_shape, list) else VMEM,
        scratch_shapes=scratch_shapes,
        input_output_aliases=aliases,
        cost_estimate=pl.CostEstimate(flops=0, bytes_accessed=0, transcendentals=0),
        compiler_params=pltpu.CompilerParams(vmem_limit_bytes=24 << 20),
        name=name,
    )(*in_hbm(*hbm_operands), *operands)


def first(q, k, v, dy, starts, filters):
    rows, width = q.shape
    wide = pltpu.VMEM((rows, width), jnp.bfloat16)
    sent = pltpu.VMEM((rows, width // 2), jnp.bfloat16)
    return own_call(
        first_kernel, "first",
        [wide] * 4 + [sent] * 2 + [
            pltpu.VMEM((2, rows, rows), jnp.float32),
            pltpu.VMEM((6, rows, rows), jnp.float32),
            pltpu.VMEM((2, rows, 2 * rows), jnp.bfloat16),
            pltpu.VMEM((2, *filters.shape), jnp.float32),
        ],
        [
            pltpu.VMEM(starts.shape, starts.dtype), pltpu.VMEM(filters.shape, filters.dtype),
            pltpu.SemaphoreType.DMA((10,)),
        ],
        (q, k, v, dy, starts, filters), (),
    )


def convolution(a, b, pair, far, c, d, masks, taps, outs, backward, half):
    rows, width = a.shape
    steps = width // 2 // LANES // math.gcd(width // 2 // LANES, STEP)
    out = jax.ShapeDtypeStruct((rows, width), jnp.bfloat16)
    part = pltpu.VMEM((rows, width // 2), jnp.bfloat16)
    anywhere = pl.BlockSpec(memory_space=pl.ANY)
    body = functools.partial(conv_kernel, backward=backward, half=half)
    operands = (a, b, pair, far, c, d, masks, taps)
    n = len(operands)
    return local_call(
        body if outs else lambda *refs: body(*refs[:n], None, None, *refs[n:]),
        ("backward" if backward else "forward") + ("_high" if half else "_low"),
        [out, out],
        [part, part, pltpu.SemaphoreType.DMA((2, steps))],
        16 * rows * rows * width,
        operands + tuple(outs or ()),
        [VMEM] * n + [anywhere] * (2 if outs else 0),
        [anywhere] * 2,
        {n: 0, n + 1: 1} if outs else {},
    )


def other_core(block):
    return lax.ppermute(block, "ctx", [(i, i ^ 1) for i in range(lax.axis_size("ctx"))])


def next_chip(block):
    size = lax.axis_size("ctx")
    pairs = [(i, i + 1) for i in range(1, size - 1, 2)]
    return lax.ppermute(block, "ctx", pairs + [(j, i) for i, j in pairs])


def factors(size):
    found, p = [], 2
    while size > 1:
        while size % p == 0:
            found.append(p)
            size //= p
        p += 1
    return found


def rounds_over_chips():
    return [
        (axis, first * math.prod(factors(lax.axis_size(axis) // first)[:n]), p)
        for axis, first in (("dp", 1), ("ctx", 2))
        for n, p in enumerate(factors(lax.axis_size(axis) // first))
    ]


def summed_over(total, axis, stride, p):
    size = lax.axis_size(axis)
    turned = lambda i, k: i + ((i // stride + k) % p - i // stride % p) * stride
    got = [lax.ppermute(total, axis, [(turned(i, k), i) for i in range(size)]) for k in range(1, p)]
    if p == 2:
        return total + got[0]
    digit = lax.axis_index(axis) // stride % p
    return jnp.sum(jnp.roll(jnp.stack([total, *got]), digit, axis=0), axis=0)


def after(value, *others):
    return lax.optimization_barrier((value, *others))[0]


def per_device(q_proj, k_proj, v_proj, out_grad, contig_starts, filters):
    q, k, v, dy = q_proj[0], k_proj[0], v_proj[0], out_grad[0]
    rows = q.shape[0]
    groups, taps = filters.shape
    assert rows == taps == LANES and lax.axis_size("ctx") % 2 == 0
    scale = 1.0 / math.sqrt(rows * lax.axis_size("ctx") * lax.axis_size("dp") * GSIZE)
    inputs = q, k, v, dy
    *partly, far_out, pair_out, keep, masks, table_masks, tap_rows = first(*inputs, contig_starts, filters)
    square = pltpu.VMEM((rows, rows), jnp.float32)
    part = pltpu.VMEM((groups // 2, rows), jnp.float32)
    unsummed = pltpu.VMEM((groups * 4, rows), jnp.float32)
    wide = pltpu.VMEM(q.shape, q.dtype)
    sent = pltpu.VMEM((rows, q.shape[1] // 2), q.dtype)
    far = next_chip(far_out)
    later_pair = other_core(pair_out)
    q, k, v, dy, theirs, pair_out, far_out = own_call(
        functools.partial(filter_partner_kernel, scale=scale), "filter_partner",
        [wide] * 4 + [part, sent, sent], [unsummed, pltpu.SemaphoreType.DMA((8,))],
        inputs, (*partly, keep, masks), {4: 0, 5: 1, 6: 2, 7: 3},
    )
    pair = other_core(pair_out)
    mine = own_call(
        filter_own_kernel, "filter_own", unsummed, [square, square],
        (), (q, k, v, dy, later_pair, masks),
    )
    later_far = next_chip(after(far_out, mine))
    mine = own_call(
        functools.partial(filter_far_kernel, scale=scale), "filter_far", part, [unsummed, square],
        (), (q, k, v, dy, far, masks, mine),
    )
    mine = mine + other_core(theirs)

    def forward(pair, far, outs, half):
        return convolution(k, v, pair, far, q, dy, table_masks, tap_rows, outs, False, half)

    def backward(pair, far, outs, half):
        return convolution(dy, q, pair, far, v, k, table_masks, tap_rows, outs, True, half)

    for n, place in enumerate(rounds_over_chips()):
        if n == 0:
            half_forward = forward(pair, far, None, 0)
        if n == 1:
            mine = after(mine, *half_forward)
            half_backward = backward(pair, far, None, 1)
        if n == 2:
            mine = after(mine, *half_backward, later_far, later_pair)
            mixed, grad_q = forward(later_pair, later_far, half_forward, 1)
        if n == 3:
            mine = after(mine, mixed, grad_q)
            grad_k, grad_v = backward(later_pair, later_far, half_backward, 0)
        mine = summed_over(mine, *place)
    mine = after(mine, grad_k, grad_v)
    halves = [mine, other_core(mine)]
    filter_grad = jnp.where(lax.axis_index("ctx") % 2 == 0, jnp.concatenate(halves), jnp.concatenate(halves[::-1]))
    return (mixed[None], grad_q[None], grad_k[None], grad_v[None], filter_grad)


def solution(mesh):
    wide = P("dp", "ctx", None)
    return jax.shard_map(
        per_device,
        mesh=mesh,
        in_specs=(wide,) * 4 + (P("dp", "ctx"), P()),
        out_specs=(wide,) * 4 + (P(),),
        check_vma=False,
    )
```

```python
import functools
import math

import jax
import jax.numpy as jnp
from jax import lax
from jax.experimental import pallas as pl
from jax.experimental.pallas import tpu as pltpu
from jax.sharding import PartitionSpec as P

GSIZE = 16
LANES = 128
BLOCK = 16
STEP = 4
VMEM = pl.BlockSpec(memory_space=pltpu.VMEM)


def product(a, b):
    return a * b


def reversed_taps(rows_of_taps):
    taps = rows_of_taps.shape[1]
    i = lax.broadcasted_iota(jnp.int32, (taps, taps), 0)
    j = lax.broadcasted_iota(jnp.int32, (taps, taps), 1)
    flip = jnp.where((i + j == 0) | (i + j == taps), 1.0, 0.0).astype(jnp.float32)
    return jnp.dot(
        rows_of_taps.astype(jnp.float32), flip,
        preferred_element_type=jnp.float32, precision=lax.Precision.HIGHEST,
    )


def lane_groups():
    return lax.broadcasted_iota(jnp.int32, (1, LANES), 1) // GSIZE


def each_tile(tile, width):
    count = width // LANES
    step = math.gcd(count, STEP)

    def body(i, carry):
        for j in range(step):
            tile(i * step + j)
        return carry

    lax.fori_loop(0, count // step, body, 0)


def aligned(mask):
    rows = mask.shape[0]
    blocks = [mask[at : at + BLOCK] for at in range(0, rows, BLOCK)]
    return jnp.concatenate(
        blocks[:1] + [pltpu.roll(block, rows - BLOCK * (i + 1), 1) for i, block in enumerate(blocks[1:])], axis=0
    )


def turned(tile, at):
    return jnp.concatenate([tile[at:], tile[:at]], axis=0) if at else tile


def for_groups(block):
    return jnp.concatenate([block] * (LANES // GSIZE), axis=0)


def half_copies(sources, targets, half, sems):
    rows, width = sources[0].shape
    lanes = pl.ds(pl.multiple_of(half * (width // 2), width // 2), width // 2)
    copies = []
    for n in range(2):
        part = pl.ds(n * (rows // 2), rows // 2)
        for source, target in zip(sources, targets):
            copies.append(
                pltpu.make_async_copy(source.at[part, lanes], target.at[part, lanes], sems.at[len(copies)])
            )
    return copies


def sent_products(inputs, half, keep_ref, kv_out, cot_out, swapped):
    q_ref, k_ref, v_ref, dy_ref = inputs
    width = kv_out.shape[1]
    lanes = pl.ds(pl.multiple_of(half * width, width), width)
    kv = product(k_ref[:, lanes], v_ref[:, lanes])
    cot = product(dy_ref[:, lanes], q_ref[:, lanes])
    kv = jnp.where(keep_ref[1][:, :1] > 0, kv, jnp.zeros_like(kv))
    cot = jnp.where(keep_ref[0][:, :1] > 0, cot, jnp.zeros_like(cot))
    kv_out[...] = jnp.where(swapped, cot, kv)
    cot_out[...] = jnp.where(swapped, kv, cot)


def first_kernel(
    q_hbm, k_hbm, v_hbm, dy_hbm, starts_hbm, filters_hbm,
    q_ref, k_ref, v_ref, dy_ref, far_ref, pair_ref, keep_ref, masks_ref, table_masks_ref, taps_ref,
    starts_ref, filters_ref, sems,
):
    rows = q_ref.shape[0]
    core = lax.axis_index("ctx") % 2
    small = [
        pltpu.make_async_copy(starts_hbm, starts_ref, sems.at[8]),
        pltpu.make_async_copy(filters_hbm, filters_ref, sems.at[9]),
    ]
    inputs = (q_ref, k_ref, v_ref, dy_ref)
    copies = half_copies((q_hbm, k_hbm, v_hbm, dy_hbm), inputs, 1 - core, sems)
    for copy in small + copies:
        copy.start()

    small[0].wait()
    starts = jnp.broadcast_to(starts_ref[...], (rows, rows)) > 0
    t = lax.broadcasted_iota(jnp.int32, (rows, rows), 0)
    s = lax.broadcasted_iota(jnp.int32, (rows, rows), 1)
    began = jnp.max(jnp.where(starts & (s <= t), s, 0), axis=1, keepdims=True)
    first = jnp.min(jnp.where(starts, s, rows), axis=1, keepdims=True)
    last = jnp.max(jnp.where(starts, s, 0), axis=1, keepdims=True)
    as_f32 = lambda mask: jnp.where(mask, 1.0, 0.0).astype(jnp.float32)
    own = as_f32((s <= t) & (s >= began))
    previous = as_f32((s > t) & (t < first))
    following = as_f32((s < t) & (t >= last))
    keep_ref[0] = as_f32(t < first)
    keep_ref[1] = as_f32(t >= last)
    for n, parts in enumerate(((own, previous), (own.T, following))):
        for m, mask in enumerate(parts):
            table_masks_ref[n, :, m * rows : (m + 1) * rows] = aligned(mask).astype(jnp.bfloat16)
    for n, mask in enumerate((own.T, following, previous.T)):
        masks_ref[n] = aligned(mask)
    small[1].wait()
    taps_ref[0] = reversed_taps(filters_ref[...])
    taps_ref[1] = filters_ref[...].astype(jnp.float32)
    for copy in copies:
        copy.wait()
    sent_products(inputs, 1 - core, keep_ref, far_ref, pair_ref, core == 0)


def tile_products(inputs, half, index):
    q_ref, k_ref, v_ref, dy_ref = inputs
    lanes = lanes_of(half, q_ref.shape[1] // 2, index)
    return product(k_ref[:, lanes], v_ref[:, lanes]), product(dy_ref[:, lanes], q_ref[:, lanes])


def wrapped_products(left, rights, masks, group):
    rows = left[0].shape[0]
    zeros = jnp.zeros_like(left[0])
    totals = [None] * len(masks)
    for at in range(0, rows, BLOCK):
        picked = jnp.concatenate(
            [
                jnp.concatenate([jnp.where(group == g, tile[at : at + BLOCK], zeros[:BLOCK]) for tile in left], axis=1)
                for g in range(LANES // GSIZE)
            ],
            axis=0,
        )
        right = jnp.concatenate(
            [
                jnp.concatenate([zeros if tile is None else turned(tile, at) for tile in tiles], axis=1)
                for tiles in rights
            ],
            axis=0,
        )
        pairs = lax.dot_general(picked, right, (((1,), (1,)), ((), ())), preferred_element_type=jnp.float32)
        for n, columns in enumerate(masks):
            for column, mask_ref in columns:
                piece = pairs[:, column * rows : (column + 1) * rows] * for_groups(mask_ref[at : at + BLOCK, :])
                totals[n] = piece if totals[n] is None else totals[n] + piece
    for total in totals:
        yield jnp.concatenate(
            [
                total[at : at + 8] + pltpu.roll(total[at + 8 : at + 16], rows - 8, 1)
                for at in range(0, total.shape[0], BLOCK)
            ],
            axis=0,
        )


def diagonals(sums_ref, groups):
    rows = sums_ref.shape[1]
    total = sums_ref[pl.ds(0, groups, stride=8), :]
    for r in range(1, 8):
        total = total + pltpu.roll(sums_ref[pl.ds(r, groups, stride=8), :], rows - r, 1)
    return total


def sums_at(index):
    count = LANES // GSIZE * 8
    return pl.ds(pl.multiple_of(index * count, count), count)


def two_tiles(index, sides, mask_ref, store, group):
    (left_a, right_a), (left_b, right_b) = sides(index), sides(index + 1)
    masks = [[(0, mask_ref)], [(1, mask_ref)]]
    rights = [[right_a, None], [None, right_b]]
    for n, total in enumerate(wrapped_products([left_a, left_b], rights, masks, group)):
        store(sums_at(index + n), total)


def lanes_of(half, width, index):
    return pl.ds(pl.multiple_of(half * width + index * LANES, LANES), LANES)


def filter_partner_kernel(
    q_hbm, k_hbm, v_hbm, dy_hbm, q_in, k_in, v_in, dy_in, keep_ref, masks_ref,
    q_ref, k_ref, v_ref, dy_ref, out_ref, pair_ref, far_ref, sums_ref, sems, *, scale
):
    del q_in, k_in, v_in, dy_in
    core = lax.axis_index("ctx") % 2
    inputs = (q_ref, k_ref, v_ref, dy_ref)
    copies = half_copies((q_hbm, k_hbm, v_hbm, dy_hbm), inputs, core, sems)
    for copy in copies:
        copy.start()
    group = lane_groups()

    def store(at, total):
        sums_ref[at, :] = total

    def tiles(index):
        two_tiles(2 * index, lambda i: tile_products(inputs, 1 - core, i), masks_ref.at[0], store, group)

    each_tile(tiles, q_ref.shape[1] // 4)
    out_ref[...] = diagonals(sums_ref, out_ref.shape[0]) * scale
    for copy in copies:
        copy.wait()
    sent_products(inputs, core, keep_ref, pair_ref, far_ref, core == 1)


def filter_own_kernel(q_ref, k_ref, v_ref, dy_ref, other_ref, masks_ref, sums_ref, cross_ref):
    inputs = (q_ref, k_ref, v_ref, dy_ref)
    width = q_ref.shape[1] // 2
    core = lax.axis_index("ctx") % 2
    even = core == 0
    cross_ref[...] = jnp.where(even, masks_ref[1], masks_ref[2])
    group = lane_groups()

    def tile(index):
        kv, cot = tile_products(inputs, core, index)
        other = other_ref[:, lanes_of(0, width, index)]
        left = [kv, jnp.where(even, kv, other)]
        rights = [[cot, None], [None, jnp.where(even, other, cot)]]
        for total in wrapped_products(left, rights, [[(0, masks_ref.at[0]), (1, cross_ref)]], group):
            sums_ref[sums_at(index), :] = total

    each_tile(tile, width)


def filter_far_kernel(q_ref, k_ref, v_ref, dy_ref, other_ref, masks_ref, base_ref, out_ref, total_ref, cross_ref, *, scale):
    inputs = (q_ref, k_ref, v_ref, dy_ref)
    width = q_ref.shape[1] // 2
    core = lax.axis_index("ctx") % 2
    even = core == 0
    cross_ref[...] = jnp.where(even, masks_ref[2], masks_ref[1])
    group = lane_groups()

    def sides(index):
        kv, cot = tile_products(inputs, core, index)
        other = other_ref[:, lanes_of(0, width, index)]
        return jnp.where(even, other, kv), jnp.where(even, cot, other)

    def store(at, total):
        total_ref[at, :] = base_ref[at, :] + total

    each_tile(lambda index: two_tiles(2 * index, sides, cross_ref, store, group), width // 2)
    out_ref[...] = diagonals(total_ref, out_ref.shape[0]) * scale


def conv_kernel(
    a_ref, b_ref, c_ref, d_ref, masks_ref, taps_ref, pair_ref, far_ref, *rest, backward, spans
):
    later = rest[: 2 * len(spans) - 2]
    others = [(pair_ref, far_ref), *zip(later[::2], later[1::2])]
    out_c_hbm, out_d_hbm, out_c_ref, out_d_ref, sems = rest[-5:]
    rows = a_ref.shape[0]
    per_tile = LANES // GSIZE
    half_tiles = a_ref.shape[1] // 2 // LANES
    even = lax.axis_index("ctx") % 2 == 0
    from_pair = even if backward else jnp.logical_not(even)
    group = lane_groups()
    mask_ref = masks_ref.at[1 if backward else 0]

    def table_start(row):
        start = pltpu.roll(jnp.broadcast_to(row, (BLOCK, rows)), 0, 1, stride=1, stride_axis=0).astype(jnp.bfloat16)
        return jnp.concatenate([start, start], axis=1)

    def lanes_at(index):
        return pl.ds(pl.multiple_of(index * LANES, LANES), LANES)

    def tile(index, near, distant):
        lanes = lanes_at(index)
        here = lanes_at(index % half_tiles)
        own = product(a_ref[:, lanes], b_ref[:, lanes])
        other = jnp.where(from_pair, near[:, here], distant[:, here])
        taps = taps_ref[1 if backward else 0, pl.ds(pl.multiple_of(index * per_tile, per_tile), per_tile), :]
        tables = jnp.concatenate([table_start(taps[g : g + 1]) for g in range(per_tile)], axis=0)
        for at in range(0, rows, BLOCK):
            x = jnp.concatenate([turned(own, at), turned(other, at)], axis=0)
            masked = tables * for_groups(mask_ref[at : at + BLOCK, :])
            every = jnp.dot(masked, x, preferred_element_type=jnp.float32)
            y = every[:BLOCK]
            for g in range(1, per_tile):
                y = jnp.where(group == g, every[g * BLOCK : (g + 1) * BLOCK], y)
            block = slice(at, at + BLOCK)
            out_c_ref[block, lanes] = (c_ref[block, lanes].astype(jnp.float32) * y).astype(jnp.bfloat16)
            out_d_ref[block, lanes] = (d_ref[block, lanes].astype(jnp.float32) * y).astype(jnp.bfloat16)

    def stored(start, count, sem):
        lanes = pl.ds(pl.multiple_of(start * LANES, count * LANES), count * LANES)
        return [
            pltpu.make_async_copy(out_c_ref.at[:, lanes], out_c_hbm.at[:, lanes], sems.at[0, sem]),
            pltpu.make_async_copy(out_d_ref.at[:, lanes], out_d_hbm.at[:, lanes], sems.at[1, sem]),
        ]

    bodies = []
    for (first, count), (near, distant) in zip(spans, others):
        step = math.gcd(count, STEP)

        def body(i, carry, first=first, step=step, near=near, distant=distant, sem=len(bodies)):
            for j in range(step):
                tile(first + i * step + j, near, distant)
            for copy in stored(first + i * step, step, sem + i):
                copy.start()
            return carry

        lax.fori_loop(0, count // step, body, 0)
        bodies += [(first + i * step, step) for i in range(count // step)]
    for n, (start, count) in enumerate(bodies):
        for copy in stored(start, count, n):
            copy.wait()


def local_call(kernel, name, out_shape, scratch_shapes, flops, operands, in_specs=None, out_specs=VMEM, aliases={}, moved=None):
    outs = out_shape if isinstance(out_shape, list) else [out_shape]
    if moved is None:
        moved = sum(math.prod(x.shape) * x.dtype.itemsize for x in [*operands, *outs])
    return pl.pallas_call(
        kernel,
        out_shape=out_shape,
        in_specs=in_specs or [VMEM] * len(operands),
        out_specs=out_specs,
        scratch_shapes=scratch_shapes,
        input_output_aliases=aliases,
        cost_estimate=pl.CostEstimate(flops=flops, bytes_accessed=moved, transcendentals=0),
        compiler_params=pltpu.CompilerParams(vmem_limit_bytes=24 << 20),
        name=name,
    )(*operands)


def in_hbm(*arrays):
    return [pltpu.with_memory_space_constraint(x, pltpu.HBM) for x in arrays]


def own_call(kernel, name, out_shape, scratch_shapes, hbm_operands, operands, aliases={}):
    return pl.pallas_call(
        kernel,
        out_shape=out_shape,
        in_specs=[pl.BlockSpec(memory_space=pltpu.HBM)] * len(hbm_operands) + [VMEM] * len(operands),
        out_specs=[VMEM] * len(out_shape) if isinstance(out_shape, list) else VMEM,
        scratch_shapes=scratch_shapes,
        input_output_aliases=aliases,
        cost_estimate=pl.CostEstimate(flops=0, bytes_accessed=0, transcendentals=0),
        compiler_params=pltpu.CompilerParams(vmem_limit_bytes=24 << 20),
        name=name,
    )(*in_hbm(*hbm_operands), *operands)


def first(q, k, v, dy, starts, filters):
    rows, width = q.shape
    wide = pltpu.VMEM((rows, width), jnp.bfloat16)
    sent = pltpu.VMEM((rows, width // 2), jnp.bfloat16)
    return own_call(
        first_kernel, "first",
        [wide] * 4 + [sent] * 2 + [
            pltpu.VMEM((2, rows, rows), jnp.float32),
            pltpu.VMEM((3, rows, rows), jnp.float32),
            pltpu.VMEM((2, rows, 2 * rows), jnp.bfloat16),
            pltpu.VMEM((2, *filters.shape), jnp.float32),
        ],
        [
            pltpu.VMEM(starts.shape, starts.dtype), pltpu.VMEM(filters.shape, filters.dtype),
            pltpu.SemaphoreType.DMA((10,)),
        ],
        (q, k, v, dy, starts, filters), (),
    )


def convolution(a, b, c, d, masks, taps, spans, others, outs, backward):
    rows, width = a.shape
    count = sum(tiles // math.gcd(tiles, STEP) for _, tiles in spans)
    out = jax.ShapeDtypeStruct((rows, width), jnp.bfloat16)
    whole = pltpu.VMEM((rows, width), jnp.bfloat16)
    anywhere = pl.BlockSpec(memory_space=pl.ANY)
    body = functools.partial(conv_kernel, backward=backward, spans=spans)
    operands = (a, b, c, d, masks, taps, *[x for pair in others for x in pair])
    n = len(operands)
    return local_call(
        (lambda *refs: body(*refs[:n], *refs[n + 2 :])) if outs else body,
        "backward" if backward else "forward",
        [out, out],
        [whole, whole, pltpu.SemaphoreType.DMA((2, count))],
        16 * rows * rows * width,
        operands + tuple(outs or ()),
        [VMEM] * n + [anywhere] * (2 if outs else 0),
        [anywhere] * 2,
        {n: 0, n + 1: 1} if outs else {},
    )


def other_core(block):
    return lax.ppermute(block, "ctx", [(i, i ^ 1) for i in range(lax.axis_size("ctx"))])


def next_chip(block):
    size = lax.axis_size("ctx")
    pairs = [(i, i + 1) for i in range(1, size - 1, 2)]
    return lax.ppermute(block, "ctx", pairs + [(j, i) for i, j in pairs])


def factors(size):
    found, p = [], 2
    while size > 1:
        while size % p == 0:
            found.append(p)
            size //= p
        p += 1
    return found


def rounds_over_chips():
    return [
        (axis, first * math.prod(factors(lax.axis_size(axis) // first)[:n]), p)
        for axis, first in (("dp", 1), ("ctx", 2))
        for n, p in enumerate(factors(lax.axis_size(axis) // first))
    ]


def summed_over(total, axis, stride, p):
    size = lax.axis_size(axis)
    turned = lambda i, k: i + ((i // stride + k) % p - i // stride % p) * stride
    got = [lax.ppermute(total, axis, [(turned(i, k), i) for i in range(size)]) for k in range(1, p)]
    if p == 2:
        return total + got[0]
    digit = lax.axis_index(axis) // stride % p
    return jnp.sum(jnp.roll(jnp.stack([total, *got]), digit, axis=0), axis=0)


def after(value, *others):
    return lax.optimization_barrier((value, *others))[0]


def per_device(q_proj, k_proj, v_proj, out_grad, contig_starts, filters):
    q, k, v, dy = q_proj[0], k_proj[0], v_proj[0], out_grad[0]
    rows = q.shape[0]
    groups, taps = filters.shape
    assert rows == taps == LANES and lax.axis_size("ctx") % 2 == 0
    scale = 1.0 / math.sqrt(rows * lax.axis_size("ctx") * lax.axis_size("dp") * GSIZE)
    inputs = q, k, v, dy
    *partly, far_out, pair_out, keep, masks, table_masks, tap_rows = first(*inputs, contig_starts, filters)
    square = pltpu.VMEM((rows, rows), jnp.float32)
    part = pltpu.VMEM((groups // 2, rows), jnp.float32)
    unsummed = pltpu.VMEM((groups * 4, rows), jnp.float32)
    wide = pltpu.VMEM(q.shape, q.dtype)
    sent = pltpu.VMEM((rows, q.shape[1] // 2), q.dtype)
    far = next_chip(far_out)
    later_pair = other_core(pair_out)
    q, k, v, dy, theirs, pair_out, far_out = own_call(
        functools.partial(filter_partner_kernel, scale=scale), "filter_partner",
        [wide] * 4 + [part, sent, sent], [unsummed, pltpu.SemaphoreType.DMA((8,))],
        inputs, (*partly, keep, masks), {4: 0, 5: 1, 6: 2, 7: 3},
    )
    pair = other_core(pair_out)
    mine = own_call(
        filter_own_kernel, "filter_own", unsummed, [square],
        (), (q, k, v, dy, later_pair, masks),
    )
    later_far = next_chip(after(far_out, mine))
    mine = own_call(
        functools.partial(filter_far_kernel, scale=scale), "filter_far", part, [unsummed, square],
        (), (q, k, v, dy, far, masks, mine),
    )
    mine = mine + other_core(theirs)

    half_tiles = q.shape[1] // 2 // LANES
    few = max(half_tiles // 2, 1)
    first_others, later_others = (pair, far), (later_pair, later_far)

    def forward(spans, others, outs=None):
        return convolution(k, v, q, dy, table_masks, tap_rows, spans, others, outs, False)

    def backward(spans, others, outs=None):
        return convolution(dy, q, v, k, table_masks, tap_rows, spans, others, outs, True)

    for n, place in enumerate(rounds_over_chips()):
        if n == 0:
            some_forward = forward([(0, few)], [first_others])
        if n == 1:
            mine = after(mine, *some_forward)
            some_backward = backward([(half_tiles, few)], [first_others])
        if n == 2:
            mine = after(mine, *some_backward, later_far, later_pair)
            mixed, grad_q = forward(
                [(few, half_tiles - few), (half_tiles, half_tiles)], [first_others, later_others], some_forward
            )
        if n == 3:
            mine = after(mine, mixed, grad_q)
            grad_k, grad_v = backward(
                [(half_tiles + few, half_tiles - few), (0, half_tiles)], [first_others, later_others], some_backward
            )
        mine = summed_over(mine, *place)
    mine = after(mine, grad_k, grad_v)
    halves = [mine, other_core(mine)]
    filter_grad = jnp.where(lax.axis_index("ctx") % 2 == 0, jnp.concatenate(halves), jnp.concatenate(halves[::-1]))
    return (mixed[None], grad_q[None], grad_k[None], grad_v[None], filter_grad)


def solution(mesh):
    wide = P("dp", "ctx", None)
    return jax.shard_map(
        per_device,
        mesh=mesh,
        in_specs=(wide,) * 4 + (P("dp", "ctx"), P()),
        out_specs=(wide,) * 4 + (P(),),
        check_vma=False,
    )
```

```python
import functools
import math

import jax
import jax.numpy as jnp
from jax import lax
from jax.experimental import pallas as pl
from jax.experimental.pallas import tpu as pltpu
from jax.sharding import PartitionSpec as P

GSIZE = 16
LANES = 128
BLOCK = 32
STEP = 4
VMEM = pl.BlockSpec(memory_space=pltpu.VMEM)


def product(a, b):
    return a * b


def reversed_taps(rows_of_taps):
    taps = rows_of_taps.shape[1]
    i = lax.broadcasted_iota(jnp.int32, (taps, taps), 0)
    j = lax.broadcasted_iota(jnp.int32, (taps, taps), 1)
    flip = jnp.where((i + j == 0) | (i + j == taps), 1.0, 0.0).astype(jnp.float32)
    return jnp.dot(
        rows_of_taps.astype(jnp.float32), flip,
        preferred_element_type=jnp.float32, precision=lax.Precision.HIGHEST,
    )


def lane_groups():
    return lax.broadcasted_iota(jnp.int32, (1, LANES), 1) // GSIZE


def each_tile(tile, width):
    count = width // LANES
    step = math.gcd(count, STEP)

    def body(i, carry):
        for j in range(step):
            tile(i * step + j)
        return carry

    lax.fori_loop(0, count // step, body, 0)


def aligned(mask):
    rows = mask.shape[0]
    blocks = [mask[at : at + BLOCK] for at in range(0, rows, BLOCK)]
    return jnp.concatenate(
        blocks[:1] + [pltpu.roll(block, rows - BLOCK * (i + 1), 1) for i, block in enumerate(blocks[1:])], axis=0
    )


def turned(tile, at):
    return jnp.concatenate([tile[at:], tile[:at]], axis=0) if at else tile


def for_groups(block):
    return jnp.concatenate([block] * (LANES // GSIZE), axis=0)


def half_copies(sources, targets, half, sems):
    rows, width = sources[0].shape
    lanes = pl.ds(pl.multiple_of(half * (width // 2), width // 2), width // 2)
    copies = []
    for n in range(2):
        part = pl.ds(n * (rows // 2), rows // 2)
        for source, target in zip(sources, targets):
            copies.append(
                pltpu.make_async_copy(source.at[part, lanes], target.at[part, lanes], sems.at[len(copies)])
            )
    return copies


def sent_products(inputs, half, keep_ref, kv_out, cot_out, swapped):
    q_ref, k_ref, v_ref, dy_ref = inputs
    width = kv_out.shape[1]
    lanes = pl.ds(pl.multiple_of(half * width, width), width)
    kv = product(k_ref[:, lanes], v_ref[:, lanes])
    cot = product(dy_ref[:, lanes], q_ref[:, lanes])
    kv = jnp.where(keep_ref[1][:, :1] > 0, kv, jnp.zeros_like(kv))
    cot = jnp.where(keep_ref[0][:, :1] > 0, cot, jnp.zeros_like(cot))
    kv_out[...] = jnp.where(swapped, cot, kv)
    cot_out[...] = jnp.where(swapped, kv, cot)


def first_kernel(
    q_hbm, k_hbm, v_hbm, dy_hbm, starts_hbm, filters_hbm,
    q_ref, k_ref, v_ref, dy_ref, far_ref, pair_ref, keep_ref, masks_ref, table_masks_ref, taps_ref,
    starts_ref, filters_ref, sems,
):
    rows = q_ref.shape[0]
    core = lax.axis_index("ctx") % 2
    small = [
        pltpu.make_async_copy(starts_hbm, starts_ref, sems.at[8]),
        pltpu.make_async_copy(filters_hbm, filters_ref, sems.at[9]),
    ]
    inputs = (q_ref, k_ref, v_ref, dy_ref)
    copies = half_copies((q_hbm, k_hbm, v_hbm, dy_hbm), inputs, 1 - core, sems)
    for copy in small + copies:
        copy.start()

    small[0].wait()
    starts = jnp.broadcast_to(starts_ref[...], (rows, rows)) > 0
    t = lax.broadcasted_iota(jnp.int32, (rows, rows), 0)
    s = lax.broadcasted_iota(jnp.int32, (rows, rows), 1)
    began = jnp.max(jnp.where(starts & (s <= t), s, 0), axis=1, keepdims=True)
    first = jnp.min(jnp.where(starts, s, rows), axis=1, keepdims=True)
    last = jnp.max(jnp.where(starts, s, 0), axis=1, keepdims=True)
    as_f32 = lambda mask: jnp.where(mask, 1.0, 0.0).astype(jnp.float32)
    own = as_f32((s <= t) & (s >= began))
    previous = as_f32((s > t) & (t < first))
    following = as_f32((s < t) & (t >= last))
    keep_ref[0] = as_f32(t < first)
    keep_ref[1] = as_f32(t >= last)
    for n, parts in enumerate(((own, previous), (own.T, following))):
        for m, mask in enumerate(parts):
            table_masks_ref[n, :, m * rows : (m + 1) * rows] = aligned(mask).astype(jnp.bfloat16)
    for n, mask in enumerate((own.T, following, previous.T)):
        masks_ref[n] = aligned(mask)
    small[1].wait()
    taps_ref[0] = reversed_taps(filters_ref[...])
    taps_ref[1] = filters_ref[...].astype(jnp.float32)
    for copy in copies:
        copy.wait()
    sent_products(inputs, 1 - core, keep_ref, far_ref, pair_ref, core == 0)


def tile_products(inputs, half, index):
    q_ref, k_ref, v_ref, dy_ref = inputs
    lanes = lanes_of(half, q_ref.shape[1] // 2, index)
    return product(k_ref[:, lanes], v_ref[:, lanes]), product(dy_ref[:, lanes], q_ref[:, lanes])


def wrapped_products(left, rights, masks, group):
    rows = left[0].shape[0]
    zeros = jnp.zeros_like(left[0])
    totals = [None] * len(masks)
    for at in range(0, rows, BLOCK):
        picked = jnp.concatenate(
            [
                jnp.concatenate([jnp.where(group == g, tile[at : at + BLOCK], zeros[:BLOCK]) for tile in left], axis=1)
                for g in range(LANES // GSIZE)
            ],
            axis=0,
        )
        right = jnp.concatenate(
            [
                jnp.concatenate([zeros if tile is None else turned(tile, at) for tile in tiles], axis=1)
                for tiles in rights
            ],
            axis=0,
        )
        pairs = lax.dot_general(picked, right, (((1,), (1,)), ((), ())), preferred_element_type=jnp.float32)
        for n, columns in enumerate(masks):
            for column, mask_ref in columns:
                piece = pairs[:, column * rows : (column + 1) * rows] * for_groups(mask_ref[at : at + BLOCK, :])
                totals[n] = piece if totals[n] is None else totals[n] + piece
    for total in totals:
        parts = []
        for at in range(0, total.shape[0], BLOCK):
            part = total[at : at + 8]
            for row in range(8, BLOCK, 8):
                part = part + pltpu.roll(total[at + row : at + row + 8], rows - row, 1)
            parts.append(part)
        yield jnp.concatenate(parts, axis=0)


def diagonals(sums_ref, groups):
    rows = sums_ref.shape[1]
    total = sums_ref[pl.ds(0, groups, stride=8), :]
    for r in range(1, 8):
        total = total + pltpu.roll(sums_ref[pl.ds(r, groups, stride=8), :], rows - r, 1)
    return total


def sums_at(index):
    count = LANES // GSIZE * 8
    return pl.ds(pl.multiple_of(index * count, count), count)


def two_tiles(index, sides, mask_ref, store, group):
    (left_a, right_a), (left_b, right_b) = sides(index), sides(index + 1)
    masks = [[(0, mask_ref)], [(1, mask_ref)]]
    rights = [[right_a, None], [None, right_b]]
    for n, total in enumerate(wrapped_products([left_a, left_b], rights, masks, group)):
        store(sums_at(index + n), total)


def lanes_of(half, width, index):
    return pl.ds(pl.multiple_of(half * width + index * LANES, LANES), LANES)


def filter_partner_kernel(
    q_hbm, k_hbm, v_hbm, dy_hbm, q_in, k_in, v_in, dy_in, keep_ref, masks_ref,
    q_ref, k_ref, v_ref, dy_ref, out_ref, pair_ref, far_ref, sums_ref, sems, *, scale
):
    del q_in, k_in, v_in, dy_in
    core = lax.axis_index("ctx") % 2
    inputs = (q_ref, k_ref, v_ref, dy_ref)
    copies = half_copies((q_hbm, k_hbm, v_hbm, dy_hbm), inputs, core, sems)
    for copy in copies:
        copy.start()
    group = lane_groups()

    def store(at, total):
        sums_ref[at, :] = total

    def tiles(index):
        two_tiles(2 * index, lambda i: tile_products(inputs, 1 - core, i), masks_ref.at[0], store, group)

    each_tile(tiles, q_ref.shape[1] // 4)
    out_ref[...] = diagonals(sums_ref, out_ref.shape[0]) * scale
    for copy in copies:
        copy.wait()
    sent_products(inputs, core, keep_ref, pair_ref, far_ref, core == 1)


def filter_own_kernel(q_ref, k_ref, v_ref, dy_ref, other_ref, masks_ref, sums_ref, cross_ref):
    inputs = (q_ref, k_ref, v_ref, dy_ref)
    width = q_ref.shape[1] // 2
    core = lax.axis_index("ctx") % 2
    even = core == 0
    cross_ref[...] = jnp.where(even, masks_ref[1], masks_ref[2])
    group = lane_groups()

    def tile(index):
        kv, cot = tile_products(inputs, core, index)
        other = other_ref[:, lanes_of(0, width, index)]
        left = [kv, jnp.where(even, kv, other)]
        rights = [[cot, None], [None, jnp.where(even, other, cot)]]
        for total in wrapped_products(left, rights, [[(0, masks_ref.at[0]), (1, cross_ref)]], group):
            sums_ref[sums_at(index), :] = total

    each_tile(tile, width)


def filter_far_kernel(q_ref, k_ref, v_ref, dy_ref, other_ref, masks_ref, base_ref, out_ref, total_ref, cross_ref, *, scale):
    inputs = (q_ref, k_ref, v_ref, dy_ref)
    width = q_ref.shape[1] // 2
    core = lax.axis_index("ctx") % 2
    even = core == 0
    cross_ref[...] = jnp.where(even, masks_ref[2], masks_ref[1])
    group = lane_groups()

    def sides(index):
        kv, cot = tile_products(inputs, core, index)
        other = other_ref[:, lanes_of(0, width, index)]
        return jnp.where(even, other, kv), jnp.where(even, cot, other)

    def store(at, total):
        total_ref[at, :] = base_ref[at, :] + total

    each_tile(lambda index: two_tiles(2 * index, sides, cross_ref, store, group), width // 2)
    out_ref[...] = diagonals(total_ref, out_ref.shape[0]) * scale


def conv_kernel(
    a_ref, b_ref, c_ref, d_ref, masks_ref, taps_ref, pair_ref, far_ref, *rest, backward, spans
):
    later = rest[: 2 * len(spans) - 2]
    others = [(pair_ref, far_ref), *zip(later[::2], later[1::2])]
    out_c_hbm, out_d_hbm, out_c_ref, out_d_ref, sems = rest[-5:]
    rows = a_ref.shape[0]
    per_tile = LANES // GSIZE
    half_tiles = a_ref.shape[1] // 2 // LANES
    even = lax.axis_index("ctx") % 2 == 0
    from_pair = even if backward else jnp.logical_not(even)
    group = lane_groups()
    mask_ref = masks_ref.at[1 if backward else 0]

    def table_start(row):
        start = pltpu.roll(jnp.broadcast_to(row, (BLOCK, rows)), 0, 1, stride=1, stride_axis=0).astype(jnp.bfloat16)
        return jnp.concatenate([start, start], axis=1)

    def lanes_at(index):
        return pl.ds(pl.multiple_of(index * LANES, LANES), LANES)

    def tile(index, near, distant):
        lanes = lanes_at(index)
        here = lanes_at(index % half_tiles)
        own = product(a_ref[:, lanes], b_ref[:, lanes])
        other = jnp.where(from_pair, near[:, here], distant[:, here])
        taps = taps_ref[1 if backward else 0, pl.ds(pl.multiple_of(index * per_tile, per_tile), per_tile), :]
        tables = jnp.concatenate([table_start(taps[g : g + 1]) for g in range(per_tile)], axis=0)
        for at in range(0, rows, BLOCK):
            x = jnp.concatenate([turned(own, at), turned(other, at)], axis=0)
            masked = tables * for_groups(mask_ref[at : at + BLOCK, :])
            every = jnp.dot(masked, x, preferred_element_type=jnp.float32)
            y = every[:BLOCK]
            for g in range(1, per_tile):
                y = jnp.where(group == g, every[g * BLOCK : (g + 1) * BLOCK], y)
            block = slice(at, at + BLOCK)
            out_c_ref[block, lanes] = (c_ref[block, lanes].astype(jnp.float32) * y).astype(jnp.bfloat16)
            out_d_ref[block, lanes] = (d_ref[block, lanes].astype(jnp.float32) * y).astype(jnp.bfloat16)

    def stored(start, count, sem):
        lanes = pl.ds(pl.multiple_of(start * LANES, count * LANES), count * LANES)
        return [
            pltpu.make_async_copy(out_c_ref.at[:, lanes], out_c_hbm.at[:, lanes], sems.at[0, sem]),
            pltpu.make_async_copy(out_d_ref.at[:, lanes], out_d_hbm.at[:, lanes], sems.at[1, sem]),
        ]

    bodies = []
    for (first, count), (near, distant) in zip(spans, others):
        step = math.gcd(count, STEP)

        def body(i, carry, first=first, step=step, near=near, distant=distant, sem=len(bodies)):
            for j in range(step):
                tile(first + i * step + j, near, distant)
            for copy in stored(first + i * step, step, sem + i):
                copy.start()
            return carry

        lax.fori_loop(0, count // step, body, 0)
        bodies += [(first + i * step, step) for i in range(count // step)]
    for n, (start, count) in enumerate(bodies):
        for copy in stored(start, count, n):
            copy.wait()


def local_call(kernel, name, out_shape, scratch_shapes, flops, operands, in_specs=None, out_specs=VMEM, aliases={}, moved=None):
    outs = out_shape if isinstance(out_shape, list) else [out_shape]
    if moved is None:
        moved = sum(math.prod(x.shape) * x.dtype.itemsize for x in [*operands, *outs])
    return pl.pallas_call(
        kernel,
        out_shape=out_shape,
        in_specs=in_specs or [VMEM] * len(operands),
        out_specs=out_specs,
        scratch_shapes=scratch_shapes,
        input_output_aliases=aliases,
        cost_estimate=pl.CostEstimate(flops=flops, bytes_accessed=moved, transcendentals=0),
        compiler_params=pltpu.CompilerParams(vmem_limit_bytes=24 << 20),
        name=name,
    )(*operands)


def in_hbm(*arrays):
    return [pltpu.with_memory_space_constraint(x, pltpu.HBM) for x in arrays]


def own_call(kernel, name, out_shape, scratch_shapes, hbm_operands, operands, aliases={}):
    return pl.pallas_call(
        kernel,
        out_shape=out_shape,
        in_specs=[pl.BlockSpec(memory_space=pltpu.HBM)] * len(hbm_operands) + [VMEM] * len(operands),
        out_specs=[VMEM] * len(out_shape) if isinstance(out_shape, list) else VMEM,
        scratch_shapes=scratch_shapes,
        input_output_aliases=aliases,
        cost_estimate=pl.CostEstimate(flops=0, bytes_accessed=0, transcendentals=0),
        compiler_params=pltpu.CompilerParams(vmem_limit_bytes=24 << 20),
        name=name,
    )(*in_hbm(*hbm_operands), *operands)


def first(q, k, v, dy, starts, filters):
    rows, width = q.shape
    wide = pltpu.VMEM((rows, width), jnp.bfloat16)
    sent = pltpu.VMEM((rows, width // 2), jnp.bfloat16)
    return own_call(
        first_kernel, "first",
        [wide] * 4 + [sent] * 2 + [
            pltpu.VMEM((2, rows, rows), jnp.float32),
            pltpu.VMEM((3, rows, rows), jnp.float32),
            pltpu.VMEM((2, rows, 2 * rows), jnp.bfloat16),
            pltpu.VMEM((2, *filters.shape), jnp.float32),
        ],
        [
            pltpu.VMEM(starts.shape, starts.dtype), pltpu.VMEM(filters.shape, filters.dtype),
            pltpu.SemaphoreType.DMA((10,)),
        ],
        (q, k, v, dy, starts, filters), (),
    )


def convolution(a, b, c, d, masks, taps, spans, others, outs, backward):
    rows, width = a.shape
    count = sum(tiles // math.gcd(tiles, STEP) for _, tiles in spans)
    out = jax.ShapeDtypeStruct((rows, width), jnp.bfloat16)
    whole = pltpu.VMEM((rows, width), jnp.bfloat16)
    anywhere = pl.BlockSpec(memory_space=pl.ANY)
    body = functools.partial(conv_kernel, backward=backward, spans=spans)
    operands = (a, b, c, d, masks, taps, *[x for pair in others for x in pair])
    n = len(operands)
    return local_call(
        (lambda *refs: body(*refs[:n], *refs[n + 2 :])) if outs else body,
        "backward" if backward else "forward",
        [out, out],
        [whole, whole, pltpu.SemaphoreType.DMA((2, count))],
        16 * rows * rows * width,
        operands + tuple(outs or ()),
        [VMEM] * n + [anywhere] * (2 if outs else 0),
        [anywhere] * 2,
        {n: 0, n + 1: 1} if outs else {},
    )


def other_core(block):
    return lax.ppermute(block, "ctx", [(i, i ^ 1) for i in range(lax.axis_size("ctx"))])


def next_chip(block):
    size = lax.axis_size("ctx")
    pairs = [(i, i + 1) for i in range(1, size - 1, 2)]
    return lax.ppermute(block, "ctx", pairs + [(j, i) for i, j in pairs])


def factors(size):
    found, p = [], 2
    while size > 1:
        while size % p == 0:
            found.append(p)
            size //= p
        p += 1
    return found


def rounds_over_chips():
    return [
        (axis, first * math.prod(factors(lax.axis_size(axis) // first)[:n]), p)
        for axis, first in (("dp", 1), ("ctx", 2))
        for n, p in enumerate(factors(lax.axis_size(axis) // first))
    ]


def summed_over(total, axis, stride, p):
    size = lax.axis_size(axis)
    turned = lambda i, k: i + ((i // stride + k) % p - i // stride % p) * stride
    got = [lax.ppermute(total, axis, [(turned(i, k), i) for i in range(size)]) for k in range(1, p)]
    if p == 2:
        return total + got[0]
    digit = lax.axis_index(axis) // stride % p
    return jnp.sum(jnp.roll(jnp.stack([total, *got]), digit, axis=0), axis=0)


def after(value, *others):
    return lax.optimization_barrier((value, *others))[0]


def per_device(q_proj, k_proj, v_proj, out_grad, contig_starts, filters):
    q, k, v, dy = q_proj[0], k_proj[0], v_proj[0], out_grad[0]
    rows = q.shape[0]
    groups, taps = filters.shape
    assert rows == taps == LANES and lax.axis_size("ctx") % 2 == 0
    scale = 1.0 / math.sqrt(rows * lax.axis_size("ctx") * lax.axis_size("dp") * GSIZE)
    inputs = q, k, v, dy
    *partly, far_out, pair_out, keep, masks, table_masks, tap_rows = first(*inputs, contig_starts, filters)
    square = pltpu.VMEM((rows, rows), jnp.float32)
    part = pltpu.VMEM((groups // 2, rows), jnp.float32)
    unsummed = pltpu.VMEM((groups * 4, rows), jnp.float32)
    wide = pltpu.VMEM(q.shape, q.dtype)
    sent = pltpu.VMEM((rows, q.shape[1] // 2), q.dtype)
    far = next_chip(far_out)
    later_pair = other_core(pair_out)
    q, k, v, dy, theirs, pair_out, far_out = own_call(
        functools.partial(filter_partner_kernel, scale=scale), "filter_partner",
        [wide] * 4 + [part, sent, sent], [unsummed, pltpu.SemaphoreType.DMA((8,))],
        inputs, (*partly, keep, masks), {4: 0, 5: 1, 6: 2, 7: 3},
    )
    pair = other_core(pair_out)
    mine = own_call(
        filter_own_kernel, "filter_own", unsummed, [square],
        (), (q, k, v, dy, later_pair, masks),
    )
    later_far = next_chip(after(far_out, mine))
    mine = own_call(
        functools.partial(filter_far_kernel, scale=scale), "filter_far", part, [unsummed, square],
        (), (q, k, v, dy, far, masks, mine),
    )
    mine = mine + other_core(theirs)

    half_tiles = q.shape[1] // 2 // LANES
    few = max(half_tiles // 2, 1)
    first_others, later_others = (pair, far), (later_pair, later_far)

    def forward(spans, others, outs=None):
        return convolution(k, v, q, dy, table_masks, tap_rows, spans, others, outs, False)

    def backward(spans, others, outs=None):
        return convolution(dy, q, v, k, table_masks, tap_rows, spans, others, outs, True)

    for n, place in enumerate(rounds_over_chips()):
        if n == 0:
            some_forward = forward([(0, few)], [first_others])
        if n == 1:
            mine = after(mine, *some_forward)
            some_backward = backward([(half_tiles, few)], [first_others])
        if n == 2:
            mine = after(mine, *some_backward, later_far, later_pair)
            mixed, grad_q = forward(
                [(few, half_tiles - few), (half_tiles, half_tiles)], [first_others, later_others], some_forward
            )
        if n == 3:
            mine = after(mine, mixed, grad_q)
            grad_k, grad_v = backward(
                [(half_tiles + few, half_tiles - few), (0, half_tiles)], [first_others, later_others], some_backward
            )
        mine = summed_over(mine, *place)
    mine = after(mine, grad_k, grad_v)
    halves = [mine, other_core(mine)]
    filter_grad = jnp.where(lax.axis_index("ctx") % 2 == 0, jnp.concatenate(halves), jnp.concatenate(halves[::-1]))
    return (mixed[None], grad_q[None], grad_k[None], grad_v[None], filter_grad)


def solution(mesh):
    wide = P("dp", "ctx", None)
    return jax.shard_map(
        per_device,
        mesh=mesh,
        in_specs=(wide,) * 4 + (P("dp", "ctx"), P()),
        out_specs=(wide,) * 4 + (P(),),
        check_vma=False,
    )
```

```python
import functools
import math

import jax
import jax.numpy as jnp
from jax import lax
from jax.experimental import pallas as pl
from jax.experimental.pallas import tpu as pltpu
from jax.sharding import PartitionSpec as P

GSIZE = 16
LANES = 128
BLOCK = 32
STEP = 4
VMEM = pl.BlockSpec(memory_space=pltpu.VMEM)


def product(a, b):
    return a * b


def reversed_taps(rows_of_taps):
    taps = rows_of_taps.shape[1]
    i = lax.broadcasted_iota(jnp.int32, (taps, taps), 0)
    j = lax.broadcasted_iota(jnp.int32, (taps, taps), 1)
    flip = jnp.where((i + j == 0) | (i + j == taps), 1.0, 0.0).astype(jnp.float32)
    return jnp.dot(
        rows_of_taps.astype(jnp.float32), flip,
        preferred_element_type=jnp.float32, precision=lax.Precision.HIGHEST,
    )


def lane_groups():
    return lax.broadcasted_iota(jnp.int32, (1, LANES), 1) // GSIZE


def each_tile(tile, width):
    count = width // LANES
    step = math.gcd(count, STEP)

    def body(i, carry):
        for j in range(step):
            tile(i * step + j)
        return carry

    lax.fori_loop(0, count // step, body, 0)


def aligned(mask):
    rows = mask.shape[0]
    blocks = [mask[at : at + BLOCK] for at in range(0, rows, BLOCK)]
    return jnp.concatenate(
        blocks[:1] + [pltpu.roll(block, rows - BLOCK * (i + 1), 1) for i, block in enumerate(blocks[1:])], axis=0
    )


def turned(tile, at):
    return jnp.concatenate([tile[at:], tile[:at]], axis=0) if at else tile


def for_groups(block):
    return jnp.concatenate([block] * (LANES // GSIZE), axis=0)


def half_copies(sources, targets, half, sems):
    rows, width = sources[0].shape
    lanes = pl.ds(pl.multiple_of(half * (width // 2), width // 2), width // 2)
    copies = []
    for n in range(2):
        part = pl.ds(n * (rows // 2), rows // 2)
        for source, target in zip(sources, targets):
            copies.append(
                pltpu.make_async_copy(source.at[part, lanes], target.at[part, lanes], sems.at[len(copies)])
            )
    return copies


def sent_products(inputs, half, keep_ref, kv_out, cot_out, swapped):
    q_ref, k_ref, v_ref, dy_ref = inputs
    width = kv_out.shape[1]
    lanes = pl.ds(pl.multiple_of(half * width, width), width)
    kv = product(k_ref[:, lanes], v_ref[:, lanes])
    cot = product(dy_ref[:, lanes], q_ref[:, lanes])
    kv = jnp.where(keep_ref[1][:, :1] > 0, kv, jnp.zeros_like(kv))
    cot = jnp.where(keep_ref[0][:, :1] > 0, cot, jnp.zeros_like(cot))
    kv_out[...] = jnp.where(swapped, cot, kv)
    cot_out[...] = jnp.where(swapped, kv, cot)


def first_kernel(
    q_hbm, k_hbm, v_hbm, dy_hbm, starts_hbm, filters_hbm,
    q_ref, k_ref, v_ref, dy_ref, far_ref, pair_ref, keep_ref, masks_ref, table_masks_ref, taps_ref,
    starts_ref, filters_ref, sems,
):
    rows = q_ref.shape[0]
    core = lax.axis_index("ctx") % 2
    small = [
        pltpu.make_async_copy(starts_hbm, starts_ref, sems.at[8]),
        pltpu.make_async_copy(filters_hbm, filters_ref, sems.at[9]),
    ]
    inputs = (q_ref, k_ref, v_ref, dy_ref)
    copies = half_copies((q_hbm, k_hbm, v_hbm, dy_hbm), inputs, 1 - core, sems)
    for copy in small + copies:
        copy.start()

    small[0].wait()
    starts = jnp.broadcast_to(starts_ref[...], (rows, rows)) > 0
    t = lax.broadcasted_iota(jnp.int32, (rows, rows), 0)
    s = lax.broadcasted_iota(jnp.int32, (rows, rows), 1)
    began = jnp.max(jnp.where(starts & (s <= t), s, 0), axis=1, keepdims=True)
    first = jnp.min(jnp.where(starts, s, rows), axis=1, keepdims=True)
    last = jnp.max(jnp.where(starts, s, 0), axis=1, keepdims=True)
    as_f32 = lambda mask: jnp.where(mask, 1.0, 0.0).astype(jnp.float32)
    own = as_f32((s <= t) & (s >= began))
    previous = as_f32((s > t) & (t < first))
    following = as_f32((s < t) & (t >= last))
    keep_ref[0] = as_f32(t < first)
    keep_ref[1] = as_f32(t >= last)
    for n, parts in enumerate(((own, previous), (own.T, following))):
        for m, mask in enumerate(parts):
            table_masks_ref[n, :, m * rows : (m + 1) * rows] = aligned(mask).astype(jnp.bfloat16)
    for n, mask in enumerate((own.T, following, previous.T)):
        masks_ref[n] = aligned(mask)
    small[1].wait()
    taps_ref[0] = reversed_taps(filters_ref[...])
    taps_ref[1] = filters_ref[...].astype(jnp.float32)
    for copy in copies:
        copy.wait()
    sent_products(inputs, 1 - core, keep_ref, far_ref, pair_ref, core == 0)


def tile_products(inputs, half, index):
    q_ref, k_ref, v_ref, dy_ref = inputs
    lanes = lanes_of(half, q_ref.shape[1] // 2, index)
    return product(k_ref[:, lanes], v_ref[:, lanes]), product(dy_ref[:, lanes], q_ref[:, lanes])


def wrapped_products(left, rights, masks, group):
    rows = left[0].shape[0]
    zeros = jnp.zeros_like(left[0])
    totals = [None] * len(masks)
    for at in range(0, rows, BLOCK):
        picked = jnp.concatenate(
            [
                jnp.concatenate([jnp.where(group == g, tile[at : at + BLOCK], zeros[:BLOCK]) for tile in left], axis=1)
                for g in range(LANES // GSIZE)
            ],
            axis=0,
        )
        right = jnp.concatenate(
            [
                jnp.concatenate([zeros if tile is None else turned(tile, at) for tile in tiles], axis=1)
                for tiles in rights
            ],
            axis=0,
        )
        pairs = lax.dot_general(picked, right, (((1,), (1,)), ((), ())), preferred_element_type=jnp.float32)
        for n, columns in enumerate(masks):
            for column, mask_ref in columns:
                piece = pairs[:, column * rows : (column + 1) * rows] * for_groups(mask_ref[at : at + BLOCK, :])
                totals[n] = piece if totals[n] is None else totals[n] + piece
    for total in totals:
        parts = []
        for at in range(0, total.shape[0], BLOCK):
            part = total[at : at + 8]
            for row in range(8, BLOCK, 8):
                part = part + pltpu.roll(total[at + row : at + row + 8], rows - row, 1)
            parts.append(part)
        yield jnp.concatenate(parts, axis=0)


def diagonals(sums_ref, groups):
    rows = sums_ref.shape[1]
    total = sums_ref[pl.ds(0, groups, stride=8), :]
    for r in range(1, 8):
        total = total + pltpu.roll(sums_ref[pl.ds(r, groups, stride=8), :], rows - r, 1)
    return total


def sums_at(index):
    count = LANES // GSIZE * 8
    return pl.ds(pl.multiple_of(index * count, count), count)


def two_tiles(index, sides, mask_ref, store, group):
    (left_a, right_a), (left_b, right_b) = sides(index), sides(index + 1)
    masks = [[(0, mask_ref)], [(1, mask_ref)]]
    rights = [[right_a, None], [None, right_b]]
    for n, total in enumerate(wrapped_products([left_a, left_b], rights, masks, group)):
        store(sums_at(index + n), total)


def lanes_of(half, width, index):
    return pl.ds(pl.multiple_of(half * width + index * LANES, LANES), LANES)


def filter_partner_kernel(
    q_hbm, k_hbm, v_hbm, dy_hbm, q_in, k_in, v_in, dy_in, keep_ref, masks_ref,
    q_ref, k_ref, v_ref, dy_ref, out_ref, pair_ref, far_ref, sums_ref, sems, *, scale
):
    del q_in, k_in, v_in, dy_in
    core = lax.axis_index("ctx") % 2
    inputs = (q_ref, k_ref, v_ref, dy_ref)
    copies = half_copies((q_hbm, k_hbm, v_hbm, dy_hbm), inputs, core, sems)
    for copy in copies:
        copy.start()
    group = lane_groups()

    def store(at, total):
        sums_ref[at, :] = total

    def tiles(index):
        two_tiles(2 * index, lambda i: tile_products(inputs, 1 - core, i), masks_ref.at[0], store, group)

    each_tile(tiles, q_ref.shape[1] // 4)
    out_ref[...] = diagonals(sums_ref, out_ref.shape[0]) * scale
    for copy in copies:
        copy.wait()
    sent_products(inputs, core, keep_ref, pair_ref, far_ref, core == 1)


def filter_own_kernel(q_ref, k_ref, v_ref, dy_ref, other_ref, masks_ref, sums_ref, cross_ref):
    inputs = (q_ref, k_ref, v_ref, dy_ref)
    width = q_ref.shape[1] // 2
    core = lax.axis_index("ctx") % 2
    even = core == 0
    cross_ref[...] = jnp.where(even, masks_ref[1], masks_ref[2])
    group = lane_groups()

    def tile(index):
        kv, cot = tile_products(inputs, core, index)
        other = other_ref[:, lanes_of(0, width, index)]
        left = [kv, jnp.where(even, kv, other)]
        rights = [[cot, None], [None, jnp.where(even, other, cot)]]
        for total in wrapped_products(left, rights, [[(0, masks_ref.at[0]), (1, cross_ref)]], group):
            sums_ref[sums_at(index), :] = total

    each_tile(tile, width)


def filter_far_kernel(q_ref, k_ref, v_ref, dy_ref, other_ref, masks_ref, base_ref, out_ref, total_ref, cross_ref, *, scale):
    inputs = (q_ref, k_ref, v_ref, dy_ref)
    width = q_ref.shape[1] // 2
    core = lax.axis_index("ctx") % 2
    even = core == 0
    cross_ref[...] = jnp.where(even, masks_ref[2], masks_ref[1])
    group = lane_groups()

    def sides(index):
        kv, cot = tile_products(inputs, core, index)
        other = other_ref[:, lanes_of(0, width, index)]
        return jnp.where(even, other, kv), jnp.where(even, cot, other)

    def store(at, total):
        total_ref[at, :] = base_ref[at, :] + total

    each_tile(lambda index: two_tiles(2 * index, sides, cross_ref, store, group), width // 2)
    out_ref[...] = diagonals(total_ref, out_ref.shape[0]) * scale


def conv_kernel(
    a_ref, b_ref, c_ref, d_ref, masks_ref, taps_ref, pair_ref, far_ref, *rest, backward, spans
):
    later = rest[: 2 * len(spans) - 2]
    others = [(pair_ref, far_ref), *zip(later[::2], later[1::2])]
    out_c_hbm, out_d_hbm, out_c_ref, out_d_ref, sems = rest[-5:]
    rows = a_ref.shape[0]
    per_tile = LANES // GSIZE
    half_tiles = a_ref.shape[1] // 2 // LANES
    even = lax.axis_index("ctx") % 2 == 0
    from_pair = even if backward else jnp.logical_not(even)
    group = lane_groups()
    mask_ref = masks_ref.at[1 if backward else 0]

    def table_start(row):
        start = pltpu.roll(jnp.broadcast_to(row, (BLOCK, rows)), 0, 1, stride=1, stride_axis=0).astype(jnp.bfloat16)
        return jnp.concatenate([start, start], axis=1)

    def lanes_at(index):
        return pl.ds(pl.multiple_of(index * LANES, LANES), LANES)

    def tile(index, near, distant):
        lanes = lanes_at(index)
        here = lanes_at(index % half_tiles)
        own = product(a_ref[:, lanes], b_ref[:, lanes])
        other = jnp.where(from_pair, near[:, here], distant[:, here])
        taps = taps_ref[1 if backward else 0, pl.ds(pl.multiple_of(index * per_tile, per_tile), per_tile), :]
        tables = jnp.concatenate([table_start(taps[g : g + 1]) for g in range(per_tile)], axis=0)
        for at in range(0, rows, BLOCK):
            x = jnp.concatenate([turned(own, at), turned(other, at)], axis=0)
            masked = tables * for_groups(mask_ref[at : at + BLOCK, :])
            every = jnp.dot(masked, x, preferred_element_type=jnp.float32)
            y = every[:BLOCK]
            for g in range(1, per_tile):
                y = jnp.where(group == g, every[g * BLOCK : (g + 1) * BLOCK], y)
            block = slice(at, at + BLOCK)
            out_c_ref[block, lanes] = (c_ref[block, lanes].astype(jnp.float32) * y).astype(jnp.bfloat16)
            out_d_ref[block, lanes] = (d_ref[block, lanes].astype(jnp.float32) * y).astype(jnp.bfloat16)

    def stored(start, count, sem):
        lanes = pl.ds(pl.multiple_of(start * LANES, count * LANES), count * LANES)
        return [
            pltpu.make_async_copy(out_c_ref.at[:, lanes], out_c_hbm.at[:, lanes], sems.at[0, sem]),
            pltpu.make_async_copy(out_d_ref.at[:, lanes], out_d_hbm.at[:, lanes], sems.at[1, sem]),
        ]

    bodies = []
    for (first, count), (near, distant) in zip(spans, others):
        step = math.gcd(count, STEP)

        def body(i, carry, first=first, step=step, near=near, distant=distant, sem=len(bodies)):
            for j in range(step):
                tile(first + i * step + j, near, distant)
            for copy in stored(first + i * step, step, sem + i):
                copy.start()
            return carry

        lax.fori_loop(0, count // step, body, 0)
        bodies += [(first + i * step, step) for i in range(count // step)]
    for n, (start, count) in enumerate(bodies):
        for copy in stored(start, count, n):
            copy.wait()


def local_call(kernel, name, out_shape, scratch_shapes, flops, operands, in_specs=None, out_specs=VMEM, aliases={}, moved=None):
    outs = out_shape if isinstance(out_shape, list) else [out_shape]
    if moved is None:
        moved = sum(math.prod(x.shape) * x.dtype.itemsize for x in [*operands, *outs])
    return pl.pallas_call(
        kernel,
        out_shape=out_shape,
        in_specs=in_specs or [VMEM] * len(operands),
        out_specs=out_specs,
        scratch_shapes=scratch_shapes,
        input_output_aliases=aliases,
        cost_estimate=pl.CostEstimate(flops=flops, bytes_accessed=moved, transcendentals=0),
        compiler_params=pltpu.CompilerParams(vmem_limit_bytes=24 << 20),
        name=name,
    )(*operands)


def in_hbm(*arrays):
    return [pltpu.with_memory_space_constraint(x, pltpu.HBM) for x in arrays]


def own_call(kernel, name, out_shape, scratch_shapes, hbm_operands, operands, aliases={}):
    return pl.pallas_call(
        kernel,
        out_shape=out_shape,
        in_specs=[pl.BlockSpec(memory_space=pltpu.HBM)] * len(hbm_operands) + [VMEM] * len(operands),
        out_specs=[VMEM] * len(out_shape) if isinstance(out_shape, list) else VMEM,
        scratch_shapes=scratch_shapes,
        input_output_aliases=aliases,
        cost_estimate=pl.CostEstimate(flops=0, bytes_accessed=0, transcendentals=0),
        compiler_params=pltpu.CompilerParams(vmem_limit_bytes=24 << 20),
        name=name,
    )(*in_hbm(*hbm_operands), *operands)


def first(q, k, v, dy, starts, filters):
    rows, width = q.shape
    wide = pltpu.VMEM((rows, width), jnp.bfloat16)
    sent = pltpu.VMEM((rows, width // 2), jnp.bfloat16)
    return own_call(
        first_kernel, "first",
        [wide] * 4 + [sent] * 2 + [
            pltpu.VMEM((2, rows, rows), jnp.float32),
            pltpu.VMEM((3, rows, rows), jnp.float32),
            pltpu.VMEM((2, rows, 2 * rows), jnp.bfloat16),
            pltpu.VMEM((2, *filters.shape), jnp.float32),
        ],
        [
            pltpu.VMEM(starts.shape, starts.dtype), pltpu.VMEM(filters.shape, filters.dtype),
            pltpu.SemaphoreType.DMA((10,)),
        ],
        (q, k, v, dy, starts, filters), (),
    )


def convolution(a, b, c, d, masks, taps, spans, others, outs, backward):
    rows, width = a.shape
    count = sum(tiles // math.gcd(tiles, STEP) for _, tiles in spans)
    out = jax.ShapeDtypeStruct((rows, width), jnp.bfloat16)
    whole = pltpu.VMEM((rows, width), jnp.bfloat16)
    anywhere = pl.BlockSpec(memory_space=pl.ANY)
    body = functools.partial(conv_kernel, backward=backward, spans=spans)
    operands = (a, b, c, d, masks, taps, *[x for pair in others for x in pair])
    n = len(operands)
    return local_call(
        (lambda *refs: body(*refs[:n], *refs[n + 2 :])) if outs else body,
        "backward" if backward else "forward",
        [out, out],
        [whole, whole, pltpu.SemaphoreType.DMA((2, count))],
        16 * rows * rows * width,
        operands + tuple(outs or ()),
        [VMEM] * n + [anywhere] * (2 if outs else 0),
        [anywhere] * 2,
        {n: 0, n + 1: 1} if outs else {},
    )


def other_core(block):
    return lax.ppermute(block, "ctx", [(i, i ^ 1) for i in range(lax.axis_size("ctx"))])


def next_chip(block):
    size = lax.axis_size("ctx")
    pairs = [(i, i + 1) for i in range(1, size - 1, 2)]
    return lax.ppermute(block, "ctx", pairs + [(j, i) for i, j in pairs])


def factors(size):
    found, p = [], 2
    while size > 1:
        while size % p == 0:
            found.append(p)
            size //= p
        p += 1
    return found


def rounds_over_chips():
    return [
        (axis, first * math.prod(factors(lax.axis_size(axis) // first)[:n]), p)
        for axis, first in (("dp", 1), ("ctx", 2))
        for n, p in enumerate(factors(lax.axis_size(axis) // first))
    ]


def summed_over(total, axis, stride, p):
    size = lax.axis_size(axis)
    turned = lambda i, k: i + ((i // stride + k) % p - i // stride % p) * stride
    got = [lax.ppermute(total, axis, [(turned(i, k), i) for i in range(size)]) for k in range(1, p)]
    if p == 2:
        return total + got[0]
    digit = lax.axis_index(axis) // stride % p
    return jnp.sum(jnp.roll(jnp.stack([total, *got]), digit, axis=0), axis=0)


def after(value, *others):
    return lax.optimization_barrier((value, *others))[0]


def per_device(q_proj, k_proj, v_proj, out_grad, contig_starts, filters):
    q, k, v, dy = q_proj[0], k_proj[0], v_proj[0], out_grad[0]
    rows = q.shape[0]
    groups, taps = filters.shape
    assert rows == taps == LANES and lax.axis_size("ctx") % 2 == 0
    scale = 1.0 / math.sqrt(rows * lax.axis_size("ctx") * lax.axis_size("dp") * GSIZE)
    inputs = q, k, v, dy
    *partly, far_out, pair_out, keep, masks, table_masks, tap_rows = first(*inputs, contig_starts, filters)
    square = pltpu.VMEM((rows, rows), jnp.float32)
    part = pltpu.VMEM((groups // 2, rows), jnp.float32)
    unsummed = pltpu.VMEM((groups * 4, rows), jnp.float32)
    wide = pltpu.VMEM(q.shape, q.dtype)
    sent = pltpu.VMEM((rows, q.shape[1] // 2), q.dtype)
    far = next_chip(far_out)
    later_pair = other_core(pair_out)
    q, k, v, dy, theirs, pair_out, far_out = own_call(
        functools.partial(filter_partner_kernel, scale=scale), "filter_partner",
        [wide] * 4 + [part, sent, sent], [unsummed, pltpu.SemaphoreType.DMA((8,))],
        inputs, (*partly, keep, masks), {4: 0, 5: 1, 6: 2, 7: 3},
    )
    pair = other_core(pair_out)
    mine = own_call(
        filter_own_kernel, "filter_own", unsummed, [square],
        (), (q, k, v, dy, later_pair, masks),
    )
    later_far = next_chip(after(far_out, mine))
    mine = own_call(
        functools.partial(filter_far_kernel, scale=scale), "filter_far", part, [unsummed, square],
        (), (q, k, v, dy, far, masks, mine),
    )
    mine = mine + other_core(theirs)

    half_tiles = q.shape[1] // 2 // LANES
    first_others, later_others = (pair, far), (later_pair, later_far)

    def forward(spans, others, outs=None):
        return convolution(k, v, q, dy, table_masks, tap_rows, spans, others, outs, False)

    def backward(spans, others, outs=None):
        return convolution(dy, q, v, k, table_masks, tap_rows, spans, others, outs, True)

    for n, place in enumerate(rounds_over_chips()):
        if n == 0:
            some_forward = forward([(0, half_tiles)], [first_others])
        if n == 1:
            mine = after(mine, *some_forward)
            some_backward = backward([(half_tiles, half_tiles)], [first_others])
        if n == 2:
            mine = after(mine, *some_backward, later_far, later_pair)
            mixed, grad_q = forward([(half_tiles, half_tiles)], [later_others], some_forward)
        if n == 3:
            mine = after(mine, mixed, grad_q)
            grad_k, grad_v = backward([(0, half_tiles)], [later_others], some_backward)
        mine = summed_over(mine, *place)
    mine = after(mine, grad_k, grad_v)
    halves = [mine, other_core(mine)]
    filter_grad = jnp.where(lax.axis_index("ctx") % 2 == 0, jnp.concatenate(halves), jnp.concatenate(halves[::-1]))
    return (mixed[None], grad_q[None], grad_k[None], grad_v[None], filter_grad)


def solution(mesh):
    wide = P("dp", "ctx", None)
    return jax.shard_map(
        per_device,
        mesh=mesh,
        in_specs=(wide,) * 4 + (P("dp", "ctx"), P()),
        out_specs=(wide,) * 4 + (P(),),
        check_vma=False,
    )
```

```python
import functools
import math

import jax
import jax.numpy as jnp
from jax import lax
from jax.experimental import pallas as pl
from jax.experimental.pallas import tpu as pltpu
from jax.sharding import PartitionSpec as P

GSIZE = 16
LANES = 128
BLOCK = 32
STEP = 4
VMEM = pl.BlockSpec(memory_space=pltpu.VMEM)


def product(a, b):
    return a * b


def reversed_taps(rows_of_taps):
    taps = rows_of_taps.shape[1]
    i = lax.broadcasted_iota(jnp.int32, (taps, taps), 0)
    j = lax.broadcasted_iota(jnp.int32, (taps, taps), 1)
    flip = jnp.where((i + j == 0) | (i + j == taps), 1.0, 0.0).astype(jnp.float32)
    return jnp.dot(
        rows_of_taps.astype(jnp.float32), flip,
        preferred_element_type=jnp.float32, precision=lax.Precision.HIGHEST,
    )


def lane_groups():
    return lax.broadcasted_iota(jnp.int32, (1, LANES), 1) // GSIZE


def each_tile(tile, width):
    count = width // LANES
    step = math.gcd(count, STEP)

    def body(i, carry):
        for j in range(step):
            tile(i * step + j)
        return carry

    lax.fori_loop(0, count // step, body, 0)


def aligned(mask):
    rows = mask.shape[0]
    blocks = [mask[at : at + BLOCK] for at in range(0, rows, BLOCK)]
    return jnp.concatenate(
        blocks[:1] + [pltpu.roll(block, rows - BLOCK * (i + 1), 1) for i, block in enumerate(blocks[1:])], axis=0
    )


def turned(tile, at):
    return jnp.concatenate([tile[at:], tile[:at]], axis=0) if at else tile


def for_groups(block):
    return jnp.concatenate([block] * (LANES // GSIZE), axis=0)


def half_copies(sources, targets, half, sems):
    rows, width = sources[0].shape
    lanes = pl.ds(pl.multiple_of(half * (width // 2), width // 2), width // 2)
    copies = []
    for n in range(2):
        part = pl.ds(n * (rows // 2), rows // 2)
        for source, target in zip(sources, targets):
            copies.append(
                pltpu.make_async_copy(source.at[part, lanes], target.at[part, lanes], sems.at[len(copies)])
            )
    return copies


def sent_products(inputs, half, keep_ref, kv_out, cot_out, swapped):
    q_ref, k_ref, v_ref, dy_ref = inputs
    width = kv_out.shape[1]
    lanes = pl.ds(pl.multiple_of(half * width, width), width)
    kv = product(k_ref[:, lanes], v_ref[:, lanes])
    cot = product(dy_ref[:, lanes], q_ref[:, lanes])
    kv = jnp.where(keep_ref[1][:, :1] > 0, kv, jnp.zeros_like(kv))
    cot = jnp.where(keep_ref[0][:, :1] > 0, cot, jnp.zeros_like(cot))
    kv_out[...] = jnp.where(swapped, cot, kv)
    cot_out[...] = jnp.where(swapped, kv, cot)


def first_kernel(
    q_hbm, k_hbm, v_hbm, dy_hbm, starts_hbm,
    q_ref, k_ref, v_ref, dy_ref, far_ref, pair_ref, keep_ref, starts_ref, sems,
):
    rows = q_ref.shape[0]
    core = lax.axis_index("ctx") % 2
    inputs = (q_ref, k_ref, v_ref, dy_ref)
    flags = pltpu.make_async_copy(starts_hbm, starts_ref, sems.at[8])
    copies = half_copies((q_hbm, k_hbm, v_hbm, dy_hbm), inputs, 1 - core, sems)
    for copy in [flags, *copies]:
        copy.start()
    flags.wait()
    starts = jnp.broadcast_to(starts_ref[...], (rows, rows)) > 0
    t = lax.broadcasted_iota(jnp.int32, (rows, rows), 0)
    s = lax.broadcasted_iota(jnp.int32, (rows, rows), 1)
    keep_ref[0] = as_f32(t < jnp.min(jnp.where(starts, s, rows), axis=1, keepdims=True))
    keep_ref[1] = as_f32(t >= jnp.max(jnp.where(starts, s, 0), axis=1, keepdims=True))
    for copy in copies:
        copy.wait()
    sent_products(inputs, 1 - core, keep_ref, far_ref, pair_ref, core == 0)


def as_f32(mask):
    return jnp.where(mask, 1.0, 0.0).astype(jnp.float32)


def make_masks(starts_ref, keep_ref, masks_ref, table_masks_ref):
    rows = starts_ref.shape[1]
    starts = jnp.broadcast_to(starts_ref[...], (rows, rows)) > 0
    t = lax.broadcasted_iota(jnp.int32, (rows, rows), 0)
    s = lax.broadcasted_iota(jnp.int32, (rows, rows), 1)
    began = jnp.max(jnp.where(starts & (s <= t), s, 0), axis=1, keepdims=True)
    own = as_f32((s <= t) & (s >= began))
    previous = jnp.where(s > t, keep_ref[0], 0.0)
    following = jnp.where(s < t, keep_ref[1], 0.0)
    for n, parts in enumerate(((own, previous), (own.T, following))):
        for m, mask in enumerate(parts):
            table_masks_ref[n, :, m * rows : (m + 1) * rows] = aligned(mask).astype(jnp.bfloat16)
    for n, mask in enumerate((own.T, following, previous.T)):
        masks_ref[n] = aligned(mask)


def tile_products(inputs, half, index):
    q_ref, k_ref, v_ref, dy_ref = inputs
    lanes = lanes_of(half, q_ref.shape[1] // 2, index)
    return product(k_ref[:, lanes], v_ref[:, lanes]), product(dy_ref[:, lanes], q_ref[:, lanes])


def wrapped_products(left, rights, masks, group):
    rows = left[0].shape[0]
    zeros = jnp.zeros_like(left[0])
    totals = [None] * len(masks)
    for at in range(0, rows, BLOCK):
        picked = jnp.concatenate(
            [
                jnp.concatenate([jnp.where(group == g, tile[at : at + BLOCK], zeros[:BLOCK]) for tile in left], axis=1)
                for g in range(LANES // GSIZE)
            ],
            axis=0,
        )
        right = jnp.concatenate(
            [
                jnp.concatenate([zeros if tile is None else turned(tile, at) for tile in tiles], axis=1)
                for tiles in rights
            ],
            axis=0,
        )
        pairs = lax.dot_general(picked, right, (((1,), (1,)), ((), ())), preferred_element_type=jnp.float32)
        for n, columns in enumerate(masks):
            for column, mask_ref in columns:
                piece = pairs[:, column * rows : (column + 1) * rows] * for_groups(mask_ref[at : at + BLOCK, :])
                totals[n] = piece if totals[n] is None else totals[n] + piece
    for total in totals:
        parts = []
        for at in range(0, total.shape[0], BLOCK):
            part = total[at : at + 8]
            for row in range(8, BLOCK, 8):
                part = part + pltpu.roll(total[at + row : at + row + 8], rows - row, 1)
            parts.append(part)
        yield jnp.concatenate(parts, axis=0)


def diagonals(sums_ref, groups):
    rows = sums_ref.shape[1]
    total = sums_ref[pl.ds(0, groups, stride=8), :]
    for r in range(1, 8):
        total = total + pltpu.roll(sums_ref[pl.ds(r, groups, stride=8), :], rows - r, 1)
    return total


def sums_at(index):
    count = LANES // GSIZE * 8
    return pl.ds(pl.multiple_of(index * count, count), count)


def two_tiles(index, sides, mask_ref, store, group):
    (left_a, right_a), (left_b, right_b) = sides(index), sides(index + 1)
    masks = [[(0, mask_ref)], [(1, mask_ref)]]
    rights = [[right_a, None], [None, right_b]]
    for n, total in enumerate(wrapped_products([left_a, left_b], rights, masks, group)):
        store(sums_at(index + n), total)


def lanes_of(half, width, index):
    return pl.ds(pl.multiple_of(half * width + index * LANES, LANES), LANES)


def filter_partner_kernel(
    q_hbm, k_hbm, v_hbm, dy_hbm, filters_hbm, q_in, k_in, v_in, dy_in, keep_ref, starts_ref,
    q_ref, k_ref, v_ref, dy_ref, out_ref, pair_ref, far_ref, masks_ref, table_masks_ref, taps_ref,
    sums_ref, filters_ref, sems, *, scale
):
    del q_in, k_in, v_in, dy_in
    core = lax.axis_index("ctx") % 2
    inputs = (q_ref, k_ref, v_ref, dy_ref)
    copies = half_copies((q_hbm, k_hbm, v_hbm, dy_hbm), inputs, core, sems)
    copies.append(pltpu.make_async_copy(filters_hbm, filters_ref, sems.at[8]))
    for copy in copies:
        copy.start()
    make_masks(starts_ref, keep_ref, masks_ref, table_masks_ref)
    group = lane_groups()

    def store(at, total):
        sums_ref[at, :] = total

    def tiles(index):
        two_tiles(2 * index, lambda i: tile_products(inputs, 1 - core, i), masks_ref.at[0], store, group)

    each_tile(tiles, q_ref.shape[1] // 4)
    out_ref[...] = diagonals(sums_ref, out_ref.shape[0]) * scale
    for copy in copies:
        copy.wait()
    taps_ref[0] = reversed_taps(filters_ref[...])
    taps_ref[1] = filters_ref[...].astype(jnp.float32)
    sent_products(inputs, core, keep_ref, pair_ref, far_ref, core == 1)


def filter_own_kernel(q_ref, k_ref, v_ref, dy_ref, other_ref, masks_ref, sums_ref, cross_ref):
    inputs = (q_ref, k_ref, v_ref, dy_ref)
    width = q_ref.shape[1] // 2
    core = lax.axis_index("ctx") % 2
    even = core == 0
    cross_ref[...] = jnp.where(even, masks_ref[1], masks_ref[2])
    group = lane_groups()

    def tile(index):
        kv, cot = tile_products(inputs, core, index)
        other = other_ref[:, lanes_of(0, width, index)]
        left = [kv, jnp.where(even, kv, other)]
        rights = [[cot, None], [None, jnp.where(even, other, cot)]]
        for total in wrapped_products(left, rights, [[(0, masks_ref.at[0]), (1, cross_ref)]], group):
            sums_ref[sums_at(index), :] = total

    each_tile(tile, width)


def filter_far_kernel(q_ref, k_ref, v_ref, dy_ref, other_ref, masks_ref, base_ref, out_ref, total_ref, cross_ref, *, scale):
    inputs = (q_ref, k_ref, v_ref, dy_ref)
    width = q_ref.shape[1] // 2
    core = lax.axis_index("ctx") % 2
    even = core == 0
    cross_ref[...] = jnp.where(even, masks_ref[2], masks_ref[1])
    group = lane_groups()

    def sides(index):
        kv, cot = tile_products(inputs, core, index)
        other = other_ref[:, lanes_of(0, width, index)]
        return jnp.where(even, other, kv), jnp.where(even, cot, other)

    def store(at, total):
        total_ref[at, :] = base_ref[at, :] + total

    each_tile(lambda index: two_tiles(2 * index, sides, cross_ref, store, group), width // 2)
    out_ref[...] = diagonals(total_ref, out_ref.shape[0]) * scale


def conv_kernel(
    a_ref, b_ref, c_ref, d_ref, masks_ref, taps_ref, pair_ref, far_ref, *rest, backward, spans
):
    later = rest[: 2 * len(spans) - 2]
    others = [(pair_ref, far_ref), *zip(later[::2], later[1::2])]
    out_c_hbm, out_d_hbm, out_c_ref, out_d_ref, sems = rest[-5:]
    rows = a_ref.shape[0]
    per_tile = LANES // GSIZE
    half_tiles = a_ref.shape[1] // 2 // LANES
    even = lax.axis_index("ctx") % 2 == 0
    from_pair = even if backward else jnp.logical_not(even)
    group = lane_groups()
    mask_ref = masks_ref.at[1 if backward else 0]

    def table_start(row):
        start = pltpu.roll(jnp.broadcast_to(row, (BLOCK, rows)), 0, 1, stride=1, stride_axis=0).astype(jnp.bfloat16)
        return jnp.concatenate([start, start], axis=1)

    def lanes_at(index):
        return pl.ds(pl.multiple_of(index * LANES, LANES), LANES)

    def tile(index, near, distant):
        lanes = lanes_at(index)
        here = lanes_at(index % half_tiles)
        own = product(a_ref[:, lanes], b_ref[:, lanes])
        other = jnp.where(from_pair, near[:, here], distant[:, here])
        taps = taps_ref[1 if backward else 0, pl.ds(pl.multiple_of(index * per_tile, per_tile), per_tile), :]
        tables = jnp.concatenate([table_start(taps[g : g + 1]) for g in range(per_tile)], axis=0)
        for at in range(0, rows, BLOCK):
            x = jnp.concatenate([turned(own, at), turned(other, at)], axis=0)
            masked = tables * for_groups(mask_ref[at : at + BLOCK, :])
            every = jnp.dot(masked, x, preferred_element_type=jnp.float32)
            y = every[:BLOCK]
            for g in range(1, per_tile):
                y = jnp.where(group == g, every[g * BLOCK : (g + 1) * BLOCK], y)
            block = slice(at, at + BLOCK)
            out_c_ref[block, lanes] = (c_ref[block, lanes].astype(jnp.float32) * y).astype(jnp.bfloat16)
            out_d_ref[block, lanes] = (d_ref[block, lanes].astype(jnp.float32) * y).astype(jnp.bfloat16)

    def stored(start, count, sem):
        lanes = pl.ds(pl.multiple_of(start * LANES, count * LANES), count * LANES)
        return [
            pltpu.make_async_copy(out_c_ref.at[:, lanes], out_c_hbm.at[:, lanes], sems.at[0, sem]),
            pltpu.make_async_copy(out_d_ref.at[:, lanes], out_d_hbm.at[:, lanes], sems.at[1, sem]),
        ]

    bodies = []
    for (first, count), (near, distant) in zip(spans, others):
        step = math.gcd(count, STEP)

        def body(i, carry, first=first, step=step, near=near, distant=distant, sem=len(bodies)):
            for j in range(step):
                tile(first + i * step + j, near, distant)
            for copy in stored(first + i * step, step, sem + i):
                copy.start()
            return carry

        lax.fori_loop(0, count // step, body, 0)
        bodies += [(first + i * step, step) for i in range(count // step)]
    for n, (start, count) in enumerate(bodies):
        for copy in stored(start, count, n):
            copy.wait()


def local_call(kernel, name, out_shape, scratch_shapes, flops, operands, in_specs=None, out_specs=VMEM, aliases={}, moved=None):
    outs = out_shape if isinstance(out_shape, list) else [out_shape]
    if moved is None:
        moved = sum(math.prod(x.shape) * x.dtype.itemsize for x in [*operands, *outs])
    return pl.pallas_call(
        kernel,
        out_shape=out_shape,
        in_specs=in_specs or [VMEM] * len(operands),
        out_specs=out_specs,
        scratch_shapes=scratch_shapes,
        input_output_aliases=aliases,
        cost_estimate=pl.CostEstimate(flops=flops, bytes_accessed=moved, transcendentals=0),
        compiler_params=pltpu.CompilerParams(vmem_limit_bytes=24 << 20),
        name=name,
    )(*operands)


def in_hbm(*arrays):
    return [pltpu.with_memory_space_constraint(x, pltpu.HBM) for x in arrays]


def own_call(kernel, name, out_shape, scratch_shapes, hbm_operands, operands, aliases={}):
    return pl.pallas_call(
        kernel,
        out_shape=out_shape,
        in_specs=[pl.BlockSpec(memory_space=pltpu.HBM)] * len(hbm_operands) + [VMEM] * len(operands),
        out_specs=[VMEM] * len(out_shape) if isinstance(out_shape, list) else VMEM,
        scratch_shapes=scratch_shapes,
        input_output_aliases=aliases,
        cost_estimate=pl.CostEstimate(flops=0, bytes_accessed=0, transcendentals=0),
        compiler_params=pltpu.CompilerParams(vmem_limit_bytes=24 << 20),
        name=name,
    )(*in_hbm(*hbm_operands), *operands)


def first(q, k, v, dy, starts):
    rows, width = q.shape
    wide = pltpu.VMEM((rows, width), jnp.bfloat16)
    sent = pltpu.VMEM((rows, width // 2), jnp.bfloat16)
    return own_call(
        first_kernel, "first",
        [wide] * 4 + [sent] * 2 + [pltpu.VMEM((2, rows, rows), jnp.float32), pltpu.VMEM(starts.shape, starts.dtype)],
        [pltpu.SemaphoreType.DMA((9,))],
        (q, k, v, dy, starts), (),
    )


def convolution(a, b, c, d, masks, taps, spans, others, outs, backward):
    rows, width = a.shape
    count = sum(tiles // math.gcd(tiles, STEP) for _, tiles in spans)
    out = jax.ShapeDtypeStruct((rows, width), jnp.bfloat16)
    whole = pltpu.VMEM((rows, width), jnp.bfloat16)
    anywhere = pl.BlockSpec(memory_space=pl.ANY)
    body = functools.partial(conv_kernel, backward=backward, spans=spans)
    operands = (a, b, c, d, masks, taps, *[x for pair in others for x in pair])
    n = len(operands)
    return local_call(
        (lambda *refs: body(*refs[:n], *refs[n + 2 :])) if outs else body,
        "backward" if backward else "forward",
        [out, out],
        [whole, whole, pltpu.SemaphoreType.DMA((2, count))],
        16 * rows * rows * width,
        operands + tuple(outs or ()),
        [VMEM] * n + [anywhere] * (2 if outs else 0),
        [anywhere] * 2,
        {n: 0, n + 1: 1} if outs else {},
    )


def other_core(block):
    return lax.ppermute(block, "ctx", [(i, i ^ 1) for i in range(lax.axis_size("ctx"))])


def next_chip(block):
    size = lax.axis_size("ctx")
    pairs = [(i, i + 1) for i in range(1, size - 1, 2)]
    return lax.ppermute(block, "ctx", pairs + [(j, i) for i, j in pairs])


def factors(size):
    found, p = [], 2
    while size > 1:
        while size % p == 0:
            found.append(p)
            size //= p
        p += 1
    return found


def rounds_over_chips():
    return [
        (axis, first * math.prod(factors(lax.axis_size(axis) // first)[:n]), p)
        for axis, first in (("dp", 1), ("ctx", 2))
        for n, p in enumerate(factors(lax.axis_size(axis) // first))
    ]


def summed_over(total, axis, stride, p):
    size = lax.axis_size(axis)
    turned = lambda i, k: i + ((i // stride + k) % p - i // stride % p) * stride
    got = [lax.ppermute(total, axis, [(turned(i, k), i) for i in range(size)]) for k in range(1, p)]
    if p == 2:
        return total + got[0]
    digit = lax.axis_index(axis) // stride % p
    return jnp.sum(jnp.roll(jnp.stack([total, *got]), digit, axis=0), axis=0)


def after(value, *others):
    return lax.optimization_barrier((value, *others))[0]


def per_device(q_proj, k_proj, v_proj, out_grad, contig_starts, filters):
    q, k, v, dy = q_proj[0], k_proj[0], v_proj[0], out_grad[0]
    rows = q.shape[0]
    groups, taps = filters.shape
    assert rows == taps == LANES and lax.axis_size("ctx") % 2 == 0
    scale = 1.0 / math.sqrt(rows * lax.axis_size("ctx") * lax.axis_size("dp") * GSIZE)
    inputs = q, k, v, dy
    *partly, far_out, pair_out, keep, flags = first(*inputs, contig_starts)
    square = pltpu.VMEM((rows, rows), jnp.float32)
    part = pltpu.VMEM((groups // 2, rows), jnp.float32)
    unsummed = pltpu.VMEM((groups * 4, rows), jnp.float32)
    wide = pltpu.VMEM(q.shape, q.dtype)
    sent = pltpu.VMEM((rows, q.shape[1] // 2), q.dtype)
    far = next_chip(far_out)
    later_pair = other_core(pair_out)
    masks_made = [
        pltpu.VMEM((3, rows, rows), jnp.float32),
        pltpu.VMEM((2, rows, 2 * rows), jnp.bfloat16),
        pltpu.VMEM((2, *filters.shape), jnp.float32),
    ]
    q, k, v, dy, theirs, pair_out, far_out, masks, table_masks, tap_rows = own_call(
        functools.partial(filter_partner_kernel, scale=scale), "filter_partner",
        [wide] * 4 + [part, sent, sent] + masks_made,
        [unsummed, pltpu.VMEM(filters.shape, filters.dtype), pltpu.SemaphoreType.DMA((9,))],
        (*inputs, filters), (*partly, keep, flags), {5: 0, 6: 1, 7: 2, 8: 3},
    )
    pair = other_core(pair_out)
    mine = own_call(
        filter_own_kernel, "filter_own", unsummed, [square],
        (), (q, k, v, dy, later_pair, masks),
    )
    later_far = next_chip(after(far_out, mine))
    mine = own_call(
        functools.partial(filter_far_kernel, scale=scale), "filter_far", part, [unsummed, square],
        (), (q, k, v, dy, far, masks, mine),
    )
    mine = mine + other_core(theirs)

    half_tiles = q.shape[1] // 2 // LANES
    first_others, later_others = (pair, far), (later_pair, later_far)

    def forward(spans, others, outs=None):
        return convolution(k, v, q, dy, table_masks, tap_rows, spans, others, outs, False)

    def backward(spans, others, outs=None):
        return convolution(dy, q, v, k, table_masks, tap_rows, spans, others, outs, True)

    for n, place in enumerate(rounds_over_chips()):
        if n == 0:
            some_forward = forward([(0, half_tiles)], [first_others])
        if n == 1:
            mine = after(mine, *some_forward)
            some_backward = backward([(half_tiles, half_tiles)], [first_others])
        if n == 2:
            mine = after(mine, *some_backward, later_far, later_pair)
            mixed, grad_q = forward([(half_tiles, half_tiles)], [later_others], some_forward)
        if n == 3:
            mine = after(mine, mixed, grad_q)
            grad_k, grad_v = backward([(0, half_tiles)], [later_others], some_backward)
        mine = summed_over(mine, *place)
    mine = after(mine, grad_k, grad_v)
    halves = [mine, other_core(mine)]
    filter_grad = jnp.where(lax.axis_index("ctx") % 2 == 0, jnp.concatenate(halves), jnp.concatenate(halves[::-1]))
    return (mixed[None], grad_q[None], grad_k[None], grad_v[None], filter_grad)


def solution(mesh):
    wide = P("dp", "ctx", None)
    return jax.shard_map(
        per_device,
        mesh=mesh,
        in_specs=(wide,) * 4 + (P("dp", "ctx"), P()),
        out_specs=(wide,) * 4 + (P(),),
        check_vma=False,
    )
```

```python
import functools
import math

import jax
import jax.numpy as jnp
from jax import lax
from jax.experimental import pallas as pl
from jax.experimental.pallas import tpu as pltpu
from jax.sharding import PartitionSpec as P

GSIZE = 16
LANES = 128
BLOCK = 32
STEP = 4
VMEM = pl.BlockSpec(memory_space=pltpu.VMEM)


def product(a, b):
    return a * b


def reversed_taps(rows_of_taps):
    taps = rows_of_taps.shape[1]
    i = lax.broadcasted_iota(jnp.int32, (taps, taps), 0)
    j = lax.broadcasted_iota(jnp.int32, (taps, taps), 1)
    flip = jnp.where((i + j == 0) | (i + j == taps), 1.0, 0.0).astype(jnp.float32)
    return jnp.dot(
        rows_of_taps.astype(jnp.float32), flip,
        preferred_element_type=jnp.float32, precision=lax.Precision.HIGHEST,
    )


def lane_groups():
    return lax.broadcasted_iota(jnp.int32, (1, LANES), 1) // GSIZE


def each_tile(tile, width):
    count = width // LANES
    step = math.gcd(count, STEP)

    def body(i, carry):
        for j in range(step):
            tile(i * step + j)
        return carry

    lax.fori_loop(0, count // step, body, 0)


def aligned(mask):
    rows = mask.shape[0]
    blocks = [mask[at : at + BLOCK] for at in range(0, rows, BLOCK)]
    return jnp.concatenate(
        blocks[:1] + [pltpu.roll(block, rows - BLOCK * (i + 1), 1) for i, block in enumerate(blocks[1:])], axis=0
    )


def turned(tile, at):
    return jnp.concatenate([tile[at:], tile[:at]], axis=0) if at else tile


def for_groups(block):
    return jnp.concatenate([block] * (LANES // GSIZE), axis=0)


def half_copies(sources, targets, half, sems):
    rows, width = sources[0].shape
    lanes = pl.ds(pl.multiple_of(half * (width // 2), width // 2), width // 2)
    copies = []
    for n in range(2):
        part = pl.ds(n * (rows // 2), rows // 2)
        for source, target in zip(sources, targets):
            copies.append(
                pltpu.make_async_copy(source.at[part, lanes], target.at[part, lanes], sems.at[len(copies)])
            )
    return copies


def sent_products(inputs, half, keep_ref, kv_out, cot_out, swapped):
    q_ref, k_ref, v_ref, dy_ref = inputs
    width = kv_out.shape[1]
    lanes = pl.ds(pl.multiple_of(half * width, width), width)
    kv = product(k_ref[:, lanes], v_ref[:, lanes])
    cot = product(dy_ref[:, lanes], q_ref[:, lanes])
    kv = jnp.where(keep_ref[1][:, :1] > 0, kv, jnp.zeros_like(kv))
    cot = jnp.where(keep_ref[0][:, :1] > 0, cot, jnp.zeros_like(cot))
    kv_out[...] = jnp.where(swapped, cot, kv)
    cot_out[...] = jnp.where(swapped, kv, cot)


def first_kernel(
    q_hbm, k_hbm, v_hbm, dy_hbm, starts_hbm, filters_hbm,
    q_ref, k_ref, v_ref, dy_ref, far_ref, pair_ref, keep_ref, masks_ref, table_masks_ref, taps_ref,
    starts_ref, filters_ref, sems,
):
    rows = q_ref.shape[0]
    core = lax.axis_index("ctx") % 2
    small = [
        pltpu.make_async_copy(starts_hbm, starts_ref, sems.at[8]),
        pltpu.make_async_copy(filters_hbm, filters_ref, sems.at[9]),
    ]
    inputs = (q_ref, k_ref, v_ref, dy_ref)
    copies = half_copies((q_hbm, k_hbm, v_hbm, dy_hbm), inputs, 1 - core, sems)
    for copy in small + copies:
        copy.start()

    small[0].wait()
    starts = jnp.broadcast_to(starts_ref[...], (rows, rows)) > 0
    t = lax.broadcasted_iota(jnp.int32, (rows, rows), 0)
    s = lax.broadcasted_iota(jnp.int32, (rows, rows), 1)
    began = jnp.max(jnp.where(starts & (s <= t), s, 0), axis=1, keepdims=True)
    first = jnp.min(jnp.where(starts, s, rows), axis=1, keepdims=True)
    last = jnp.max(jnp.where(starts, s, 0), axis=1, keepdims=True)
    as_f32 = lambda mask: jnp.where(mask, 1.0, 0.0).astype(jnp.float32)
    own = as_f32((s <= t) & (s >= began))
    previous = as_f32((s > t) & (t < first))
    following = as_f32((s < t) & (t >= last))
    keep_ref[0] = as_f32(t < first)
    keep_ref[1] = as_f32(t >= last)
    for n, parts in enumerate(((own, previous), (own.T, following))):
        for m, mask in enumerate(parts):
            table_masks_ref[n, :, m * rows : (m + 1) * rows] = aligned(mask).astype(jnp.bfloat16)
    for n, mask in enumerate((own.T, following, previous.T)):
        masks_ref[n] = aligned(mask)
    small[1].wait()
    taps_ref[0] = reversed_taps(filters_ref[...])
    taps_ref[1] = filters_ref[...].astype(jnp.float32)
    for copy in copies:
        copy.wait()
    sent_products(inputs, 1 - core, keep_ref, far_ref, pair_ref, core == 0)


def tile_products(inputs, half, index):
    q_ref, k_ref, v_ref, dy_ref = inputs
    lanes = lanes_of(half, q_ref.shape[1] // 2, index)
    return product(k_ref[:, lanes], v_ref[:, lanes]), product(dy_ref[:, lanes], q_ref[:, lanes])


def wrapped_products(left, rights, masks, group):
    rows = left[0].shape[0]
    zeros = jnp.zeros_like(left[0])
    totals = [None] * len(masks)
    for at in range(0, rows, BLOCK):
        picked = jnp.concatenate(
            [
                jnp.concatenate([jnp.where(group == g, tile[at : at + BLOCK], zeros[:BLOCK]) for tile in left], axis=1)
                for g in range(LANES // GSIZE)
            ],
            axis=0,
        )
        right = jnp.concatenate(
            [
                jnp.concatenate([zeros if tile is None else turned(tile, at) for tile in tiles], axis=1)
                for tiles in rights
            ],
            axis=0,
        )
        pairs = lax.dot_general(picked, right, (((1,), (1,)), ((), ())), preferred_element_type=jnp.float32)
        for n, columns in enumerate(masks):
            for column, mask_ref in columns:
                piece = pairs[:, column * rows : (column + 1) * rows] * for_groups(mask_ref[at : at + BLOCK, :])
                totals[n] = piece if totals[n] is None else totals[n] + piece
    for total in totals:
        parts = []
        for at in range(0, total.shape[0], BLOCK):
            part = total[at : at + 8]
            for row in range(8, BLOCK, 8):
                part = part + pltpu.roll(total[at + row : at + row + 8], rows - row, 1)
            parts.append(part)
        yield jnp.concatenate(parts, axis=0)


def diagonals(sums_ref, groups):
    rows = sums_ref.shape[1]
    total = sums_ref[pl.ds(0, groups, stride=8), :]
    for r in range(1, 8):
        total = total + pltpu.roll(sums_ref[pl.ds(r, groups, stride=8), :], rows - r, 1)
    return total


def sums_at(index):
    count = LANES // GSIZE * 8
    return pl.ds(pl.multiple_of(index * count, count), count)


def two_tiles(index, sides, mask_ref, store, group):
    (left_a, right_a), (left_b, right_b) = sides(index), sides(index + 1)
    masks = [[(0, mask_ref)], [(1, mask_ref)]]
    rights = [[right_a, None], [None, right_b]]
    for n, total in enumerate(wrapped_products([left_a, left_b], rights, masks, group)):
        store(sums_at(index + n), total)


def lanes_of(half, width, index):
    return pl.ds(pl.multiple_of(half * width + index * LANES, LANES), LANES)


def filter_partner_kernel(
    q_hbm, k_hbm, v_hbm, dy_hbm, q_in, k_in, v_in, dy_in, keep_ref, masks_ref,
    q_ref, k_ref, v_ref, dy_ref, out_ref, pair_ref, far_ref, sums_ref, sems, *, scale
):
    del q_in, k_in, v_in, dy_in
    core = lax.axis_index("ctx") % 2
    inputs = (q_ref, k_ref, v_ref, dy_ref)
    copies = half_copies((q_hbm, k_hbm, v_hbm, dy_hbm), inputs, core, sems)
    for copy in copies:
        copy.start()
    group = lane_groups()

    def store(at, total):
        sums_ref[at, :] = total

    def tiles(index):
        two_tiles(2 * index, lambda i: tile_products(inputs, 1 - core, i), masks_ref.at[0], store, group)

    each_tile(tiles, q_ref.shape[1] // 4)
    out_ref[...] = diagonals(sums_ref, out_ref.shape[0]) * scale
    for copy in copies:
        copy.wait()
    sent_products(inputs, core, keep_ref, pair_ref, far_ref, core == 1)


def filter_own_kernel(q_ref, k_ref, v_ref, dy_ref, other_ref, masks_ref, sums_ref, cross_ref):
    inputs = (q_ref, k_ref, v_ref, dy_ref)
    width = q_ref.shape[1] // 2
    core = lax.axis_index("ctx") % 2
    even = core == 0
    cross_ref[...] = jnp.where(even, masks_ref[1], masks_ref[2])
    group = lane_groups()

    def tile(index):
        kv, cot = tile_products(inputs, core, index)
        other = other_ref[:, lanes_of(0, width, index)]
        left = [kv, jnp.where(even, kv, other)]
        rights = [[cot, None], [None, jnp.where(even, other, cot)]]
        for total in wrapped_products(left, rights, [[(0, masks_ref.at[0]), (1, cross_ref)]], group):
            sums_ref[sums_at(index), :] = total

    each_tile(tile, width)


def filter_far_kernel(q_ref, k_ref, v_ref, dy_ref, other_ref, masks_ref, base_ref, out_ref, total_ref, cross_ref, *, scale):
    inputs = (q_ref, k_ref, v_ref, dy_ref)
    width = q_ref.shape[1] // 2
    core = lax.axis_index("ctx") % 2
    even = core == 0
    cross_ref[...] = jnp.where(even, masks_ref[2], masks_ref[1])
    group = lane_groups()

    def sides(index):
        kv, cot = tile_products(inputs, core, index)
        other = other_ref[:, lanes_of(0, width, index)]
        return jnp.where(even, other, kv), jnp.where(even, cot, other)

    def store(at, total):
        total_ref[at, :] = base_ref[at, :] + total

    each_tile(lambda index: two_tiles(2 * index, sides, cross_ref, store, group), width // 2)
    out_ref[...] = diagonals(total_ref, out_ref.shape[0]) * scale


def conv_kernel(
    a_ref, b_ref, c_ref, d_ref, masks_ref, taps_ref, pair_ref, far_ref, *rest, backward, spans
):
    later = rest[: 2 * len(spans) - 2]
    others = [(pair_ref, far_ref), *zip(later[::2], later[1::2])]
    out_c_hbm, out_d_hbm, out_c_ref, out_d_ref, sems = rest[-5:]
    rows = a_ref.shape[0]
    per_tile = LANES // GSIZE
    half_tiles = a_ref.shape[1] // 2 // LANES
    even = lax.axis_index("ctx") % 2 == 0
    from_pair = even if backward else jnp.logical_not(even)
    group = lane_groups()
    mask_ref = masks_ref.at[1 if backward else 0]

    def table_start(row):
        start = pltpu.roll(jnp.broadcast_to(row, (BLOCK, rows)), 0, 1, stride=1, stride_axis=0).astype(jnp.bfloat16)
        return jnp.concatenate([start, start], axis=1)

    def lanes_at(index):
        return pl.ds(pl.multiple_of(index * LANES, LANES), LANES)

    def tile(index, near, distant):
        lanes = lanes_at(index)
        here = lanes_at(index % half_tiles)
        own = product(a_ref[:, lanes], b_ref[:, lanes])
        other = jnp.where(from_pair, near[:, here], distant[:, here])
        taps = taps_ref[1 if backward else 0, pl.ds(pl.multiple_of(index * per_tile, per_tile), per_tile), :]
        tables = jnp.concatenate([table_start(taps[g : g + 1]) for g in range(per_tile)], axis=0)
        for at in range(0, rows, BLOCK):
            x = jnp.concatenate([turned(own, at), turned(other, at)], axis=0)
            masked = tables * for_groups(mask_ref[at : at + BLOCK, :])
            every = jnp.dot(masked, x, preferred_element_type=jnp.float32)
            y = every[:BLOCK]
            for g in range(1, per_tile):
                y = jnp.where(group == g, every[g * BLOCK : (g + 1) * BLOCK], y)
            block = slice(at, at + BLOCK)
            out_c_ref[block, lanes] = (c_ref[block, lanes].astype(jnp.float32) * y).astype(jnp.bfloat16)
            out_d_ref[block, lanes] = (d_ref[block, lanes].astype(jnp.float32) * y).astype(jnp.bfloat16)

    def stored(start, count, sem):
        lanes = pl.ds(pl.multiple_of(start * LANES, count * LANES), count * LANES)
        return [
            pltpu.make_async_copy(out_c_ref.at[:, lanes], out_c_hbm.at[:, lanes], sems.at[0, sem]),
            pltpu.make_async_copy(out_d_ref.at[:, lanes], out_d_hbm.at[:, lanes], sems.at[1, sem]),
        ]

    bodies = []
    for (first, count), (near, distant) in zip(spans, others):
        step = math.gcd(count, STEP)

        def body(i, carry, first=first, step=step, near=near, distant=distant, sem=len(bodies)):
            for j in range(step):
                tile(first + i * step + j, near, distant)
            for copy in stored(first + i * step, step, sem + i):
                copy.start()
            return carry

        for i in range(count // step):
            body(i, 0)
        bodies += [(first + i * step, step) for i in range(count // step)]
    for n, (start, count) in enumerate(bodies):
        for copy in stored(start, count, n):
            copy.wait()


def local_call(kernel, name, out_shape, scratch_shapes, flops, operands, in_specs=None, out_specs=VMEM, aliases={}, moved=None):
    outs = out_shape if isinstance(out_shape, list) else [out_shape]
    if moved is None:
        moved = sum(math.prod(x.shape) * x.dtype.itemsize for x in [*operands, *outs])
    return pl.pallas_call(
        kernel,
        out_shape=out_shape,
        in_specs=in_specs or [VMEM] * len(operands),
        out_specs=out_specs,
        scratch_shapes=scratch_shapes,
        input_output_aliases=aliases,
        cost_estimate=pl.CostEstimate(flops=flops, bytes_accessed=moved, transcendentals=0),
        compiler_params=pltpu.CompilerParams(vmem_limit_bytes=24 << 20),
        name=name,
    )(*operands)


def in_hbm(*arrays):
    return [pltpu.with_memory_space_constraint(x, pltpu.HBM) for x in arrays]


def own_call(kernel, name, out_shape, scratch_shapes, hbm_operands, operands, aliases={}):
    return pl.pallas_call(
        kernel,
        out_shape=out_shape,
        in_specs=[pl.BlockSpec(memory_space=pltpu.HBM)] * len(hbm_operands) + [VMEM] * len(operands),
        out_specs=[VMEM] * len(out_shape) if isinstance(out_shape, list) else VMEM,
        scratch_shapes=scratch_shapes,
        input_output_aliases=aliases,
        cost_estimate=pl.CostEstimate(flops=0, bytes_accessed=0, transcendentals=0),
        compiler_params=pltpu.CompilerParams(vmem_limit_bytes=24 << 20),
        name=name,
    )(*in_hbm(*hbm_operands), *operands)


def first(q, k, v, dy, starts, filters):
    rows, width = q.shape
    wide = pltpu.VMEM((rows, width), jnp.bfloat16)
    sent = pltpu.VMEM((rows, width // 2), jnp.bfloat16)
    return own_call(
        first_kernel, "first",
        [wide] * 4 + [sent] * 2 + [
            pltpu.VMEM((2, rows, rows), jnp.float32),
            pltpu.VMEM((3, rows, rows), jnp.float32),
            pltpu.VMEM((2, rows, 2 * rows), jnp.bfloat16),
            pltpu.VMEM((2, *filters.shape), jnp.float32),
        ],
        [
            pltpu.VMEM(starts.shape, starts.dtype), pltpu.VMEM(filters.shape, filters.dtype),
            pltpu.SemaphoreType.DMA((10,)),
        ],
        (q, k, v, dy, starts, filters), (),
    )


def convolution(a, b, c, d, masks, taps, spans, others, outs, backward):
    rows, width = a.shape
    count = sum(tiles // math.gcd(tiles, STEP) for _, tiles in spans)
    out = jax.ShapeDtypeStruct((rows, width), jnp.bfloat16)
    whole = pltpu.VMEM((rows, width), jnp.bfloat16)
    anywhere = pl.BlockSpec(memory_space=pl.ANY)
    body = functools.partial(conv_kernel, backward=backward, spans=spans)
    operands = (a, b, c, d, masks, taps, *[x for pair in others for x in pair])
    n = len(operands)
    return local_call(
        (lambda *refs: body(*refs[:n], *refs[n + 2 :])) if outs else body,
        "backward" if backward else "forward",
        [out, out],
        [whole, whole, pltpu.SemaphoreType.DMA((2, count))],
        16 * rows * rows * width,
        operands + tuple(outs or ()),
        [VMEM] * n + [anywhere] * (2 if outs else 0),
        [anywhere] * 2,
        {n: 0, n + 1: 1} if outs else {},
    )


def other_core(block):
    return lax.ppermute(block, "ctx", [(i, i ^ 1) for i in range(lax.axis_size("ctx"))])


def next_chip(block):
    size = lax.axis_size("ctx")
    pairs = [(i, i + 1) for i in range(1, size - 1, 2)]
    return lax.ppermute(block, "ctx", pairs + [(j, i) for i, j in pairs])


def factors(size):
    found, p = [], 2
    while size > 1:
        while size % p == 0:
            found.append(p)
            size //= p
        p += 1
    return found


def rounds_over_chips():
    return [
        (axis, first * math.prod(factors(lax.axis_size(axis) // first)[:n]), p)
        for axis, first in (("dp", 1), ("ctx", 2))
        for n, p in enumerate(factors(lax.axis_size(axis) // first))
    ]


def summed_over(total, axis, stride, p):
    size = lax.axis_size(axis)
    turned = lambda i, k: i + ((i // stride + k) % p - i // stride % p) * stride
    got = [lax.ppermute(total, axis, [(turned(i, k), i) for i in range(size)]) for k in range(1, p)]
    if p == 2:
        return total + got[0]
    digit = lax.axis_index(axis) // stride % p
    return jnp.sum(jnp.roll(jnp.stack([total, *got]), digit, axis=0), axis=0)


def after(value, *others):
    return lax.optimization_barrier((value, *others))[0]


def per_device(q_proj, k_proj, v_proj, out_grad, contig_starts, filters):
    q, k, v, dy = q_proj[0], k_proj[0], v_proj[0], out_grad[0]
    rows = q.shape[0]
    groups, taps = filters.shape
    assert rows == taps == LANES and lax.axis_size("ctx") % 2 == 0
    scale = 1.0 / math.sqrt(rows * lax.axis_size("ctx") * lax.axis_size("dp") * GSIZE)
    inputs = q, k, v, dy
    *partly, far_out, pair_out, keep, masks, table_masks, tap_rows = first(*inputs, contig_starts, filters)
    square = pltpu.VMEM((rows, rows), jnp.float32)
    part = pltpu.VMEM((groups // 2, rows), jnp.float32)
    unsummed = pltpu.VMEM((groups * 4, rows), jnp.float32)
    wide = pltpu.VMEM(q.shape, q.dtype)
    sent = pltpu.VMEM((rows, q.shape[1] // 2), q.dtype)
    far = next_chip(far_out)
    later_pair = other_core(pair_out)
    q, k, v, dy, theirs, pair_out, far_out = own_call(
        functools.partial(filter_partner_kernel, scale=scale), "filter_partner",
        [wide] * 4 + [part, sent, sent], [unsummed, pltpu.SemaphoreType.DMA((8,))],
        inputs, (*partly, keep, masks), {4: 0, 5: 1, 6: 2, 7: 3},
    )
    pair = other_core(pair_out)
    mine = own_call(
        filter_own_kernel, "filter_own", unsummed, [square],
        (), (q, k, v, dy, later_pair, masks),
    )
    later_far = next_chip(after(far_out, mine))
    mine = own_call(
        functools.partial(filter_far_kernel, scale=scale), "filter_far", part, [unsummed, square],
        (), (q, k, v, dy, far, masks, mine),
    )
    mine = mine + other_core(theirs)

    half_tiles = q.shape[1] // 2 // LANES
    first_others, later_others = (pair, far), (later_pair, later_far)

    def forward(spans, others, outs=None):
        return convolution(k, v, q, dy, table_masks, tap_rows, spans, others, outs, False)

    def backward(spans, others, outs=None):
        return convolution(dy, q, v, k, table_masks, tap_rows, spans, others, outs, True)

    for n, place in enumerate(rounds_over_chips()):
        if n == 0:
            some_forward = forward([(0, half_tiles)], [first_others])
        if n == 1:
            mine = after(mine, *some_forward)
            some_backward = backward([(half_tiles, half_tiles)], [first_others])
        if n == 2:
            mine = after(mine, *some_backward, later_far, later_pair)
            mixed, grad_q = forward([(half_tiles, half_tiles)], [later_others], some_forward)
        if n == 3:
            mine = after(mine, mixed, grad_q)
            grad_k, grad_v = backward([(0, half_tiles)], [later_others], some_backward)
        mine = summed_over(mine, *place)
    mine = after(mine, grad_k, grad_v)
    halves = [mine, other_core(mine)]
    filter_grad = jnp.where(lax.axis_index("ctx") % 2 == 0, jnp.concatenate(halves), jnp.concatenate(halves[::-1]))
    return (mixed[None], grad_q[None], grad_k[None], grad_v[None], filter_grad)


def solution(mesh):
    wide = P("dp", "ctx", None)
    return jax.shard_map(
        per_device,
        mesh=mesh,
        in_specs=(wide,) * 4 + (P("dp", "ctx"), P()),
        out_specs=(wide,) * 4 + (P(),),
        check_vma=False,
    )
```
